32 devices in a mesh: wide: 4 (over z), narrow: 8 (over y, x, core).
Axes of the slice: x: 2, y: 2, z: 4, core: 2. Of those that a mesh axis runs over, the one named last changes fastest.
Arguments:
- tokens: bfloat16 [64, 1024, 512], P(('wide', 'narrow')), may hold values from -6 to 6
- cotangent: bfloat16 [64, 1024, 512], P(('wide', 'narrow')), may hold values from -6 to 6
- seq_counts: int32 [32], replicated, may hold values from 1 to 2, as said below
- micro_assign: int32 [32, 2], replicated, may hold values from 0 to 1, each once within a row
- norm_params: float32 [4, 512], P(None, ('wide', 'narrow'))
- norm_first: float32 [4, 512], P(None, ('wide', 'narrow'))
- norm_second: float32 [4, 512], P(None, ('wide', 'narrow'))
- project_weight: float32 [512, 1536], P(('wide', 'narrow')), may hold values from -0.25 to 0.25
- project_first: float32 [512, 1536], P(('wide', 'narrow'))
- project_second: float32 [512, 1536], P(('wide', 'narrow'))
- output_weight: float32 [512, 512], P(('wide', 'narrow')), may hold values from -2 to 2
- output_first: float32 [512, 512], P(('wide', 'narrow'))
- output_second: float32 [512, 512], P(('wide', 'narrow'))
- control_weight: float32 [512, 8], P(('wide', 'narrow')), may hold values from -0.125 to 0.125
- control_first: float32 [512, 8], P(('wide', 'narrow'))
- control_second: float32 [512, 8], P(('wide', 'narrow'))
- up_weight: float32 [8, 512, 2048], P('narrow', 'wide'), may hold values from -1 to 1
- up_first: float32 [8, 512, 2048], P('narrow', 'wide')
- up_second: float32 [8, 512, 2048], P('narrow', 'wide')
- down_weight: float32 [8, 2048, 512], P('narrow', 'wide'), may hold values from -1 to 1
- down_first: float32 [8, 2048, 512], P('narrow', 'wide')
- down_second: float32 [8, 2048, 512], P('narrow', 'wide')
Outputs:
- out_rows: bfloat16 [64, 1024, 512], P(('wide', 'narrow'))
- grad_tokens: float32 [64, 1024, 512], P(('wide', 'narrow'))
- grad_norm: float32 [], replicated
- norm_new: float32 [4, 512], P(None, ('wide', 'narrow'))
- norm_first_new: float32 [4, 512], P(None, ('wide', 'narrow'))
- norm_second_new: float32 [4, 512], P(None, ('wide', 'narrow'))
- norm_low: bfloat16 [4, 512], P(None, ('wide', 'narrow'))
- project_new: float32 [512, 1536], P(('wide', 'narrow'))
- project_first_new: float32 [512, 1536], P(('wide', 'narrow'))
- project_second_new: float32 [512, 1536], P(('wide', 'narrow'))
- project_low: bfloat16 [512, 1536], P(('wide', 'narrow'))
- output_new: float32 [512, 512], P(('wide', 'narrow'))
- output_first_new: float32 [512, 512], P(('wide', 'narrow'))
- output_second_new: float32 [512, 512], P(('wide', 'narrow'))
- output_low: bfloat16 [512, 512], P(('wide', 'narrow'))
- control_new: float32 [512, 8], P(('wide', 'narrow'))
- control_first_new: float32 [512, 8], P(('wide', 'narrow'))
- control_second_new: float32 [512, 8], P(('wide', 'narrow'))
- control_low: bfloat16 [512, 8], P(('wide', 'narrow'))
- up_new: float32 [8, 512, 2048], P('narrow', 'wide')
- up_first_new: float32 [8, 512, 2048], P('narrow', 'wide')
- up_second_new: float32 [8, 512, 2048], P('narrow', 'wide')
- up_low: bfloat16 [8, 512, 2048], P('narrow', 'wide')
- down_new: float32 [8, 2048, 512], P('narrow', 'wide')
- down_first_new: float32 [8, 2048, 512], P('narrow', 'wide')
- down_second_new: float32 [8, 2048, 512], P('narrow', 'wide')
- down_low: bfloat16 [8, 2048, 512], P('narrow', 'wide')
The draws below stay inside these ranges and needn't reach their ends.
Inputs may be any that keep to these rules, and one draw needn't show every extreme that they name: `seq_counts`: among the devices that share an index of wide, at least one holds 2 live slots; live slots are the first ones of a device. `micro_assign`: each row names every micro-batch once.
All inputs are finite; a program needn't handle non-finite values.
Results may differ from the reference program's by a relative error of at most 0.019.
Values may be sent and summed in bfloat16 or wider, within the bound.
A program may use at most 320 MiB of HBM per device.

```python
import math
import jax
import jax.numpy as jnp
from jax import lax

D = 512
HEADS = 8
FF = 2048
SEQ_LEN = 1024
MB = 2
EXP_DEV = 1
STEP = 5
EXPERTS = 8
SEQS = 64
N_WIDE = 4
N_NARROW = 8


CLIP_NORM = 0.05


def gradient_scale(kind_number):
    token_root = math.sqrt(0.75 * SEQS * SEQ_LEN)
    expert_root = math.sqrt(SEQS * SEQ_LEN * EXP_DEV / EXPERTS)
    raw_sizes = [4.0 * token_root, 3.0 * token_root, 0.1 * token_root, 8.0 * token_root, 0.2 * expert_root, 0.2 * expert_root]
    entry_counts = [4 * D, 3 * D * D, D * D, D * EXPERTS, EXPERTS * D * FF, EXPERTS * FF * D]
    total = math.sqrt(sum((count_value * size_value * size_value for count_value, size_value in zip(entry_counts, raw_sizes))))
    return CLIP_NORM * raw_sizes[kind_number] / total


def momentum_draw(key, extent, kind_number, salt_value):
    folded = jax.random.fold_in(key, salt_value)
    size_key, sign_key = jax.random.split(folded)
    magnitude = jnp.exp(jax.random.uniform(size_key, extent, jnp.float32, math.log(0.5), math.log(2.0)))
    sign_values = jnp.where(jax.random.bernoulli(sign_key, 0.5, extent), 1.0, -1.0)
    return (gradient_scale(kind_number) * magnitude * sign_values).astype(jnp.float32)


def variance_draw(key, extent, kind_number, salt_value):
    folded = jax.random.fold_in(key, salt_value)
    magnitude = jnp.exp(jax.random.uniform(folded, extent, jnp.float32, 0.0, math.log(4.0)))
    scale_value = gradient_scale(kind_number)
    return (scale_value * scale_value * magnitude).astype(jnp.float32)


def draw_seq_counts(key, part):
    folded = jax.random.fold_in(key, 101)
    count_key, place_key = jax.random.split(folded)
    drawn_counts = jax.random.randint(count_key, (N_WIDE, N_NARROW), 1, MB + 1)
    full_place = jax.random.randint(place_key, (N_WIDE, 1), 0, N_NARROW)
    positions = jnp.arange(N_NARROW, dtype=jnp.int32)[None, :]
    return jnp.where(positions == full_place, MB, drawn_counts).reshape(-1).astype(jnp.int32)


def draw_norm_params(key, part):
    folded = jax.random.fold_in(key, 102)
    gain_key, bias_key = jax.random.split(folded)
    ramp = jnp.arange(D, dtype=jnp.float32) / max(D - 1, 1)
    rising = jnp.exp(math.log(0.5) + math.log(3.0) * ramp)
    noise = jax.random.uniform(gain_key, (2, D), jnp.float32, 0.75, 1.35)
    biases = 0.08 * jnp.clip(jax.random.normal(bias_key, (2, D), jnp.float32), -3.0, 3.0)
    gains = rising[None, :] * noise
    return jnp.stack([gains[0], biases[0], gains[1], biases[1]]).astype(jnp.float32)


def draw_norm_first(key, part):
    return momentum_draw(key, (4, D), 0, 103)


def draw_norm_second(key, part):
    return variance_draw(key, (4, D), 0, 104)


def draw_project_first(key, part):
    return momentum_draw(key, (D, 3 * D), 1, 105)


def draw_project_second(key, part):
    return variance_draw(key, (D, 3 * D), 1, 106)


def draw_output_first(key, part):
    return momentum_draw(key, (D, D), 2, 107)


def draw_output_second(key, part):
    return variance_draw(key, (D, D), 2, 108)


def draw_control_first(key, part):
    return momentum_draw(key, (D, EXPERTS), 3, 109)


def draw_control_second(key, part):
    return variance_draw(key, (D, EXPERTS), 3, 110)


def draw_up_first(key, part):
    return momentum_draw(key, (EXPERTS, D, FF), 4, 111)


def draw_up_second(key, part):
    return variance_draw(key, (EXPERTS, D, FF), 4, 112)


def draw_down_first(key, part):
    return momentum_draw(key, (EXPERTS, FF, D), 5, 113)


def draw_down_second(key, part):
    return variance_draw(key, (EXPERTS, FF, D), 5, 114)


def block_scale(key, shape, pieces, least, top_value):
    factor_of = 1.0
    for position, parts in pieces:
        steps = jax.random.uniform(jax.random.fold_in(jax.random.fold_in(key, 6), position), (parts,), jnp.float32, least / len(pieces), top_value / len(pieces))
        factor_of = factor_of * jnp.repeat(jnp.exp(steps), shape[position] // parts).reshape((-1,) + (1,) * (len(shape) - 1 - position))
    return factor_of


def normal_values(key, dims, scale, bound, pieces=(), kind=jnp.bfloat16):
    array = jax.random.normal(key, dims, jnp.float32) * scale
    if len(pieces) > 0:
        array = block_scale(key, dims, pieces, -0.22, 0.18) * array
    return jnp.clip(array, min=-bound, max=bound).astype(kind)


def setup_inputs(seed: int = 0) -> dict:
    arg_keys = jax.random.split(jax.random.key(seed), 23)
    tokens = normal_values(arg_keys[0], (SEQS, SEQ_LEN, D), 1.0, 6.0, ((0, 32),))
    cotangent = normal_values(arg_keys[1], (SEQS, SEQ_LEN, D), 1.0, 6.0, ((0, 32),))
    seq_counts = draw_seq_counts(jax.random.fold_in(arg_keys[22], 71), 0)
    micro_assign = jax.vmap(lambda own: jax.random.permutation(own, MB))(jax.random.split(arg_keys[3], (N_WIDE * N_NARROW))).reshape((N_WIDE * N_NARROW, MB)).astype(jnp.int32)
    norm_params = draw_norm_params(jax.random.fold_in(arg_keys[22], 71), 0)
    norm_first = draw_norm_first(jax.random.fold_in(arg_keys[22], 71), 0)
    norm_second = draw_norm_second(jax.random.fold_in(arg_keys[22], 71), 0)
    project_weight = normal_values(arg_keys[7], (D, 3 * D), D ** -0.5, 0.25, ((0, 32),), jnp.float32)
    project_first = draw_project_first(jax.random.fold_in(arg_keys[22], 71), 0)
    project_second = draw_project_second(jax.random.fold_in(arg_keys[22], 71), 0)
    output_weight = normal_values(arg_keys[10], (D, D), (D // 64) ** -0.5, 2.0, ((0, 32),), jnp.float32)
    output_first = draw_output_first(jax.random.fold_in(arg_keys[22], 71), 0)
    output_second = draw_output_second(jax.random.fold_in(arg_keys[22], 71), 0)
    control_weight = normal_values(arg_keys[13], (D, EXPERTS), (4 * D) ** -0.5, 0.125, ((0, 32),), jnp.float32)
    control_first = draw_control_first(jax.random.fold_in(arg_keys[22], 71), 0)
    control_second = draw_control_second(jax.random.fold_in(arg_keys[22], 71), 0)
    up_weight = normal_values(arg_keys[16], (EXPERTS, D, FF), (D // 16) ** -0.5, 1.0, ((0, 8), (1, 4)), jnp.float32)
    up_first = draw_up_first(jax.random.fold_in(arg_keys[22], 71), 0)
    up_second = draw_up_second(jax.random.fold_in(arg_keys[22], 71), 0)
    down_weight = normal_values(arg_keys[19], (EXPERTS, FF, D), (FF // 64) ** -0.5, 1.0, ((0, 8), (1, 4)), jnp.float32)
    down_first = draw_down_first(jax.random.fold_in(arg_keys[22], 71), 0)
    down_second = draw_down_second(jax.random.fold_in(arg_keys[22], 71), 0)
    return dict(tokens=tokens, cotangent=cotangent, seq_counts=seq_counts, micro_assign=micro_assign, norm_params=norm_params, norm_first=norm_first, norm_second=norm_second, project_weight=project_weight, project_first=project_first, project_second=project_second, output_weight=output_weight, output_first=output_first, output_second=output_second, control_weight=control_weight, control_first=control_first, control_second=control_second, up_weight=up_weight, up_first=up_first, up_second=up_second, down_weight=down_weight, down_first=down_first, down_second=down_second)


PRECISE = lax.Precision.HIGHEST
NEG_LARGE = -1e+30
NORM_EPS = 1e-05
CLIP_NORM = 0.05
BETA_ONE = 0.5
BETA_TWO = 0.5
ADAM_EPS = 1e-08
DECAY_RATE = 0.1

@jax.custom_vjp
def low(v):
    return lax.optimization_barrier(v.astype(jnp.bfloat16)).astype(jnp.float32)

@jax.custom_vjp
def low_back(v):
    return v

def low_keep(v):
    return (low(v), None)

def low_pass(kept, grad):
    return (grad,)

def back_keep(v):
    return (v, None)

def back_low(kept, grad):
    return (low(grad),)
low.defvjp(low_keep, low_pass)
low_back.defvjp(back_keep, back_low)

def layer_norm(values, norm_gain, norm_bias):
    row_mean = lax.optimization_barrier(jnp.mean(values, axis=-1, keepdims=True))
    centred = values - row_mean
    variance = lax.optimization_barrier(jnp.mean(centred * centred, axis=-1, keepdims=True))
    return centred * lax.rsqrt(variance + NORM_EPS) * norm_gain + norm_bias

def attention(queries, key_rows, values):
    members, length, model_width = queries.shape
    head_size = model_width // HEADS
    query_heads = queries.reshape(members, length, HEADS, head_size)
    key_heads = key_rows.reshape(members, length, HEADS, head_size)
    value_heads = values.reshape(members, length, HEADS, head_size)
    scores = jnp.einsum('nqhd,nkhd->nhqk', query_heads, key_heads, precision=PRECISE) * (1.0 / math.sqrt(head_size))
    scores = low_back(scores)
    causal = jnp.arange(length, dtype=jnp.int32)[None, :] <= jnp.arange(length, dtype=jnp.int32)[:, None]
    scores = jnp.where(causal[None, None], scores, NEG_LARGE)
    row_max = lax.optimization_barrier(jnp.max(scores, axis=-1, keepdims=True))
    exponent = jnp.exp(scores - row_max)
    probs = low(exponent / lax.optimization_barrier(jnp.sum(exponent, axis=-1, keepdims=True)))
    attended = jnp.einsum('nhqk,nkhd->nqhd', probs, value_heads, precision=PRECISE)
    return attended.reshape(members, length, model_width)

def group_forward(params, inputs, live_member):
    norms, project_weight, output_weight, control_weight, up_weight, down_weight = params
    model_width = inputs.shape[-1]
    normed = low(layer_norm(inputs, norms[0], norms[1]))
    project = low(low_back(jnp.einsum('nld,de->nle', normed, low(project_weight), precision=PRECISE)))
    attended = low(low_back(attention(project[..., :model_width], project[..., model_width:2 * model_width], project[..., 2 * model_width:])))
    hidden = inputs + low_back(jnp.einsum('nld,de->nle', attended, low(output_weight), precision=PRECISE))
    normed_two = low(layer_norm(hidden, norms[2], norms[3]))
    logits = low(low_back(jnp.einsum('nld,de->nle', normed_two, low(control_weight), precision=PRECISE)))
    live_cube = live_member[:, None, None]
    masked = jnp.where(live_cube > 0, logits, NEG_LARGE)
    col_max = lax.optimization_barrier(jnp.max(masked, axis=0, keepdims=True))
    exponent = jnp.exp(masked - col_max) * live_cube
    weights = exponent / lax.optimization_barrier(jnp.sum(exponent, axis=0, keepdims=True))
    mixture = low(low_back(jnp.einsum('nle,nld->eld', weights, normed_two, precision=PRECISE)))
    hidden_pre = low_back(jnp.einsum('eld,edf->elf', mixture, low(up_weight), precision=PRECISE))
    hidden_act = low(jax.nn.gelu(hidden_pre))
    expert_out = low(low_back(jnp.einsum('elf,efd->eld', hidden_act, low(down_weight), precision=PRECISE)))
    return hidden + jnp.einsum('nle,eld->nld', weights, expert_out, precision=PRECISE)

def adam_update(weight, first_state, second_state, gradient, factor, rate, decay):
    clipped = gradient * factor
    first_new = BETA_ONE * first_state + (1.0 - BETA_ONE) * clipped
    second_new = BETA_TWO * second_state + (1.0 - BETA_TWO) * clipped * clipped
    first_hat = first_new / (1.0 - BETA_ONE ** STEP)
    second_hat = second_new / (1.0 - BETA_TWO ** STEP)
    weight_new = weight - rate * (first_hat / (jnp.sqrt(second_hat) + ADAM_EPS) + decay * weight)
    return (weight_new, first_new, second_new, weight_new.astype(jnp.bfloat16))

def reference(tokens, cotangent, seq_counts, micro_assign, norm_params, norm_first, norm_second, project_weight, project_first, project_second, output_weight, output_first, output_second, control_weight, control_first, control_second, up_weight, up_first, up_second, down_weight, down_first, down_second):
    device_total = N_WIDE * N_NARROW
    batch_ids = jnp.arange(MB, dtype=jnp.int32)
    slot_of = lax.optimization_barrier(jnp.sum(batch_ids[None, None, :] * (micro_assign[:, None, :] == batch_ids[None, :, None]).astype(jnp.int32), axis=2))
    live_slots = (slot_of < seq_counts[:, None]).astype(jnp.float32)
    seq_index = jnp.arange(device_total, dtype=jnp.int32)[:, None] * MB + slot_of
    order = seq_index.reshape(N_WIDE, N_NARROW, MB).transpose(0, 2, 1).reshape(-1).astype(jnp.int32)
    live_groups = live_slots.reshape(N_WIDE, N_NARROW, MB).transpose(0, 2, 1).reshape(N_WIDE * MB, N_NARROW)
    group_shape = (N_WIDE * MB, N_NARROW, SEQ_LEN, D)
    inputs = tokens.astype(jnp.float32)[order].reshape(group_shape)
    cot_groups = cotangent.astype(jnp.float32)[order].reshape(group_shape)
    params = (norm_params, project_weight, output_weight, control_weight, up_weight, down_weight)
    checked = jax.checkpoint(group_forward)

    def whole(weights_all, inputs_all):
        return lax.map(lambda pair: checked(weights_all, pair[0], pair[1]), (inputs_all, live_groups))
    finals, pull_back = jax.vjp(whole, params, inputs)
    grads, grad_inputs = pull_back(cot_groups)
    out_rows = jnp.zeros(tokens.shape, jnp.float32).at[order].set(finals.reshape(-1, SEQ_LEN, D)).astype(jnp.bfloat16)
    grad_tokens = jnp.zeros(tokens.shape, jnp.float32).at[order].set(grad_inputs.reshape(-1, SEQ_LEN, D))
    squares = jnp.float32(0.0)
    for gradient in grads:
        squares = squares + jnp.sum(gradient * gradient)
    grad_norm = jnp.sqrt(squares)
    factor = CLIP_NORM / jnp.maximum(grad_norm, CLIP_NORM)
    norm_out = adam_update(norm_params, norm_first, norm_second, grads[0], factor, 0.3, 0.0)
    project_out = adam_update(project_weight, project_first, project_second, grads[1], factor, 0.03, DECAY_RATE)
    output_out = adam_update(output_weight, output_first, output_second, grads[2], factor, 0.2, DECAY_RATE)
    control_out = adam_update(control_weight, control_first, control_second, grads[3], factor, 0.015, DECAY_RATE)
    up_out = adam_update(up_weight, up_first, up_second, grads[4], factor, 0.1, DECAY_RATE)
    down_out = adam_update(down_weight, down_first, down_second, grads[5], factor, 0.1, DECAY_RATE)
    return (out_rows, grad_tokens, grad_norm, norm_out[0], norm_out[1], norm_out[2], norm_out[3], project_out[0], project_out[1], project_out[2], project_out[3], output_out[0], output_out[1], output_out[2], output_out[3], control_out[0], control_out[1], control_out[2], control_out[3], up_out[0], up_out[1], up_out[2], up_out[3], down_out[0], down_out[1], down_out[2], down_out[3])
```

```python
import functools
import math

import jax
import jax.numpy as jnp
from jax import lax
from jax.experimental import pallas as pl
from jax.experimental.pallas import tpu as pltpu
from jax.sharding import PartitionSpec as P

HEADS = 8
STEP = 5
NEG_LARGE = -1e30
NORM_EPS = 1e-05
CLIP_NORM = 0.05
BETA_ONE = 0.5
BETA_TWO = 0.5
ADAM_EPS = 1e-08
DECAY_RATE = 0.1

BF = jnp.bfloat16
F32 = jnp.float32
MESH = pl.DeviceIdType.MESH
LANES = 128
ROWS = 256
GELU_A = math.sqrt(2.0 / math.pi)
GELU_B = 0.044715


def dot(a, b, ca, cb):
    return lax.dot_general(a, b, (((ca,), (cb,)), ((), ())), preferred_element_type=F32)


def norm_stats(v):
    centred = v - jnp.mean(v, axis=-1, keepdims=True)
    rstd = lax.rsqrt(jnp.mean(centred * centred, axis=-1, keepdims=True) + NORM_EPS)
    return centred * rstd, rstd


def norm_back(grad, gain, xhat, rstd):
    t = grad * gain
    return rstd * (t - jnp.mean(t, axis=-1, keepdims=True) - xhat * jnp.mean(t * xhat, axis=-1, keepdims=True))


def remote(src, dst, send, recv, device):
    return pltpu.make_async_remote_copy(
        src_ref=src, dst_ref=dst, send_sem=send, recv_sem=recv, device_id=device, device_id_type=MESH
    )


def greet(devices):
    barrier = pltpu.get_barrier_semaphore()
    for device in devices:
        pl.semaphore_signal(barrier, inc=1, device_id=device, device_id_type=MESH)
    pl.semaphore_wait(barrier, len(devices))


def gather_kernel(wides, narrows, shard_ref, out_ref, local_sem, z_sem, p_sem, c_sem, recv_sem):
    w, n = lax.axis_index("wide"), lax.axis_index("narrow")
    half = narrows // 2
    q, parity = n // 2, lax.rem(n, 2)
    z_peers = [lax.rem(w + k, wides) for k in range(1, wides)]
    p_peers = [lax.rem(q + k, half) * 2 + parity for k in range(1, half)]
    core = n + 1 - 2 * parity
    greet([(z, n) for z in z_peers] + [(w, p) for p in p_peers] + [(w, core)])
    own = pltpu.make_async_copy(shard_ref, out_ref.at[w, n], local_sem)
    own.start()
    sends = []

    def send(src, zw, zn, sem, device):
        copy = remote(src, out_ref.at[zw, zn], sem, recv_sem.at[zw, zn], device)
        copy.start()
        sends.append(copy)

    def arrived(zw, zn):
        remote(shard_ref, out_ref.at[zw, zn], z_sem.at[0], recv_sem.at[zw, zn], (w, n)).wait_recv()

    for k, z in enumerate(z_peers):
        send(shard_ref, w, n, z_sem.at[k], (z, n))
    for k, p in enumerate(p_peers):
        send(shard_ref, w, n, p_sem.at[0, k], (w, p))
    send(shard_ref, w, n, c_sem.at[0, 0], (w, core))
    for j in range(1, wides):
        zw = lax.rem(w + wides - j, wides)
        arrived(zw, n)
        for k, p in enumerate(p_peers):
            send(out_ref.at[zw, n], zw, n, p_sem.at[j, k], (w, p))
        send(out_ref.at[zw, n], zw, n, c_sem.at[j, 0], (w, core))
    for i in range(1, half):
        zn = lax.rem(q + half - i, half) * 2 + parity
        for j in range(wides):
            zw = lax.rem(w + wides - j, wides)
            arrived(zw, zn)
            send(out_ref.at[zw, zn], zw, zn, c_sem.at[j, i], (w, core))
    for i in range(half):
        for j in range(wides):
            arrived(j, 2 * i + 1 - parity)
    own.wait()
    for copy in sends:
        copy.wait_send()


def gather_shared(shard, wides, narrows):
    half = narrows // 2
    hbm = pl.BlockSpec(memory_space=pl.ANY)
    return pl.pallas_call(
        functools.partial(gather_kernel, wides, narrows),
        out_shape=jax.ShapeDtypeStruct((wides, narrows) + shard.shape, shard.dtype),
        in_specs=[hbm],
        out_specs=hbm,
        scratch_shapes=[
            pltpu.SemaphoreType.DMA,
            pltpu.SemaphoreType.DMA((wides - 1,)),
            pltpu.SemaphoreType.DMA((wides, half - 1)),
            pltpu.SemaphoreType.DMA((wides, half)),
            pltpu.SemaphoreType.DMA((wides, narrows)),
        ],
        compiler_params=pltpu.CompilerParams(collective_id=0, has_side_effects=True),
        name="gather_shared",
    )(shard)


def norm_rows(extra, experts):
    turned = jnp.transpose(extra.astype(F32))
    return turned[experts : experts + 4] + turned[experts + 4 : experts + 8] + turned[experts + 8 : experts + 12]


def fwd_kernel(experts, slot_ref, x_ref, wts_ref, qkv_ref, o_ref, lse_ref, hid_ref, u_ref, lse_col, nrm_ref):
    length, width = x_ref.shape[1:]
    blocks = length // ROWS
    head = width // HEADS
    scale = 1.0 / math.sqrt(head)
    wq = wts_ref.at[:, pl.ds(0, 3 * width)]
    wo = wts_ref.at[:, pl.ds(3 * width, width)]
    nrm_ref[0:4, :] = norm_rows(wts_ref[:, 4 * width :], experts)

    def project(i, _):
        at = pl.ds(i * ROWS, ROWS)
        xhat, _ = norm_stats(x_ref[0, at, :].astype(F32))
        al = (xhat * nrm_ref[0:1, :] + nrm_ref[1:2, :]).astype(BF)
        qkv_ref[0, at, :] = dot(al, wq[...], 1, 0).astype(BF)
        return 0

    lax.fori_loop(0, blocks, project, 0)
    lse_col[...] = jnp.zeros_like(lse_col)
    lane = lax.broadcasted_iota(jnp.int32, (1, LANES), 1)
    keep = lax.broadcasted_iota(jnp.int32, (ROWS, ROWS), 1) <= lax.broadcasted_iota(jnp.int32, (ROWS, ROWS), 0)
    for i in range(blocks):
        keys = (i + 1) * ROWS
        at = pl.ds(i * ROWS, ROWS)

        def pair(hp, _, i=i, keys=keys, at=at):
            lanes = pl.ds(pl.multiple_of(hp * LANES, LANES), LANES)
            klanes = pl.ds(pl.multiple_of(hp * LANES + width, LANES), LANES)
            vlanes = pl.ds(pl.multiple_of(hp * LANES + 2 * width, LANES), LANES)
            q = qkv_ref[0, at, lanes]
            k = qkv_ref[0, pl.ds(0, keys), klanes]
            v = qkv_ref[0, pl.ds(0, keys), vlanes]
            acc = None
            for h in range(2):
                mine = lane // head == h
                qm = jnp.where(mine, q * scale, 0).astype(BF)
                vm = jnp.where(mine, v, 0).astype(BF)
                s = dot(qm, k, 1, 1)
                diag = jnp.where(keep, s[:, i * ROWS :], NEG_LARGE)
                s = diag if i == 0 else jnp.concatenate([s[:, : i * ROWS], diag], axis=1)
                m = jnp.max(s, axis=1, keepdims=True)
                p = jnp.exp(s - m)
                total = jnp.sum(p, axis=1, keepdims=True)
                part = dot((p * (1.0 / total)).astype(BF), vm, 1, 0)
                acc = part if acc is None else acc + part
                lse_col[at, :] = jnp.where(lane == hp * 2 + h, m + jnp.log(total), lse_col[at, :])
            o_ref[0, at, lanes] = acc.astype(BF)
            return 0

        lax.fori_loop(0, HEADS // 2, pair, 0)
    lse_ref[0] = jnp.transpose(lse_col[...])[:HEADS, :]

    def finish(i, _):
        at = pl.ds(i * ROWS, ROWS)
        hidden = x_ref[0, at, :].astype(F32) + dot(o_ref[0, at, :], wo[...], 1, 0)
        hid_ref[0, at, :] = hidden
        xhat, _ = norm_stats(hidden)
        u_ref[0, at, :] = (xhat * nrm_ref[2:3, :] + nrm_ref[3:4, :]).astype(BF)
        return 0

    lax.fori_loop(0, blocks, finish, 0)


def whole_spec(shape):
    return pl.BlockSpec(shape, lambda i, s: (0,) * len(shape))


def each_spec(*shape):
    return pl.BlockSpec((1,) + shape, lambda i, s: (i,) + (0,) * len(shape))


def attend(slots, tokens, wts, experts):
    count, length, width = tokens.shape
    return pl.pallas_call(
        functools.partial(fwd_kernel, experts),
        grid_spec=pltpu.PrefetchScalarGridSpec(
            num_scalar_prefetch=1,
            grid=(count,),
            in_specs=[pl.BlockSpec((1, length, width), lambda i, s: (s[i], 0, 0)), whole_spec(wts.shape)],
            out_specs=[
                each_spec(length, 3 * width),
                each_spec(length, width),
                each_spec(HEADS, length),
                each_spec(length, width),
                each_spec(length, width),
            ],
            scratch_shapes=[pltpu.VMEM((length, LANES), F32), pltpu.VMEM((8, width), F32)],
        ),
        out_shape=[
            jax.ShapeDtypeStruct((count, length, 3 * width), BF),
            jax.ShapeDtypeStruct((count, length, width), BF),
            jax.ShapeDtypeStruct((count, HEADS, length), F32),
            jax.ShapeDtypeStruct((count, length, width), F32),
            jax.ShapeDtypeStruct((count, length, width), BF),
        ],
        compiler_params=pltpu.CompilerParams(vmem_limit_bytes=56 << 20),
        name="attention",
    )(slots, tokens, wts)


def bwd_kernel(experts, slot_ref, x_ref, cf_ref, md_ref, hid_ref, qkv_ref, o_ref, lse_ref, wts_ref,
               gt_ref, out_ref, dwq_ref, dwo_ref, dex_ref, dh_ref, do_ref, dqkv_ref, dk_ref, dv_ref, nrm_ref, dn_ref):
    length, width = x_ref.shape[1:]
    blocks = length // ROWS
    part = md_ref.shape[3]
    parts = ROWS // part
    head = width // HEADS
    scale = 1.0 / math.sqrt(head)
    wq = wts_ref.at[:, pl.ds(0, 3 * width)]
    wo = wts_ref.at[:, pl.ds(3 * width, width)]
    nrm_ref[0:4, :] = norm_rows(wts_ref[:, 4 * width :], experts)

    @pl.when(pl.program_id(0) == 0)
    def _():
        dwq_ref[...] = jnp.zeros_like(dwq_ref)
        dwo_ref[...] = jnp.zeros_like(dwo_ref)
        dn_ref[...] = jnp.zeros_like(dn_ref)

    def first(i, _):
        at = pl.ds(i * ROWS, ROWS)
        hidden = hid_ref[0, at, :]
        mix = md_ref[0, pl.ds(i * parts, parts), 0].reshape(ROWS, width).astype(F32)
        out_ref[0, at, :] = (hidden + mix).astype(BF)
        xhat, rstd = norm_stats(hidden)
        du = md_ref[0, pl.ds(i * parts, parts), 1].reshape(ROWS, width).astype(F32)
        dn_ref[2:3, :] += jnp.sum(du * xhat, axis=0, keepdims=True)
        dn_ref[3:4, :] += jnp.sum(du, axis=0, keepdims=True)
        dh = cf_ref[0, at, :].astype(F32) + norm_back(du, nrm_ref[2:3, :], xhat, rstd)
        dh_ref[at, :] = dh
        db = dh.astype(BF)
        do_ref[at, :] = dot(db, wo[...], 1, 1).astype(BF)
        dwo_ref[...] += dot(o_ref[0, at, :], db, 0, 0)
        return 0

    lax.fori_loop(0, blocks, first, 0)
    lane = lax.broadcasted_iota(jnp.int32, (1, LANES), 1)
    keep = lax.broadcasted_iota(jnp.int32, (ROWS, ROWS), 0) <= lax.broadcasted_iota(jnp.int32, (ROWS, ROWS), 1)

    def pair(hp, _):
        lanes = pl.ds(pl.multiple_of(hp * LANES, LANES), LANES)
        klanes = pl.ds(pl.multiple_of(hp * LANES + width, LANES), LANES)
        vlanes = pl.ds(pl.multiple_of(hp * LANES + 2 * width, LANES), LANES)
        for i in range(blocks):
            keys = (i + 1) * ROWS
            at = pl.ds(i * ROWS, ROWS)
            q = qkv_ref[0, at, lanes]
            k = qkv_ref[0, pl.ds(0, keys), klanes]
            v = qkv_ref[0, pl.ds(0, keys), vlanes]
            do = do_ref[at, lanes]
            dq = dk = dv = None
            for h in range(2):
                mine = lane // head == h
                qm = jnp.where(mine, q * scale, 0).astype(BF)
                dom = jnp.where(mine, do, 0).astype(BF)
                km = jnp.where(mine, k * scale, 0).astype(BF)
                s = dot(k, qm, 1, 1)
                s = s - lse_ref[0, pl.ds(hp * 2 + h, 1), at]
                diag = jnp.where(keep, s[i * ROWS :], NEG_LARGE)
                p = jnp.exp(diag if i == 0 else jnp.concatenate([s[: i * ROWS], diag], axis=0))
                pdp = p * dot(v, dom, 1, 1)
                inner = jnp.sum(pdp, axis=0, keepdims=True)
                ds = (pdp - p * inner).astype(BF)
                a = dot(p.astype(BF), dom, 1, 0)
                b = dot(ds, qm, 1, 0)
                c = dot(ds, km, 0, 0)
                dv, dk, dq = (a, b, c) if h == 0 else (dv + a, dk + b, dq + c)
            dqkv_ref[at, lanes] = dq.astype(BF)
            if i:
                dk_ref[: i * ROWS, :] += dk[: i * ROWS]
                dv_ref[: i * ROWS, :] += dv[: i * ROWS]
            dk_ref[i * ROWS : keys, :] = dk[i * ROWS :]
            dv_ref[i * ROWS : keys, :] = dv[i * ROWS :]
        dqkv_ref[:, klanes] = dk_ref[...].astype(BF)
        dqkv_ref[:, vlanes] = dv_ref[...].astype(BF)
        return 0

    lax.fori_loop(0, HEADS // 2, pair, 0)

    def last(i, _):
        at = pl.ds(i * ROWS, ROWS)
        xhat, rstd = norm_stats(x_ref[0, at, :].astype(F32))
        al = (xhat * nrm_ref[0:1, :] + nrm_ref[1:2, :]).astype(BF)
        dqkv = dqkv_ref[at, :]
        dwq_ref[...] += dot(al, dqkv, 0, 0)
        da = dot(dqkv, wq[...], 1, 1)
        dn_ref[0:1, :] += jnp.sum(da * xhat, axis=0, keepdims=True)
        dn_ref[1:2, :] += jnp.sum(da, axis=0, keepdims=True)
        gt_ref[0, at, :] = dh_ref[at, :] + norm_back(da, nrm_ref[0:1, :], xhat, rstd)
        return 0

    lax.fori_loop(0, blocks, last, 0)

    @pl.when(pl.program_id(0) == pl.num_programs(0) - 1)
    def _():
        stacked = jnp.concatenate([dn_ref[...], jnp.zeros((LANES - 8, width), F32)], axis=0)
        dex_ref[...] = jnp.transpose(stacked)


def attend_back(slots, tokens, cot, moved, hid, qkv, o, lse, wts, experts):
    count, length, width = tokens.shape
    slot = pl.BlockSpec((1, length, width), lambda i, s: (s[i], 0, 0))
    return pl.pallas_call(
        functools.partial(bwd_kernel, experts),
        grid_spec=pltpu.PrefetchScalarGridSpec(
            num_scalar_prefetch=1,
            grid=(count,),
            in_specs=[
                slot,
                slot,
                each_spec(*moved.shape[1:]),
                each_spec(length, width),
                each_spec(length, 3 * width),
                each_spec(length, width),
                each_spec(HEADS, length),
                whole_spec(wts.shape),
            ],
            out_specs=[
                slot,
                slot,
                whole_spec((width, 3 * width)),
                whole_spec((width, width)),
                whole_spec((width, LANES)),
            ],
            scratch_shapes=[
                pltpu.VMEM((length, width), F32),
                pltpu.VMEM((length, width), BF),
                pltpu.VMEM((length, 3 * width), BF),
                pltpu.VMEM((length, LANES), F32),
                pltpu.VMEM((length, LANES), F32),
                pltpu.VMEM((8, width), F32),
                pltpu.VMEM((8, width), F32),
            ],
        ),
        out_shape=[
            jax.ShapeDtypeStruct((count, length, width), F32),
            jax.ShapeDtypeStruct((count, length, width), BF),
            jax.ShapeDtypeStruct((width, 3 * width), F32),
            jax.ShapeDtypeStruct((width, width), F32),
            jax.ShapeDtypeStruct((width, LANES), F32),
        ],
        compiler_params=pltpu.CompilerParams(vmem_limit_bytes=60 << 20),
        name="attention_back",
    )(slots, tokens, cot, moved, hid, qkv, o, lse, wts)


def expert_kernel(narrows, counts, u_ref, cf_ref, live_ref, wc_ref, upd_ref,
                  md_ref, grad_ref, dwc_ref,
                  in_buf, xd_out, xd_in, yx_out, yx_in, md_out, w_buf, du_buf, dw_buf, up_buf, down_buf, dup, ddown,
                  load_sem, send_sem, recv_sem):
    w_id, me = lax.axis_index("wide"), lax.axis_index("narrow")
    micros, length, width = counts
    part = length // narrows
    chunk_parts = ROWS // part
    hidden_width = up_buf.shape[1]
    wides = upd_ref.shape[0]
    up_rows = width // wides
    down_rows = hidden_width // wides
    folds = hidden_width // width
    fold_rows = down_rows // folds
    lane = lax.broadcasted_iota(jnp.int32, (1, LANES), 1)

    loads = []
    for j in range(wides):
        loads.append(pltpu.make_async_copy(
            upd_ref.at[j, pl.ds(0, up_rows)], up_buf.at[pl.ds(j * up_rows, up_rows)], load_sem.at[j, 0]))
        for c in range(folds):
            loads.append(pltpu.make_async_copy(
                upd_ref.at[j, pl.ds(up_rows, fold_rows), pl.ds(c * width, width)],
                down_buf.at[pl.ds(j * down_rows + c * fold_rows, fold_rows)], load_sem.at[j, 1 + c]))
    for copy in loads:
        copy.start()
    greet([(w_id, lax.rem(me + k, narrows)) for k in range(1, narrows)])
    dup[...] = jnp.zeros_like(dup)
    ddown[...] = jnp.zeros_like(ddown)
    dwc_ref[...] = jnp.zeros_like(dwc_ref)

    def send(stage, mb, source, target, peer):
        @pl.when(peer != me)
        def _():
            remote(source, target, send_sem.at[stage, mb, peer], recv_sem.at[stage, mb, me], (w_id, peer)).start()

        @pl.when(peer == me)
        def _():
            pltpu.make_async_copy(source, target, recv_sem.at[stage, mb, me]).start()

    def received(stage, mb, peer, target):
        pltpu.make_async_copy(target, target, recv_sem.at[stage, mb, peer]).wait()

    def sent(stage, mb, source):
        def one(k, _):
            peer = lax.rem(me + k, narrows)
            pltpu.make_async_copy(source, source, send_sem.at[stage, mb, peer]).wait()
            return 0

        lax.fori_loop(1, narrows, one, 0)

    def send_rows(mb):
        def one(k, _):
            peer = lax.rem(me + k, narrows)
            rows = pl.ds(peer * part, part)
            send(0, mb, u_ref.at[mb, rows], in_buf.at[mb, me, 0], peer)
            send(1, mb, cf_ref.at[mb, rows], in_buf.at[mb, me, 1], peer)
            return 0

        lax.fori_loop(0, narrows, one, 0)

    def mix(mb):
        def logits(n, _):
            received(0, mb, n, in_buf.at[mb, n, 0])
            received(1, mb, n, in_buf.at[mb, n, 1])
            w_buf[mb, n] = dot(in_buf[mb, n, 0], wc_ref[...], 1, 0).astype(BF).astype(F32)
            return 0

        lax.fori_loop(0, narrows, logits, 0)

        def rows_of(c, _):
            at = pl.ds(c * 16, 16)
            logit = [
                jnp.where(live_ref[mb, pl.ds(n, 1), :] > 0, w_buf[mb, n, at, :], NEG_LARGE) for n in range(narrows)
            ]
            top = functools.reduce(jnp.maximum, logit)
            exps = [jnp.exp(logit[n] - top) * live_ref[mb, pl.ds(n, 1), :] for n in range(narrows)]
            total = functools.reduce(jnp.add, exps)
            inverse = 1.0 / total
            weights = [e * inverse for e in exps]
            for n in range(narrows):
                w_buf[mb, n, at, :] = weights[n]
            for which in range(2):
                values = [in_buf[mb, n, which, at, :].astype(F32) for n in range(narrows)]
                for e in range(narrows):
                    acc = functools.reduce(
                        jnp.add, [weights[n][:, e : e + 1] * values[n] for n in range(narrows)])
                    xd_out[mb, e, which, at, :] = acc.astype(BF)
            return 0

        lax.fori_loop(0, part // 16, rows_of, 0)

        def one(k, _):
            peer = lax.rem(me + k, narrows)
            send(2, mb, xd_out.at[mb, peer], xd_in.at[mb, me], peer)
            return 0

        lax.fori_loop(0, narrows, one, 0)

    def expert(mb):
        def chunk(c, _):
            at = pl.ds(c * chunk_parts, chunk_parts)
            for k in range(chunk_parts):
                received(2, mb, c * chunk_parts + k, xd_in.at[mb, c * chunk_parts + k])
            x = xd_in[mb, at, 0].reshape(ROWS, width)
            dy = xd_in[mb, at, 1].reshape(ROWS, width)

            def tile(j, carry):
                y, dx = carry
                cols = pl.ds(pl.multiple_of(j * width, width), width)
                z = dot(x, up_buf[:, cols], 1, 0)
                zz = z * z
                t = jnp.tanh(GELU_A * (z + GELU_B * z * zz))
                ga = (0.5 * z * (1.0 + t)).astype(BF)
                slope = 0.5 * (1.0 + t) + (0.5 * GELU_A) * z * (1.0 - t * t) * (1.0 + (3.0 * GELU_B) * zz)
                y = y + dot(ga, down_buf[cols, :], 1, 0)
                dz = (dot(dy, down_buf[cols, :], 1, 1) * slope).astype(BF)
                dx = dx + dot(dz, up_buf[:, cols], 1, 1)
                ddown[cols, :] += dot(ga, dy, 0, 0)
                dup[:, cols] += dot(x, dz, 0, 0)
                return y, dx

            zero = jnp.zeros((ROWS, width), F32)
            y, dx = lax.fori_loop(0, folds, tile, (zero, zero))
            yx_out[mb, at, 0] = y.astype(BF).reshape(chunk_parts, part, width)
            yx_out[mb, at, 1] = dx.astype(BF).reshape(chunk_parts, part, width)
            for k in range(chunk_parts):
                peer = c * chunk_parts + k
                send(3, mb, yx_out.at[mb, peer], yx_in.at[mb, me], peer)
            return 0

        lax.fori_loop(0, length // ROWS, chunk, 0)

    def combine(mb):
        def wait(e, _):
            received(3, mb, e, yx_in.at[mb, e])
            return 0

        lax.fori_loop(0, narrows, wait, 0)

        def member(n, _):
            def rows_of(c, _):
                at = pl.ds(c * 16, 16)
                u = in_buf[mb, n, 0, at, :].astype(F32)
                cf = in_buf[mb, n, 1, at, :].astype(F32)
                weights = w_buf[mb, n, at, :]
                mixed = du = None
                dw = jnp.zeros((16, LANES), F32)
                for e in range(narrows):
                    y = yx_in[mb, e, 0, at, :].astype(F32)
                    dx = yx_in[mb, e, 1, at, :].astype(F32)
                    weight = weights[:, e : e + 1]
                    mixed = weight * y if e == 0 else mixed + weight * y
                    du = weight * dx if e == 0 else du + weight * dx
                    dw = jnp.where(lane == e, jnp.sum(dx * u + cf * y, axis=1, keepdims=True), dw)
                md_out[mb, n, 0, at, :] = mixed.astype(BF)
                du_buf[n, at, :] = du
                dw_buf[n, at, :] = dw
                return 0

            lax.fori_loop(0, part // 16, rows_of, 0)
            return 0

        lax.fori_loop(0, narrows, member, 0)

        def group(n, acc):
            return acc + w_buf[mb, n] * dw_buf[n]

        inner = lax.fori_loop(0, narrows, group, jnp.zeros((part, LANES), F32))

        def finish(n, _):
            dc = (w_buf[mb, n] * (dw_buf[n] - inner)).astype(BF)
            du = du_buf[n] + dot(dc, wc_ref[...], 1, 1)
            md_out[mb, n, 1] = du.astype(BF)
            dwc_ref[...] += dot(in_buf[mb, n, 0], dc, 0, 0)
            send(4, mb, md_out.at[mb, n], md_ref.at[mb, me], n)
            return 0

        lax.fori_loop(0, narrows, finish, 0)

    send_rows(0)
    for copy in loads:
        copy.wait()
    for mb in range(micros):
        if mb + 1 < micros:
            send_rows(mb + 1)
        mix(mb)
    for mb in range(micros):
        expert(mb)
    for mb in range(micros):
        combine(mb)
    for j in range(wides):
        grad_ref[j, :up_rows] = dup[j * up_rows : (j + 1) * up_rows].astype(BF)
        for c in range(folds):
            rows = j * down_rows + c * fold_rows
            grad_ref[j, up_rows:, c * width : (c + 1) * width] = ddown[rows : rows + fold_rows].astype(BF)
    for mb in range(micros):
        def wait(p, _, mb=mb):
            received(4, mb, p, md_ref.at[mb, p])
            return 0

        lax.fori_loop(0, narrows, wait, 0)
        sent(0, mb, in_buf.at[mb, 0, 0])
        sent(1, mb, in_buf.at[mb, 0, 1])
        sent(2, mb, xd_out.at[mb, 0])
        sent(3, mb, yx_out.at[mb, 0])
        sent(4, mb, md_out.at[mb, 0])


def run_experts(u, cf, live, wc, upd, narrows):
    micros, length, width = u.shape
    part = length // narrows
    wides, packed_rows, hidden_width = upd.shape
    folds = hidden_width // width
    hbm = pl.BlockSpec(memory_space=pl.ANY)
    vmem = pl.BlockSpec(memory_space=pltpu.VMEM)
    pairs = pltpu.VMEM((micros, narrows, 2, part, width), BF)
    return pl.pallas_call(
        functools.partial(expert_kernel, narrows, (micros, length, width)),
        out_shape=[
            jax.ShapeDtypeStruct((micros, narrows, 2, part, width), BF),
            jax.ShapeDtypeStruct(upd.shape, BF),
            jax.ShapeDtypeStruct((width, LANES), F32),
        ],
        in_specs=[hbm, hbm, vmem, vmem, hbm],
        out_specs=[hbm, vmem, vmem],
        scratch_shapes=[pairs] * 6 + [
            pltpu.VMEM((micros, narrows, part, LANES), F32),
            pltpu.VMEM((narrows, part, width), F32),
            pltpu.VMEM((narrows, part, LANES), F32),
            pltpu.VMEM((width, hidden_width), BF),
            pltpu.VMEM((hidden_width, width), BF),
            pltpu.VMEM((width, hidden_width), F32),
            pltpu.VMEM((hidden_width, width), F32),
            pltpu.SemaphoreType.DMA((wides, 1 + folds)),
            pltpu.SemaphoreType.DMA((5, micros, narrows)),
            pltpu.SemaphoreType.DMA((5, micros, narrows)),
        ],
        compiler_params=pltpu.CompilerParams(
            collective_id=1, has_side_effects=True, vmem_limit_bytes=62 << 20),
        name="experts",
    )(u, cf, live, wc, upd)


def reduce_kernel(wides, narrows, wq_ref, wo_ref, ex_ref, dwc_ref, out_ref,
                  s1, r1, s2, r2, s3, r3, total, c_sem, p_sem, z_sem, cr_sem, pr_sem, zr_sem):
    w, n = lax.axis_index("wide"), lax.axis_index("narrow")
    half = narrows // 2
    q, parity = n // 2, lax.rem(n, 2)
    core = n + 1 - 2 * parity
    z_peers = [lax.rem(w + k, wides) for k in range(1, wides)]
    p_peers = [lax.rem(q + k, half) for k in range(1, half)]
    greet([(w, core)] + [(w, p * 2 + parity) for p in p_peers] + [(z, n) for z in z_peers])
    a, b = wq_ref.shape[2], wq_ref.shape[2] + wo_ref.shape[2]

    def parts(index):
        return wq_ref[index], wo_ref[index], ex_ref[index] + dwc_ref[index]

    sends = []
    for k in range(half):
        there = lax.rem(q + 1 + k, half)

        def fill(z, _, there=there):
            one, two, three = parts(z * narrows + 2 * there + 1 - parity)
            s1[there, z, :, :a] = one.astype(BF)
            s1[there, z, :, a:b] = two.astype(BF)
            s1[there, z, :, b:] = three.astype(BF)
            return 0

        lax.fori_loop(0, wides, fill, 0)
        copy = remote(s1.at[there], r1.at[there], c_sem.at[k], cr_sem.at[there], (w, core))
        copy.start()
        sends.append(copy)
    for k in range(half):
        there = lax.rem(q + 1 + k, half)
        remote(s1.at[there], r1.at[there], c_sem.at[k], cr_sem.at[there], (w, core)).wait_recv()
        last = k == half - 1

        def add(z, _, there=there, last=last):
            one, two, three = parts(z * narrows + 2 * there + parity)
            got = r1[there, z].astype(F32)
            one, two, three = one + got[:, :a], two + got[:, a:b], three + got[:, b:]
            if last:
                total[z, :, :a], total[z, :, a:b], total[z, :, b:] = one, two, three
            else:
                s2[there, z, :, :a] = one.astype(BF)
                s2[there, z, :, a:b] = two.astype(BF)
                s2[there, z, :, b:] = three.astype(BF)
            return 0

        lax.fori_loop(0, wides, add, 0)
        if not last:
            copy = remote(s2.at[there], r2.at[q], p_sem.at[k], pr_sem.at[q], (w, there * 2 + parity))
            copy.start()
            sends.append(copy)
    for k in range(1, half):
        there = lax.rem(q + k, half)
        remote(s2.at[there], r2.at[there], p_sem.at[0], pr_sem.at[there], (w, n)).wait_recv()
    for k in range(wides):
        z = lax.rem(w + 1 + k, wides)
        acc = total[z]
        for i in range(1, half):
            acc = acc + r2[lax.rem(q + i, half), z].astype(F32)
        if k < wides - 1:
            s3[z] = acc.astype(BF)
            copy = remote(s3.at[z], r3.at[w], z_sem.at[k], zr_sem.at[w], (z, n))
            copy.start()
            sends.append(copy)
        else:
            out_ref[...] = acc
    for k in range(1, wides):
        z = lax.rem(w + k, wides)
        remote(s3.at[z], r3.at[z], z_sem.at[0], zr_sem.at[z], (w, n)).wait_recv()
        out_ref[...] += r3[z].astype(F32)
    for copy in sends:
        copy.wait_send()


def reduce_shared(dwq, dwo, dex, dwc, wides, narrows):
    half = narrows // 2
    rows = dwq.shape[1]
    cols = dwq.shape[2] + dwo.shape[2] + dex.shape[2]
    vmem = pl.BlockSpec(memory_space=pltpu.VMEM)
    block = (half, wides, rows, cols)
    sems = pltpu.SemaphoreType.DMA
    return pl.pallas_call(
        functools.partial(reduce_kernel, wides, narrows),
        out_shape=jax.ShapeDtypeStruct((rows, cols), F32),
        in_specs=[vmem] * 4,
        out_specs=vmem,
        scratch_shapes=[pltpu.VMEM(block, BF)] * 4
        + [pltpu.VMEM(block[1:], BF)] * 2
        + [pltpu.VMEM(block[1:], F32)]
        + [sems((half,)), sems((half,)), sems((wides,))] * 2,
        compiler_params=pltpu.CompilerParams(
            collective_id=2, has_side_effects=True, vmem_limit_bytes=60 << 20),
        name="reduce_shared",
    )(dwq, dwo, dex, dwc)


def total_kernel(wides, narrows, part_ref, out_ref, got_n, mid, got_w, send_n, recv_n, send_w, recv_w):
    w, n = lax.axis_index("wide"), lax.axis_index("narrow")
    n_peers = [lax.rem(n + k, narrows) for k in range(1, narrows)]
    z_peers = [lax.rem(w + k, wides) for k in range(1, wides)]
    greet([(w, p) for p in n_peers] + [(z, n) for z in z_peers])
    sends = []
    for k, p in enumerate(n_peers):
        copy = remote(part_ref, got_n.at[n], send_n.at[k], recv_n.at[n], (w, p))
        copy.start()
        sends.append(copy)
    got_n[n] = part_ref[...]
    for p in n_peers:
        remote(part_ref, got_n.at[p], send_n.at[0], recv_n.at[p], (w, n)).wait_recv()
    acc = got_n[0]
    for k in range(1, narrows):
        acc = acc + got_n[k]
    mid[...] = acc
    got_w[w] = acc
    for k, z in enumerate(z_peers):
        copy = remote(mid, got_w.at[w], send_w.at[k], recv_w.at[w], (z, n))
        copy.start()
        sends.append(copy)
    for z in z_peers:
        remote(mid, got_w.at[z], send_w.at[0], recv_w.at[z], (w, n)).wait_recv()
    acc = got_w[0]
    for k in range(1, wides):
        acc = acc + got_w[k]
    out_ref[...] = acc
    for copy in sends:
        copy.wait_send()


def sum_everywhere(part, wides, narrows):
    vmem = pl.BlockSpec(memory_space=pltpu.VMEM)
    sems = pltpu.SemaphoreType.DMA
    return pl.pallas_call(
        functools.partial(total_kernel, wides, narrows),
        out_shape=jax.ShapeDtypeStruct(part.shape, F32),
        in_specs=[vmem],
        out_specs=vmem,
        scratch_shapes=[
            pltpu.VMEM((narrows,) + part.shape, F32),
            pltpu.VMEM(part.shape, F32),
            pltpu.VMEM((wides,) + part.shape, F32),
            sems((narrows - 1,)),
            sems((narrows,)),
            sems((wides - 1,)),
            sems((wides,)),
        ],
        compiler_params=pltpu.CompilerParams(collective_id=3, has_side_effects=True),
        name="sum_everywhere",
    )(part)


def adam_update(weight, first_state, second_state, gradient, factor, rate, decay):
    clipped = gradient * factor
    first_new = BETA_ONE * first_state + (1.0 - BETA_ONE) * clipped
    second_new = BETA_TWO * second_state + (1.0 - BETA_TWO) * clipped * clipped
    first_hat = first_new / (1.0 - BETA_ONE**STEP)
    second_hat = second_new / (1.0 - BETA_TWO**STEP)
    weight_new = weight - rate * (first_hat / (jnp.sqrt(second_hat) + ADAM_EPS) + decay * weight)
    return (weight_new, first_new, second_new, weight_new.astype(BF))


def per_device(
    tokens, cotangent, seq_counts, micro_assign,
    norm_params, norm_first, norm_second,
    project_weight, project_first, project_second,
    output_weight, output_first, output_second,
    control_weight, control_first, control_second,
    up_weight, up_first, up_second,
    down_weight, down_first, down_second,
):
    wides, narrows = lax.axis_size("wide"), lax.axis_size("narrow")
    wide_index, narrow_index = lax.axis_index("wide"), lax.axis_index("narrow")
    devices = wides * narrows
    micro_count, length, width = tokens.shape
    experts = control_weight.shape[1]
    rows = project_weight.shape[0]
    padded = max(rows, 16)
    hidden_width = up_weight.shape[2]
    folds = hidden_width // width

    first_device = wide_index * narrows
    row_counts = lax.dynamic_slice_in_dim(seq_counts, first_device, narrows)
    row_assign = lax.dynamic_slice_in_dim(micro_assign, first_device, narrows, 0)
    slot_numbers = jnp.arange(micro_count, dtype=jnp.int32)
    micros = jnp.arange(micro_count, dtype=jnp.int32)
    member_slots = jnp.sum(
        slot_numbers[None, None, :] * (row_assign[None] == micros[:, None, None]).astype(jnp.int32), axis=2
    )
    live = (member_slots < row_counts[None]).astype(F32)
    live = jnp.broadcast_to(live[:, :, None], (micro_count, narrows, LANES))
    slots = lax.dynamic_index_in_dim(member_slots, narrow_index, 1, keepdims=False)

    norm_turned = norm_params.T
    high = lax.reduce_precision(norm_turned, 8, 7)
    middle = lax.reduce_precision(norm_turned - high, 8, 7)
    lower = norm_turned - high - middle
    extra = jnp.concatenate([control_weight, high, middle, lower], axis=1).astype(BF)
    extra = jnp.pad(extra, ((0, 0), (0, LANES - extra.shape[1])))
    shard = jnp.concatenate([project_weight.astype(BF), output_weight.astype(BF), extra], axis=1)
    shard = jnp.pad(shard, ((0, padded - rows), (0, 0)))
    wts = gather_shared(shard, wides, narrows).reshape(devices, padded, -1)[:, :rows].reshape(width, -1)

    down_rows = down_weight.shape[1]
    fold_rows = down_rows // folds
    down_folded = down_weight[0].reshape(folds, fold_rows, width).transpose(1, 0, 2).reshape(fold_rows, hidden_width)
    packed = jnp.concatenate([up_weight[0], down_folded], axis=0).astype(BF)
    upd = lax.all_gather(packed, "wide", axis=0, tiled=False)

    qkv, o, lse, hid, u = attend(slots, tokens, wts, experts)
    cf = jnp.stack([lax.dynamic_index_in_dim(cotangent, slots[k], 0, keepdims=False) for k in range(micro_count)])
    wc = jnp.where(jnp.arange(LANES)[None, :] < experts, wts[:, 4 * width :], 0)
    moved, grads, dwc = run_experts(u, cf, live, wc, upd, narrows)
    expert_grad = lax.psum_scatter(grads, "wide", scatter_dimension=0, tiled=False).astype(F32)

    grad_tokens, out_rows, dwq, dwo, dex = attend_back(
        slots, tokens, cotangent, moved, hid, qkv, o, lse, wts, experts)
    dex = jnp.roll(dex, experts, axis=1)

    def by_owner(grad):
        return jnp.pad(grad.reshape(devices, rows, -1), ((0, 0), (0, padded - rows), (0, 0)))

    shared = reduce_shared(by_owner(dwq), by_owner(dwo), by_owner(dex), by_owner(dwc), wides, narrows)[:rows]
    project_grad = shared[:, : 3 * width]
    output_grad = shared[:, 3 * width : 4 * width]
    control_grad = shared[:, 4 * width : 4 * width + experts]
    norm_grad = shared[:, 4 * width + experts : 4 * width + experts + 4].T
    up_rows = up_weight.shape[1]
    up_grad = expert_grad[None, :up_rows]
    down_grad = (
        expert_grad[up_rows:].reshape(fold_rows, folds, width).transpose(1, 0, 2).reshape(1, down_rows, width)
    )
    squares = jnp.sum(shared * shared) + jnp.sum(expert_grad * expert_grad)
    total = sum_everywhere(jnp.full((8, LANES), squares, F32), wides, narrows)
    grad_norm = jnp.sqrt(total[0, 0])
    factor = CLIP_NORM / jnp.maximum(grad_norm, CLIP_NORM)
    norm_out = adam_update(norm_params, norm_first, norm_second, norm_grad, factor, 0.3, 0.0)
    project_out = adam_update(
        project_weight, project_first, project_second, project_grad, factor, 0.03, DECAY_RATE)
    output_out = adam_update(output_weight, output_first, output_second, output_grad, factor, 0.2, DECAY_RATE)
    control_out = adam_update(
        control_weight, control_first, control_second, control_grad, factor, 0.015, DECAY_RATE)
    up_out = adam_update(up_weight, up_first, up_second, up_grad, factor, 0.1, DECAY_RATE)
    down_out = adam_update(down_weight, down_first, down_second, down_grad, factor, 0.1, DECAY_RATE)
    return (out_rows, grad_tokens, grad_norm) + norm_out + project_out + output_out + control_out + up_out + down_out


def solution(mesh):
    both = ("wide", "narrow")
    rows3, cols, rows2, expert = P(both, None, None), P(None, both), P(both, None), P("narrow", "wide", None)
    return jax.shard_map(
        per_device,
        mesh=mesh,
        in_specs=(rows3, rows3, P(), P()) + (cols,) * 3 + (rows2,) * 9 + (expert,) * 6,
        out_specs=(rows3, rows3, P()) + (cols,) * 4 + (rows2,) * 12 + (expert,) * 8,
        check_vma=False,
    )
```

```python
import functools
import math

import jax
import jax.numpy as jnp
from jax import lax
from jax.experimental import pallas as pl
from jax.experimental.pallas import tpu as pltpu
from jax.sharding import PartitionSpec as P

HEADS = 8
STEP = 5
NEG_LARGE = -1e30
NORM_EPS = 1e-05
CLIP_NORM = 0.05
BETA_ONE = 0.5
BETA_TWO = 0.5
ADAM_EPS = 1e-08
DECAY_RATE = 0.1

BF = jnp.bfloat16
F32 = jnp.float32
MESH = pl.DeviceIdType.MESH
LANES = 128
ROWS = 256
GELU_A = math.sqrt(2.0 / math.pi)
GELU_B = 0.044715


def dot(a, b, ca, cb):
    return lax.dot_general(a, b, (((ca,), (cb,)), ((), ())), preferred_element_type=F32)


def norm_stats(v):
    centred = v - jnp.mean(v, axis=-1, keepdims=True)
    rstd = lax.rsqrt(jnp.mean(centred * centred, axis=-1, keepdims=True) + NORM_EPS)
    return centred * rstd, rstd


def norm_back(grad, gain, xhat, rstd):
    t = grad * gain
    return rstd * (t - jnp.mean(t, axis=-1, keepdims=True) - xhat * jnp.mean(t * xhat, axis=-1, keepdims=True))


def remote(src, dst, send, recv, device):
    return pltpu.make_async_remote_copy(
        src_ref=src, dst_ref=dst, send_sem=send, recv_sem=recv, device_id=device, device_id_type=MESH
    )


def greet(devices):
    barrier = pltpu.get_barrier_semaphore()
    for device in devices:
        pl.semaphore_signal(barrier, inc=1, device_id=device, device_id_type=MESH)
    pl.semaphore_wait(barrier, len(devices))


def norm_rows(extra, experts):
    turned = jnp.transpose(extra.astype(F32))
    return turned[experts : experts + 4] + turned[experts + 4 : experts + 8] + turned[experts + 8 : experts + 12]


U, CF, XD, YX, DU, MIX = range(6)


def block_kernel(wides, narrows, rows, flag_ref, live_ref, tok_ref, cot_ref, shard_ref, upw_ref, downw_ref,
                 gt_ref, out_ref, dwq_ref, dwo_ref, dex_ref, dwc_ref, ownup_ref, owndown_ref, gotup_ref, gotdown_ref,
                 raw, wts, uc, qkv_buf, o_buf, lse_buf, lse_col, nrm, dn, in_buf, xd_out, xd_in, yx_in, w_buf, dw_buf,
                 wc_buf, up_buf, down_buf, g_buf, dk_ref, dv_ref,
                 gz_sem, gp_sem, gc_sem, gr_sem, hop_sem, hopr_sem, send_sem, recv_sem, rs_sem, rsr_sem, own_sem, io_sem):
    w_id, me = lax.axis_index("wide"), lax.axis_index("narrow")
    micros, length, width = tok_ref.shape
    blocks = length // ROWS
    part = length // narrows
    head = width // HEADS
    scale = 1.0 / math.sqrt(head)
    hidden_width = up_buf.shape[1]
    up_rows = width // wides
    down_rows = hidden_width // wides
    folds = hidden_width // width
    chunk_parts = ROWS // part
    half = narrows // 2
    q_id, parity = me // 2, lax.rem(me, 2)
    core = me + 1 - 2 * parity
    lane = lax.broadcasted_iota(jnp.int32, (1, LANES), 1)
    padded = shard_ref.shape[0]
    wq, wo = wts.at[:, pl.ds(0, 3 * width)], wts.at[:, pl.ds(3 * width, width)]

    def pick(ref, mb, at):
        value = ref[0, at, :].astype(F32)
        for j in range(1, micros):
            chosen = flag_ref[mb * micros + j : mb * micros + j + 1, 0:1] > 0
            value = jnp.where(chosen, ref[j, at, :].astype(F32), value)
        return value

    z_peers = [lax.rem(w_id + k, wides) for k in range(1, wides)]
    p_peers = [lax.rem(q_id + k, half) * 2 + parity for k in range(1, half)]
    greet([(z, me) for z in z_peers] + [(w_id, lax.rem(me + k, narrows)) for k in range(1, narrows)])

    def slot(zw, zn):
        return raw.at[pl.ds(pl.multiple_of((zw * narrows + zn) * padded, padded), padded)]

    own = pltpu.make_async_copy(shard_ref, slot(w_id, me), own_sem.at[0])
    own.start()
    gather_sends = []

    def spread(src, zw, zn, sem, device):
        copy = remote(src, slot(zw, zn), sem, gr_sem.at[zw, zn], device)
        copy.start()
        gather_sends.append(copy)

    def arrived(zw, zn):
        pltpu.make_async_copy(shard_ref, slot(zw, zn), gr_sem.at[zw, zn]).wait()

    for k, z in enumerate(z_peers):
        spread(shard_ref, w_id, me, gz_sem.at[k], (z, me))
    for k, p in enumerate(p_peers):
        spread(shard_ref, w_id, me, gp_sem.at[0, k], (w_id, p))
    spread(shard_ref, w_id, me, gc_sem.at[0, 0], (w_id, core))

    def up_part(z):
        return up_buf.at[pl.ds(pl.multiple_of(z * up_rows, up_rows), up_rows)]

    def down_part(z):
        return down_buf.at[pl.ds(pl.multiple_of(z * down_rows, down_rows), down_rows)]

    up_buf[pl.ds(pl.multiple_of(w_id * up_rows, up_rows), up_rows), :] = upw_ref[...].astype(BF)
    down_buf[pl.ds(pl.multiple_of(w_id * down_rows, down_rows), down_rows), :] = downw_ref[...].astype(BF)

    def hop_send(hop):
        @pl.when((w_id >= hop - 1) & (w_id < wides - 1))
        def _():
            for i, piece in enumerate((up_part, down_part)):
                source = piece(w_id - (hop - 1))
                remote(source, source, hop_sem.at[hop - 1, 0, i], hopr_sem.at[hop - 1, 0, i], (w_id + 1, me)).start()

        @pl.when((w_id + (hop - 1) <= wides - 1) & (w_id > 0))
        def _():
            for i, piece in enumerate((up_part, down_part)):
                source = piece(w_id + (hop - 1))
                remote(source, source, hop_sem.at[hop - 1, 1, i], hopr_sem.at[hop - 1, 1, i], (w_id - 1, me)).start()

    def hop_arrived(hop):
        @pl.when(w_id >= hop)
        def _():
            for i, piece in enumerate((up_part, down_part)):
                target = piece(w_id - hop)
                pltpu.make_async_copy(target, target, hopr_sem.at[hop - 1, 0, i]).wait()

        @pl.when(w_id + hop <= wides - 1)
        def _():
            for i, piece in enumerate((up_part, down_part)):
                target = piece(w_id + hop)
                pltpu.make_async_copy(target, target, hopr_sem.at[hop - 1, 1, i]).wait()

    def hop_sent(hop):
        @pl.when((w_id >= hop - 1) & (w_id < wides - 1))
        def _():
            for i, piece in enumerate((up_part, down_part)):
                source = piece(w_id - (hop - 1))
                pltpu.make_async_copy(source, source, hop_sem.at[hop - 1, 0, i]).wait()

        @pl.when((w_id + (hop - 1) <= wides - 1) & (w_id > 0))
        def _():
            for i, piece in enumerate((up_part, down_part)):
                source = piece(w_id + (hop - 1))
                pltpu.make_async_copy(source, source, hop_sem.at[hop - 1, 1, i]).wait()

    for j in range(1, wides):
        zw = lax.rem(w_id + wides - j, wides)
        arrived(zw, me)
        for k, p in enumerate(p_peers):
            spread(slot(zw, me), zw, me, gp_sem.at[j, k], (w_id, p))
        spread(slot(zw, me), zw, me, gc_sem.at[j, 0], (w_id, core))
    hop_send(1)

    def choose(i, _):
        at = pl.ds(i * ROWS, ROWS)
        for mb in range(micros):
            uc[mb, 1, at, :] = pick(cot_ref, mb, at).astype(BF)
        return 0

    lax.fori_loop(0, blocks, choose, 0)
    dwc_ref[...] = jnp.zeros_like(dwc_ref)
    for i in range(1, half):
        zn = lax.rem(q_id + half - i, half) * 2 + parity
        for j in range(wides):
            zw = lax.rem(w_id + wides - j, wides)
            arrived(zw, zn)
            spread(slot(zw, zn), zw, zn, gc_sem.at[j, i], (w_id, core))

    def send(stage, mb, source, target, peer):
        @pl.when(peer != me)
        def _():
            remote(source, target, send_sem.at[stage, mb, peer], recv_sem.at[stage, mb, me], (w_id, peer)).start()

        @pl.when(peer == me)
        def _():
            pltpu.make_async_copy(source, target, recv_sem.at[stage, mb, me]).start()

    def received(stage, mb, peer, target):
        pltpu.make_async_copy(target, target, recv_sem.at[stage, mb, peer]).wait()

    def sent(stage, mb, source):
        def one(k, _):
            peer = lax.rem(me + k, narrows)
            pltpu.make_async_copy(source, source, send_sem.at[stage, mb, peer]).wait()
            return 0

        lax.fori_loop(1, narrows, one, 0)

    def part_rows(n):
        return pl.ds(pl.multiple_of(n * part, part), part)

    def to_all(body):
        def one(k, _):
            body(lax.rem(me + k, narrows))
            return 0

        lax.fori_loop(0, narrows, one, 0)

    def send_rows(which, mb):
        to_all(lambda peer: send(
            which, mb, uc.at[mb, which, part_rows(peer)], in_buf.at[mb, me, which], peer))

    for mb in range(micros):
        send_rows(CF, mb)
    for i in range(half):
        for j in range(wides):
            arrived(j, 2 * i + 1 - parity)
    own.wait()

    if rows == padded:
        pltpu.sync_copy(raw, wts)
    else:
        fold, group = padded // rows, raw.shape[1]
        for f in range(fold):
            start, stop = f * group, min((f + 1) * group, wts.shape[1])
            if start >= stop:
                break
            for i in range(width // LANES):
                here = lax.broadcasted_iota(jnp.int32, (LANES, raw.shape[0]), 0) + i * LANES
                there = lax.broadcasted_iota(jnp.int32, (LANES, raw.shape[0]), 1)
                match = (here // rows) * padded + f * rows + lax.rem(here, rows) == there
                take = jnp.where(match, 1.0, 0.0).astype(BF)
                wts[i * LANES : (i + 1) * LANES, start:stop] = dot(take, raw[:, : stop - start], 1, 0).astype(BF)
    extra = wts[:, 4 * width :]
    nrm[0:4, :] = norm_rows(extra, narrows)
    wc_buf[...] = jnp.where(lane < narrows, extra.astype(F32), 0).astype(BF)

    def forward(mb, hooks):
        def project(i, _):
            at = pl.ds(i * ROWS, ROWS)
            xhat, _ = norm_stats(pick(tok_ref, mb, at))
            al = (xhat * nrm[0:1, :] + nrm[1:2, :]).astype(BF)
            qkv_buf[mb, at, :] = dot(al, wq[...], 1, 0).astype(BF)
            return 0

        lax.fori_loop(0, blocks, project, 0)
        lse_col[...] = jnp.zeros_like(lse_col)
        keep = lax.broadcasted_iota(jnp.int32, (ROWS, ROWS), 1) <= lax.broadcasted_iota(jnp.int32, (ROWS, ROWS), 0)
        for i in range(blocks):
            keys = (i + 1) * ROWS
            at = pl.ds(i * ROWS, ROWS)

            def pair(hp, _, i=i, keys=keys, at=at):
                lanes = pl.ds(pl.multiple_of(hp * LANES, LANES), LANES)
                klanes = pl.ds(pl.multiple_of(hp * LANES + width, LANES), LANES)
                vlanes = pl.ds(pl.multiple_of(hp * LANES + 2 * width, LANES), LANES)
                q = qkv_buf[mb, at, lanes]
                k = qkv_buf[mb, pl.ds(0, keys), klanes]
                v = qkv_buf[mb, pl.ds(0, keys), vlanes]
                acc = None
                for h in range(2):
                    mine = lane // head == h
                    qm = jnp.where(mine, q * scale, 0).astype(BF)
                    vm = jnp.where(mine, v, 0).astype(BF)
                    s = dot(qm, k, 1, 1)
                    diag = jnp.where(keep, s[:, i * ROWS :], NEG_LARGE)
                    s = diag if i == 0 else jnp.concatenate([s[:, : i * ROWS], diag], axis=1)
                    m = jnp.max(s, axis=1, keepdims=True)
                    p = jnp.exp(s - m)
                    total = jnp.sum(p, axis=1, keepdims=True)
                    one = dot((p * (1.0 / total)).astype(BF), vm, 1, 0)
                    acc = one if acc is None else acc + one
                    lse_col[at, :] = jnp.where(lane == hp * 2 + h, m + jnp.log(total), lse_col[at, :])
                o_buf[mb, at, lanes] = acc.astype(BF)
                return 0

            lax.fori_loop(0, HEADS // 2, pair, 0)
            for hook in hooks.get(i, ()):
                hook()
        lse_buf[mb] = jnp.transpose(lse_col[...])[:HEADS, :]

        def finish(i, _):
            at = pl.ds(i * ROWS, ROWS)
            hidden = pick(tok_ref, mb, at) + dot(o_buf[mb, at, :], wo[...], 1, 0)
            xhat, _ = norm_stats(hidden)
            uc[mb, 0, at, :] = (xhat * nrm[2:3, :] + nrm[3:4, :]).astype(BF)
            return 0

        lax.fori_loop(0, blocks, finish, 0)

    def mix(mb):
        def logits(n, _):
            received(U, mb, n, in_buf.at[mb, n, 0])
            received(CF, mb, n, in_buf.at[mb, n, 1])
            w_buf[mb, n] = dot(in_buf[mb, n, 0], wc_buf[...], 1, 0).astype(BF).astype(F32)
            return 0

        lax.fori_loop(0, narrows, logits, 0)

        def rows_of(c, _):
            at = pl.ds(c * 16, 16)
            logit = [
                jnp.where(live_ref[mb, pl.ds(n, 1), :] > 0, w_buf[mb, n, at, :], NEG_LARGE) for n in range(narrows)
            ]
            top = functools.reduce(jnp.maximum, logit)
            exps = [jnp.exp(logit[n] - top) * live_ref[mb, pl.ds(n, 1), :] for n in range(narrows)]
            inverse = 1.0 / functools.reduce(jnp.add, exps)
            weights = [e * inverse for e in exps]
            for n in range(narrows):
                w_buf[mb, n, at, :] = weights[n]
            for which in range(2):
                values = [in_buf[mb, n, which, at, :].astype(F32) for n in range(narrows)]
                for e in range(narrows):
                    acc = functools.reduce(
                        jnp.add, [weights[n][:, e : e + 1] * values[n] for n in range(narrows)])
                    xd_out[mb, e, which, at, :] = acc.astype(BF)
            return 0

        lax.fori_loop(0, part // 16, rows_of, 0)
        to_all(lambda peer: send(XD, mb, xd_out.at[mb, peer], xd_in.at[mb, me], peer))

    def expert(mb):
        sent(U, mb, uc.at[mb, 0, pl.ds(0, part)])
        sent(CF, mb, uc.at[mb, 0, pl.ds(0, part)])

        def chunk(c, _):
            at = pl.ds(c * chunk_parts, chunk_parts)
            for k in range(chunk_parts):
                received(XD, mb, c * chunk_parts + k, xd_in.at[mb, c * chunk_parts + k])
            x = xd_in[mb, at, 0].reshape(ROWS, width)
            dy = xd_in[mb, at, 1].reshape(ROWS, width)

            def tile(j, carry):
                y, dx = carry
                cols = pl.ds(pl.multiple_of(j * width, width), width)
                z = dot(x, up_buf[:, cols], 1, 0)
                zz = z * z
                t = jnp.tanh(GELU_A * (z + GELU_B * z * zz))
                ga = (0.5 * z * (1.0 + t)).astype(BF)
                slope = 0.5 * (1.0 + t) + (0.5 * GELU_A) * z * (1.0 - t * t) * (1.0 + (3.0 * GELU_B) * zz)
                y = y + dot(ga, down_buf[cols, :], 1, 0)
                dz = (dot(dy, down_buf[cols, :], 1, 1) * slope).astype(BF)
                dx = dx + dot(dz, up_buf[:, cols], 1, 1)
                g_buf[folds + j] += dot(ga, dy, 0, 0)
                g_buf[j] += dot(x, dz, 0, 0)
                return y, dx

            zero = jnp.zeros((ROWS, width), F32)
            y, dx = lax.fori_loop(0, folds, tile, (zero, zero))
            xd_in[mb, at, 0] = y.astype(BF).reshape(chunk_parts, part, width)
            xd_in[mb, at, 1] = dx.astype(BF).reshape(chunk_parts, part, width)
            for k in range(chunk_parts):
                peer = c * chunk_parts + k
                send(YX, mb, xd_in.at[mb, peer], yx_in.at[mb, me], peer)
            return 0

        lax.fori_loop(0, blocks, chunk, 0)

    du_at = folds

    def du_rows(n):
        per = width // part
        return du_at + n // per, pl.ds(pl.multiple_of(lax.rem(n, per) * part, part), part)

    def combine(mb):
        sent(XD, mb, xd_out.at[mb, 0])

        def wait(e, _):
            received(YX, mb, e, yx_in.at[mb, e])
            return 0

        lax.fori_loop(0, narrows, wait, 0)

        def member(n, _):
            tile, rows_n = du_rows(n)

            def rows_of(c, _):
                at = pl.ds(c * 16, 16)
                u = in_buf[mb, n, 0, at, :].astype(F32)
                cf = in_buf[mb, n, 1, at, :].astype(F32)
                weights = w_buf[mb, n, at, :]
                mixed = du = None
                dw = jnp.zeros((16, LANES), F32)
                for e in range(narrows):
                    y = yx_in[mb, e, 0, at, :].astype(F32)
                    dx = yx_in[mb, e, 1, at, :].astype(F32)
                    weight = weights[:, e : e + 1]
                    mixed = weight * y if e == 0 else mixed + weight * y
                    du = weight * dx if e == 0 else du + weight * dx
                    dw = jnp.where(lane == e, jnp.sum(dx * u + cf * y, axis=1, keepdims=True), dw)
                xd_out[mb, n, 0, at, :] = mixed.astype(BF)
                g_buf[tile, pl.ds(pl.multiple_of(lax.rem(n, width // part) * part + c * 16, 16), 16), :] = du
                dw_buf[n, at, :] = dw
                return 0

            lax.fori_loop(0, part // 16, rows_of, 0)
            return 0

        lax.fori_loop(0, narrows, member, 0)

        def group(n, acc):
            return acc + w_buf[mb, n] * dw_buf[n]

        inner = lax.fori_loop(0, narrows, group, jnp.zeros((part, LANES), F32))

        def finish(n, _):
            tile, rows_n = du_rows(n)
            dc = (w_buf[mb, n] * (dw_buf[n] - inner)).astype(BF)
            du = g_buf[tile, rows_n, :] + dot(dc, wc_buf[...], 1, 1)
            xd_out[mb, n, 1] = du.astype(BF)
            dwc_ref[...] += dot(in_buf[mb, n, 0], dc, 0, 0)
            send(DU, mb, xd_out.at[mb, n, 1], uc.at[mb, 0, part_rows(me)], n)
            return 0

        lax.fori_loop(0, narrows, finish, 0)

    def send_mixed(mb):
        to_all(lambda peer: send(MIX, mb, xd_out.at[mb, peer, 0], uc.at[mb, 1, part_rows(me)], peer))

    tiles = length // width
    per_tile = width // ROWS

    def tile_rows(first, i):
        return first + i // per_tile, pl.ds(pl.multiple_of(lax.rem(i, per_tile) * ROWS, ROWS), ROWS)

    def out_copies(mb):
        copies = [pltpu.make_async_copy(o_buf.at[mb], out_ref.at[mb], io_sem.at[0])]
        for i in range(tiles):
            copies.append(pltpu.make_async_copy(
                g_buf.at[i], gt_ref.at[mb, pl.ds(i * width, width)], io_sem.at[1 + i]))
        return copies

    def backward(mb):
        to_all(lambda peer: received(DU, mb, peer, uc.at[mb, 0, part_rows(peer)]))

        def first(i, _):
            at = pl.ds(i * ROWS, ROWS)
            low = o_buf[mb, at, :]
            hidden = pick(tok_ref, mb, at) + dot(low, wo[...], 1, 0)
            tile, rows_i = tile_rows(tiles, i)
            g_buf[tile, rows_i, :] = hidden
            xhat, rstd = norm_stats(hidden)
            du = uc[mb, 0, at, :].astype(F32)
            dn[2:3, :] += jnp.sum(du * xhat, axis=0, keepdims=True)
            dn[3:4, :] += jnp.sum(du, axis=0, keepdims=True)
            dh = pick(cot_ref, mb, at) + norm_back(du, nrm[2:3, :], xhat, rstd)
            tile, rows_i = tile_rows(0, i)
            g_buf[tile, rows_i, :] = dh
            db = dh.astype(BF)
            dwo_ref[...] += dot(low, db, 0, 0)
            o_buf[mb, at, :] = dot(db, wo[...], 1, 1).astype(BF)
            return 0

        lax.fori_loop(0, blocks, first, 0)
        keep = lax.broadcasted_iota(jnp.int32, (ROWS, ROWS), 0) <= lax.broadcasted_iota(jnp.int32, (ROWS, ROWS), 1)

        def pair(hp, _):
            lanes = pl.ds(pl.multiple_of(hp * LANES, LANES), LANES)
            klanes = pl.ds(pl.multiple_of(hp * LANES + width, LANES), LANES)
            vlanes = pl.ds(pl.multiple_of(hp * LANES + 2 * width, LANES), LANES)
            for i in range(blocks):
                keys = (i + 1) * ROWS
                at = pl.ds(i * ROWS, ROWS)
                q = qkv_buf[mb, at, lanes]
                k = qkv_buf[mb, pl.ds(0, keys), klanes]
                v = qkv_buf[mb, pl.ds(0, keys), vlanes]
                do = o_buf[mb, at, lanes]
                dq = dk = dv = None
                for h in range(2):
                    mine = lane // head == h
                    qm = jnp.where(mine, q * scale, 0).astype(BF)
                    dom = jnp.where(mine, do, 0).astype(BF)
                    km = jnp.where(mine, k * scale, 0).astype(BF)
                    s = dot(k, qm, 1, 1) - lse_buf[mb, pl.ds(hp * 2 + h, 1), at]
                    diag = jnp.where(keep, s[i * ROWS :], NEG_LARGE)
                    p = jnp.exp(diag if i == 0 else jnp.concatenate([s[: i * ROWS], diag], axis=0))
                    pdp = p * dot(v, dom, 1, 1)
                    inner = jnp.sum(pdp, axis=0, keepdims=True)
                    ds = (pdp - p * inner).astype(BF)
                    a = dot(p.astype(BF), dom, 1, 0)
                    b = dot(ds, qm, 1, 0)
                    c = dot(ds, km, 0, 0)
                    dv, dk, dq = (a, b, c) if h == 0 else (dv + a, dk + b, dq + c)
                qkv_buf[mb, at, lanes] = dq.astype(BF)
                if i:
                    dk_ref[: i * ROWS, :] += dk[: i * ROWS]
                    dv_ref[: i * ROWS, :] += dv[: i * ROWS]
                dk_ref[i * ROWS : keys, :] = dk[i * ROWS :]
                dv_ref[i * ROWS : keys, :] = dv[i * ROWS :]
            qkv_buf[mb, :, klanes] = dk_ref[...].astype(BF)
            qkv_buf[mb, :, vlanes] = dv_ref[...].astype(BF)
            return 0

        lax.fori_loop(0, HEADS // 2, pair, 0)
        to_all(lambda peer: received(MIX, mb, peer, uc.at[mb, 1, part_rows(peer)]))

        def last(i, _):
            at = pl.ds(i * ROWS, ROWS)
            xhat, rstd = norm_stats(pick(tok_ref, mb, at))
            al = (xhat * nrm[0:1, :] + nrm[1:2, :]).astype(BF)
            dqkv = qkv_buf[mb, at, :]
            dwq_ref[...] += dot(al, dqkv, 0, 0)
            da = dot(dqkv, wq[...], 1, 1)
            dn[0:1, :] += jnp.sum(da * xhat, axis=0, keepdims=True)
            dn[1:2, :] += jnp.sum(da, axis=0, keepdims=True)
            tile, rows_i = tile_rows(0, i)
            g_buf[tile, rows_i, :] = g_buf[tile, rows_i, :] + norm_back(da, nrm[0:1, :], xhat, rstd)
            tile, rows_i = tile_rows(tiles, i)
            o_buf[mb, at, :] = (g_buf[tile, rows_i, :] + uc[mb, 1, at, :].astype(F32)).astype(BF)
            return 0

        lax.fori_loop(0, blocks, last, 0)
        for copy in out_copies(mb):
            copy.start()

    def relay(hop):
        def run():
            hop_arrived(hop)
            if hop < wides - 1:
                hop_send(hop + 1)

        return run

    relays = [relay(hop) for hop in range(1, wides - 1)]
    for mb in range(micros):
        hooks = {}
        if mb == 0 and relays:
            hooks[min(2, blocks - 1)] = [relays.pop(0)]
        elif relays and mb == micros - 1:
            hooks[min(1, blocks - 1)] = relays
        if mb > 0:
            hooks[min(2, blocks - 1)] = [functools.partial(mix, mb - 1)]
        forward(mb, hooks)
        send_rows(U, mb)
    mix(micros - 1)
    hop_arrived(wides - 1)
    g_buf[...] = jnp.zeros_like(g_buf)
    for mb in range(micros):
        expert(mb)
    for hop in range(1, wides):
        hop_sent(hop)

    for j in range(folds):
        up_buf[:, j * width : (j + 1) * width] = g_buf[j].astype(BF)
        down_buf[j * width : (j + 1) * width, :] = g_buf[folds + j].astype(BF)
    for k, z in enumerate(z_peers):
        remote(up_part(z), gotup_ref.at[k], rs_sem.at[k, 0], rsr_sem.at[k, 0], (z, me)).start()
        remote(down_part(z), gotdown_ref.at[k], rs_sem.at[k, 1], rsr_sem.at[k, 1], (z, me)).start()
    owned = [
        pltpu.make_async_copy(
            g_buf.at[j, pl.ds(pl.multiple_of(w_id * up_rows, up_rows), up_rows)],
            ownup_ref.at[:, pl.ds(j * width, width)], own_sem.at[1 + j])
        for j in range(folds)
    ]
    piece = min(down_rows, width)
    first_row = w_id * down_rows
    for j in range(down_rows // piece):
        row = first_row + j * piece
        owned.append(pltpu.make_async_copy(
            g_buf.at[folds + row // width, pl.ds(pl.multiple_of(lax.rem(row, width), piece), piece)],
            owndown_ref.at[pl.ds(j * piece, piece)], own_sem.at[1 + folds + j]))
    for copy in owned:
        copy.start()
    for copy in owned:
        copy.wait()

    dwq_ref[...] = jnp.zeros_like(dwq_ref)
    dwo_ref[...] = jnp.zeros_like(dwo_ref)
    dn[...] = jnp.zeros_like(dn)
    for mb in range(micros):
        combine(mb)
    for mb in range(micros):
        send_mixed(mb)
    for mb in range(micros):
        if mb > 0:
            for copy in out_copies(mb - 1):
                copy.wait()
        backward(mb)
    dex_ref[...] = jnp.transpose(jnp.concatenate([dn[...], jnp.zeros((LANES - 8, width), F32)], axis=0))

    for copy in out_copies(micros - 1):
        copy.wait()
    for copy in gather_sends:
        copy.wait_send()
    for k in range(wides - 1):
        for i, (mine, theirs) in enumerate(((up_part(0), gotup_ref.at[k]), (down_part(0), gotdown_ref.at[k]))):
            pltpu.make_async_copy(mine, mine, rs_sem.at[k, i]).wait()
            pltpu.make_async_copy(theirs, theirs, rsr_sem.at[k, i]).wait()
    for mb in range(micros):
        sent(YX, mb, xd_in.at[mb, 0])
        sent(DU, mb, xd_out.at[mb, 0, 0])
        sent(MIX, mb, xd_out.at[mb, 0, 0])


def run_block(flags, live, tokens, cot, shard, up, down, wides, narrows, rows):
    micros, length, width = tokens.shape
    part = length // narrows
    hidden_width = up.shape[1]
    folds = hidden_width // width
    devices = wides * narrows
    hbm = pl.BlockSpec(memory_space=pl.ANY)
    vmem = pl.BlockSpec(memory_space=pltpu.VMEM)
    pairs = pltpu.VMEM((micros, narrows, 2, part, width), BF)
    sems = pltpu.SemaphoreType.DMA
    half = narrows // 2
    cols = 4 * width + LANES
    return pl.pallas_call(
        functools.partial(block_kernel, wides, narrows, rows),
        out_shape=[
            jax.ShapeDtypeStruct((micros, length, width), F32),
            jax.ShapeDtypeStruct((micros, length, width), BF),
            jax.ShapeDtypeStruct((width, 3 * width), F32),
            jax.ShapeDtypeStruct((width, width), F32),
            jax.ShapeDtypeStruct((width, LANES), F32),
            jax.ShapeDtypeStruct((width, LANES), F32),
            jax.ShapeDtypeStruct(up.shape, F32),
            jax.ShapeDtypeStruct(down.shape, F32),
            jax.ShapeDtypeStruct((wides - 1,) + up.shape, BF),
            jax.ShapeDtypeStruct((wides - 1,) + down.shape, BF),
        ],
        in_specs=[vmem] * 7,
        out_specs=[hbm, hbm, vmem, vmem, vmem, vmem, hbm, hbm, hbm, hbm],
        scratch_shapes=[
            pltpu.VMEM((devices * shard.shape[0], shard.shape[1]), BF),
            pltpu.VMEM((width, cols), BF),
            pltpu.VMEM((micros, 2, length, width), BF),
            pltpu.VMEM((micros, length, 3 * width), BF),
            pltpu.VMEM((micros, length, width), BF),
            pltpu.VMEM((micros, HEADS, length), F32),
            pltpu.VMEM((length, LANES), F32),
            pltpu.VMEM((8, width), F32),
            pltpu.VMEM((8, width), F32),
            pairs,
            pairs,
            pairs,
            pairs,
            pltpu.VMEM((micros, narrows, part, LANES), F32),
            pltpu.VMEM((narrows, part, LANES), F32),
            pltpu.VMEM((width, LANES), BF),
            pltpu.VMEM((width, hidden_width), BF),
            pltpu.VMEM((hidden_width, width), BF),
            pltpu.VMEM((2 * folds, width, width), F32),
            pltpu.VMEM((length, LANES), F32),
            pltpu.VMEM((length, LANES), F32),
            sems((wides - 1,)),
            sems((wides, half - 1)),
            sems((wides, half)),
            sems((wides, narrows)),
            sems((wides - 1, 2, 2)),
            sems((wides - 1, 2, 2)),
            sems((6, micros, narrows)),
            sems((6, micros, narrows)),
            sems((wides - 1, 2)),
            sems((wides - 1, 2)),
            sems((1 + 2 * folds,)),
            sems((1 + length // width,)),
        ],
        compiler_params=pltpu.CompilerParams(
            collective_id=0, has_side_effects=True, vmem_limit_bytes=64 << 20),
        name="block",
    )(flags, live, tokens, cot, shard, up, down)


def reduce_kernel(wides, narrows, wq_ref, wo_ref, ex_ref, dwc_ref, out_ref,
                  s1, r1, s2, r2, s3, r3, total, c_sem, p_sem, z_sem, cr_sem, pr_sem, zr_sem):
    w, n = lax.axis_index("wide"), lax.axis_index("narrow")
    half = narrows // 2
    q, parity = n // 2, lax.rem(n, 2)
    core = n + 1 - 2 * parity
    z_peers = [lax.rem(w + k, wides) for k in range(1, wides)]
    p_peers = [lax.rem(q + k, half) for k in range(1, half)]
    greet([(w, core)] + [(w, p * 2 + parity) for p in p_peers] + [(z, n) for z in z_peers])
    a, b = wq_ref.shape[2], wq_ref.shape[2] + wo_ref.shape[2]

    def parts(index):
        return wq_ref[index], wo_ref[index], ex_ref[index] + dwc_ref[index]

    sends = []
    for k in range(half):
        there = lax.rem(q + 1 + k, half)

        def fill(z, _, there=there):
            one, two, three = parts(z * narrows + 2 * there + 1 - parity)
            s1[there, z, :, :a] = one.astype(BF)
            s1[there, z, :, a:b] = two.astype(BF)
            s1[there, z, :, b:] = three.astype(BF)
            return 0

        lax.fori_loop(0, wides, fill, 0)
        copy = remote(s1.at[there], r1.at[there], c_sem.at[k], cr_sem.at[there], (w, core))
        copy.start()
        sends.append(copy)
    for k in range(half):
        there = lax.rem(q + 1 + k, half)
        remote(s1.at[there], r1.at[there], c_sem.at[k], cr_sem.at[there], (w, core)).wait_recv()
        last = k == half - 1

        def add(z, _, there=there, last=last):
            one, two, three = parts(z * narrows + 2 * there + parity)
            got = r1[there, z].astype(F32)
            one, two, three = one + got[:, :a], two + got[:, a:b], three + got[:, b:]
            if last:
                total[z, :, :a], total[z, :, a:b], total[z, :, b:] = one, two, three
            else:
                s2[there, z, :, :a] = one.astype(BF)
                s2[there, z, :, a:b] = two.astype(BF)
                s2[there, z, :, b:] = three.astype(BF)
            return 0

        lax.fori_loop(0, wides, add, 0)
        if not last:
            copy = remote(s2.at[there], r2.at[q], p_sem.at[k], pr_sem.at[q], (w, there * 2 + parity))
            copy.start()
            sends.append(copy)
    for k in range(1, half):
        there = lax.rem(q + k, half)
        remote(s2.at[there], r2.at[there], p_sem.at[0], pr_sem.at[there], (w, n)).wait_recv()
    for k in range(wides):
        z = lax.rem(w + 1 + k, wides)
        acc = total[z]
        for i in range(1, half):
            acc = acc + r2[lax.rem(q + i, half), z].astype(F32)
        if k < wides - 1:
            s3[z] = acc.astype(BF)
            copy = remote(s3.at[z], r3.at[w], z_sem.at[k], zr_sem.at[w], (z, n))
            copy.start()
            sends.append(copy)
        else:
            out_ref[...] = acc
    for k in range(1, wides):
        z = lax.rem(w + k, wides)
        remote(s3.at[z], r3.at[z], z_sem.at[0], zr_sem.at[z], (w, n)).wait_recv()
        out_ref[...] += r3[z].astype(F32)
    for copy in sends:
        copy.wait_send()


def reduce_shared(dwq, dwo, dex, dwc, wides, narrows):
    half = narrows // 2
    rows = dwq.shape[1]
    cols = dwq.shape[2] + dwo.shape[2] + dex.shape[2]
    vmem = pl.BlockSpec(memory_space=pltpu.VMEM)
    block = (half, wides, rows, cols)
    sems = pltpu.SemaphoreType.DMA
    return pl.pallas_call(
        functools.partial(reduce_kernel, wides, narrows),
        out_shape=jax.ShapeDtypeStruct((rows, cols), F32),
        in_specs=[vmem] * 4,
        out_specs=vmem,
        scratch_shapes=[pltpu.VMEM(block, BF)] * 4
        + [pltpu.VMEM(block[1:], BF)] * 2
        + [pltpu.VMEM(block[1:], F32)]
        + [sems((half,)), sems((half,)), sems((wides,))] * 2,
        compiler_params=pltpu.CompilerParams(
            collective_id=2, has_side_effects=True, vmem_limit_bytes=60 << 20),
        name="reduce_shared",
    )(dwq, dwo, dex, dwc)


def total_kernel(wides, narrows, part_ref, out_ref, got_n, mid, got_w, send_n, recv_n, send_w, recv_w):
    w, n = lax.axis_index("wide"), lax.axis_index("narrow")
    n_peers = [lax.rem(n + k, narrows) for k in range(1, narrows)]
    z_peers = [lax.rem(w + k, wides) for k in range(1, wides)]
    greet([(w, p) for p in n_peers] + [(z, n) for z in z_peers])
    sends = []
    for k, p in enumerate(n_peers):
        copy = remote(part_ref, got_n.at[n], send_n.at[k], recv_n.at[n], (w, p))
        copy.start()
        sends.append(copy)
    got_n[n] = part_ref[...]
    for p in n_peers:
        remote(part_ref, got_n.at[p], send_n.at[0], recv_n.at[p], (w, n)).wait_recv()
    acc = got_n[0]
    for k in range(1, narrows):
        acc = acc + got_n[k]
    mid[...] = acc
    got_w[w] = acc
    for k, z in enumerate(z_peers):
        copy = remote(mid, got_w.at[w], send_w.at[k], recv_w.at[w], (z, n))
        copy.start()
        sends.append(copy)
    for z in z_peers:
        remote(mid, got_w.at[z], send_w.at[0], recv_w.at[z], (w, n)).wait_recv()
    acc = got_w[0]
    for k in range(1, wides):
        acc = acc + got_w[k]
    out_ref[...] = acc
    for copy in sends:
        copy.wait_send()


def sum_everywhere(part, wides, narrows):
    vmem = pl.BlockSpec(memory_space=pltpu.VMEM)
    sems = pltpu.SemaphoreType.DMA
    return pl.pallas_call(
        functools.partial(total_kernel, wides, narrows),
        out_shape=jax.ShapeDtypeStruct(part.shape, F32),
        in_specs=[vmem],
        out_specs=vmem,
        scratch_shapes=[
            pltpu.VMEM((narrows,) + part.shape, F32),
            pltpu.VMEM(part.shape, F32),
            pltpu.VMEM((wides,) + part.shape, F32),
            sems((narrows - 1,)),
            sems((narrows,)),
            sems((wides - 1,)),
            sems((wides,)),
        ],
        compiler_params=pltpu.CompilerParams(collective_id=3, has_side_effects=True),
        name="sum_everywhere",
    )(part)


def adam_update(weight, first_state, second_state, gradient, factor, rate, decay):
    clipped = gradient * factor
    first_new = BETA_ONE * first_state + (1.0 - BETA_ONE) * clipped
    second_new = BETA_TWO * second_state + (1.0 - BETA_TWO) * clipped * clipped
    first_hat = first_new / (1.0 - BETA_ONE**STEP)
    second_hat = second_new / (1.0 - BETA_TWO**STEP)
    weight_new = weight - rate * (first_hat / (jnp.sqrt(second_hat) + ADAM_EPS) + decay * weight)
    return (weight_new, first_new, second_new, weight_new.astype(BF))


def per_device(
    tokens, cotangent, seq_counts, micro_assign,
    norm_params, norm_first, norm_second,
    project_weight, project_first, project_second,
    output_weight, output_first, output_second,
    control_weight, control_first, control_second,
    up_weight, up_first, up_second,
    down_weight, down_first, down_second,
):
    wides, narrows = lax.axis_size("wide"), lax.axis_size("narrow")
    wide_index, narrow_index = lax.axis_index("wide"), lax.axis_index("narrow")
    devices = wides * narrows
    micro_count, length, width = tokens.shape
    experts = control_weight.shape[1]
    rows = project_weight.shape[0]
    padded = max(rows, 16)

    first_device = wide_index * narrows
    row_counts = lax.dynamic_slice_in_dim(seq_counts, first_device, narrows)
    row_assign = lax.dynamic_slice_in_dim(micro_assign, first_device, narrows, 0)
    slot_numbers = jnp.arange(micro_count, dtype=jnp.int32)
    micros = jnp.arange(micro_count, dtype=jnp.int32)
    member_slots = jnp.sum(
        slot_numbers[None, None, :] * (row_assign[None] == micros[:, None, None]).astype(jnp.int32), axis=2
    )
    live = (member_slots < row_counts[None]).astype(F32)
    live = jnp.broadcast_to(live[:, :, None], (micro_count, narrows, LANES))
    slots = lax.dynamic_index_in_dim(member_slots, narrow_index, 1, keepdims=False)
    flags = (slots[:, None] == slot_numbers[None, :]).astype(F32).reshape(-1, 1)
    flags = jnp.pad(jnp.broadcast_to(flags, (flags.shape[0], LANES)), ((0, -flags.shape[0] % 8), (0, 0)))

    norm_turned = norm_params.T
    high = lax.reduce_precision(norm_turned, 8, 7)
    middle = lax.reduce_precision(norm_turned - high, 8, 7)
    lower = norm_turned - high - middle
    extra = jnp.concatenate([control_weight, high, middle, lower], axis=1).astype(BF)
    extra = jnp.pad(extra, ((0, 0), (0, LANES - extra.shape[1])))
    shard = jnp.concatenate([project_weight.astype(BF), output_weight.astype(BF), extra], axis=1)
    if rows < padded:
        fold = padded // rows
        group = -(-(shard.shape[1] // LANES) // fold) * LANES
        shard = jnp.pad(shard, ((0, 0), (0, fold * group - shard.shape[1])))
        shard = shard.reshape(rows, fold, group).transpose(1, 0, 2).reshape(padded, group)

    grad_rows, out_low, dwq, dwo, dex, dwc, own_up, own_down, got_up, got_down = run_block(
        flags, live, tokens, cotangent, shard, up_weight[0], down_weight[0], wides, narrows, rows)
    place = [micro_assign[first_device + narrow_index, j] for j in range(micro_count)]
    grad_tokens = jnp.stack([lax.dynamic_index_in_dim(grad_rows, place[j], 0, False) for j in range(micro_count)])
    out_rows = jnp.stack([lax.dynamic_index_in_dim(out_low, place[j], 0, False) for j in range(micro_count)])
    up_grad = own_up + jnp.sum(got_up.astype(F32), axis=0)
    down_grad = own_down + jnp.sum(got_down.astype(F32), axis=0)
    dex = jnp.pad(dex[:, :4], ((0, 0), (experts, LANES - 4 - experts)))

    def by_owner(grad):
        return jnp.pad(grad.reshape(devices, rows, -1), ((0, 0), (0, padded - rows), (0, 0)))

    shared = reduce_shared(by_owner(dwq), by_owner(dwo), by_owner(dex), by_owner(dwc), wides, narrows)[:rows]
    project_grad = shared[:, : 3 * width]
    output_grad = shared[:, 3 * width : 4 * width]
    control_grad = shared[:, 4 * width : 4 * width + experts]
    norm_grad = shared[:, 4 * width + experts : 4 * width + experts + 4].T
    squares = jnp.sum(shared * shared) + jnp.sum(up_grad * up_grad) + jnp.sum(down_grad * down_grad)
    total = sum_everywhere(jnp.full((8, LANES), squares, F32), wides, narrows)
    grad_norm = jnp.sqrt(total[0, 0])
    factor = CLIP_NORM / jnp.maximum(grad_norm, CLIP_NORM)
    norm_out = adam_update(norm_params, norm_first, norm_second, norm_grad, factor, 0.3, 0.0)
    project_out = adam_update(
        project_weight, project_first, project_second, project_grad, factor, 0.03, DECAY_RATE)
    output_out = adam_update(output_weight, output_first, output_second, output_grad, factor, 0.2, DECAY_RATE)
    control_out = adam_update(
        control_weight, control_first, control_second, control_grad, factor, 0.015, DECAY_RATE)
    up_out = adam_update(up_weight, up_first, up_second, up_grad[None], factor, 0.1, DECAY_RATE)
    down_out = adam_update(down_weight, down_first, down_second, down_grad[None], factor, 0.1, DECAY_RATE)
    return (out_rows, grad_tokens, grad_norm) + norm_out + project_out + output_out + control_out + up_out + down_out


def solution(mesh):
    both = ("wide", "narrow")
    rows3, cols, rows2, expert = P(both, None, None), P(None, both), P(both, None), P("narrow", "wide", None)
    return jax.shard_map(
        per_device,
        mesh=mesh,
        in_specs=(rows3, rows3, P(), P()) + (cols,) * 3 + (rows2,) * 9 + (expert,) * 6,
        out_specs=(rows3, rows3, P()) + (cols,) * 4 + (rows2,) * 12 + (expert,) * 8,
        check_vma=False,
    )
```

```python
import functools
import math

import jax
import jax.numpy as jnp
from jax import lax
from jax.experimental import pallas as pl
from jax.experimental.pallas import tpu as pltpu
from jax.sharding import PartitionSpec as P

HEADS = 8
STEP = 5
NEG_LARGE = -1e30
NORM_EPS = 1e-05
CLIP_NORM = 0.05
BETA_ONE = 0.5
BETA_TWO = 0.5
ADAM_EPS = 1e-08
DECAY_RATE = 0.1

BF = jnp.bfloat16
F32 = jnp.float32
MESH = pl.DeviceIdType.MESH
LANES = 128
ROWS = 256
GELU_A = math.sqrt(2.0 / math.pi)
GELU_B = 0.044715


def dot(a, b, ca, cb):
    return lax.dot_general(a, b, (((ca,), (cb,)), ((), ())), preferred_element_type=F32)


def norm_stats(v):
    centred = v - jnp.mean(v, axis=-1, keepdims=True)
    rstd = lax.rsqrt(jnp.mean(centred * centred, axis=-1, keepdims=True) + NORM_EPS)
    return centred * rstd, rstd


def norm_back(grad, gain, xhat, rstd):
    t = grad * gain
    return rstd * (t - jnp.mean(t, axis=-1, keepdims=True) - xhat * jnp.mean(t * xhat, axis=-1, keepdims=True))


def remote(src, dst, send, recv, device):
    return pltpu.make_async_remote_copy(
        src_ref=src, dst_ref=dst, send_sem=send, recv_sem=recv, device_id=device, device_id_type=MESH
    )


def greet(devices):
    barrier = pltpu.get_barrier_semaphore()
    for device in devices:
        pl.semaphore_signal(barrier, inc=1, device_id=device, device_id_type=MESH)
    pl.semaphore_wait(barrier, len(devices))


def norm_rows(extra, experts):
    turned = jnp.transpose(extra.astype(F32))
    return turned[experts : experts + 4] + turned[experts + 4 : experts + 8] + turned[experts + 8 : experts + 12]


U, CF, XD, YX, DU, MIX = range(6)


def fold_rows(value):
    acc = value[:8]
    for i in range(8, value.shape[0], 8):
        acc = acc + value[i : i + 8]
    out = acc[:, :LANES]
    for i in range(LANES, value.shape[1], LANES):
        out = out + acc[:, i : i + LANES]
    return out


def block_kernel(wides, narrows, rows, *refs):
    own_shard = rows % 16 == 0
    refs = list(refs)
    count_ref, assign_ref, tok_ref, cot_ref = refs[:4]
    shard_in = refs[4 : 8 if own_shard else 5]
    (upw_ref, downw_ref,
     gt_ref, out_ref, shared_ref, upg_ref, downg_ref, total_ref, got_ref,
     flag_ref, live_ref, shard_ref, raw, wts, uc, qkv_buf, o_buf, lse_buf, nrm, dn, in_buf, xd_out, xd_in, yx_in,
     w_buf, dw_buf, wc_buf, up_buf, down_buf, g_buf, h_buf, dk_ref, dv_ref, dwo_ref, dwc_ref,
     s1, r1, r2, s3, r3, sum_buf, sq_buf, sq_n, sq_w,
     gz_sem, gp_sem, gc_sem, gr_sem, hop_sem, hopr_sem, send_sem, recv_sem, rs_sem, rsr_sem, own_sem, io_sem,
     c_sem, p_sem, z_sem, cr_sem, pr_sem, zr_sem, sn_sem, snr_sem, sw_sem, swr_sem) = refs[4 + len(shard_in):]
    lse_col = dk_ref
    if own_shard:
        raw = wts
    w_id, me = lax.axis_index("wide"), lax.axis_index("narrow")
    micros, length, width = tok_ref.shape
    blocks = length // ROWS
    part = length // narrows
    head = width // HEADS
    scale = 1.0 / math.sqrt(head)
    hidden_width = up_buf.shape[1]
    up_rows = width // wides
    down_rows = hidden_width // wides
    folds = hidden_width // width
    chunk_parts = ROWS // part
    half = narrows // 2
    q_id, parity = me // 2, lax.rem(me, 2)
    core = me + 1 - 2 * parity
    lane = lax.broadcasted_iota(jnp.int32, (1, LANES), 1)
    padded = shard_ref.shape[0]
    wq, wo = wts.at[:, pl.ds(0, 3 * width)], wts.at[:, pl.ds(3 * width, width)]

    def part_rows(n):
        return pl.ds(pl.multiple_of(n * part, part), part)

    def pick(ref, mb, at):
        value = ref[0, at, :].astype(F32)
        for j in range(1, micros):
            chosen = flag_ref[mb * micros + j : mb * micros + j + 1, 0:1] > 0
            value = jnp.where(chosen, ref[j, at, :].astype(F32), value)
        return value

    loads = [
        pltpu.make_async_copy(
            upw_ref.at[:, pl.ds(j * width, width)], h_buf.at[0, pl.ds(j * up_rows, up_rows)], own_sem.at[1 + j])
        for j in range(folds)
    ]
    loads.append(pltpu.make_async_copy(downw_ref, h_buf.at[1, pl.ds(0, down_rows)], own_sem.at[1 + folds]))
    for j in range(micros):
        loads.append(pltpu.make_async_copy(cot_ref.at[j], yx_in.at[j, :, 0], io_sem.at[j]))
    for copy in loads:
        copy.start()
    z_peers = [lax.rem(w_id + k, wides) for k in range(1, wides)]
    p_peers = [lax.rem(q_id + k, half) * 2 + parity for k in range(1, half)]
    greet([(z, me) for z in z_peers] + [(w_id, lax.rem(me + k, narrows)) for k in range(1, narrows)])

    if own_shard:
        proj_ref, outw_ref, ctrl_ref, norm_ref = shard_in
        shard_ref[:, : 3 * width] = proj_ref[...].astype(BF)
        shard_ref[:, 3 * width : 4 * width] = outw_ref[...].astype(BF)

        def spot(count, start):
            at = lax.broadcasted_iota(jnp.int32, (count, LANES), 0) + start
            return jnp.where(at == lax.broadcasted_iota(jnp.int32, (count, LANES), 1), 1.0, 0.0).astype(BF)

        extra = dot(ctrl_ref[...].astype(BF), spot(narrows, 0), 0, 0)
        left = norm_ref[...]
        for k in range(3):
            low = left.astype(BF)
            extra = extra + dot(low, spot(4, narrows + 4 * k), 0, 0)
            left = left - low.astype(F32)
        shard_ref[:, 4 * width :] = extra.astype(BF)
    else:
        shard_ref[...] = shard_in[0][...]

    def slot(zw, zn):
        return raw.at[pl.ds(pl.multiple_of((zw * narrows + zn) * padded, padded), padded)]

    own = pltpu.make_async_copy(shard_ref, slot(w_id, me), own_sem.at[0])
    own.start()
    gather_sends = []

    def spread(src, zw, zn, sem, device):
        copy = remote(src, slot(zw, zn), sem, gr_sem.at[zw, zn], device)
        copy.start()
        gather_sends.append(copy)

    def arrived(zw, zn):
        pltpu.make_async_copy(shard_ref, slot(zw, zn), gr_sem.at[zw, zn]).wait()

    for k, z in enumerate(z_peers):
        spread(shard_ref, w_id, me, gz_sem.at[k], (z, me))
    for k, p in enumerate(p_peers):
        spread(shard_ref, w_id, me, gp_sem.at[0, k], (w_id, p))
    spread(shard_ref, w_id, me, gc_sem.at[0, 0], (w_id, core))

    def up_part(z):
        return up_buf.at[pl.ds(pl.multiple_of(z * up_rows, up_rows), up_rows)]

    def down_part(z):
        return down_buf.at[pl.ds(pl.multiple_of(z * down_rows, down_rows), down_rows)]

    for copy in loads:
        copy.wait()
    own_up = pl.ds(pl.multiple_of(w_id * up_rows, up_rows), up_rows)
    for j in range(folds):
        up_buf[own_up, j * width : (j + 1) * width] = h_buf[0, j * up_rows : (j + 1) * up_rows, :].astype(BF)
    down_buf[pl.ds(pl.multiple_of(w_id * down_rows, down_rows), down_rows), :] = h_buf[1, :down_rows, :].astype(BF)

    def hop_send(hop):
        @pl.when((w_id >= hop - 1) & (w_id < wides - 1))
        def _():
            for i, piece in enumerate((up_part, down_part)):
                source = piece(w_id - (hop - 1))
                remote(source, source, hop_sem.at[hop - 1, 0, i], hopr_sem.at[hop - 1, 0, i], (w_id + 1, me)).start()

        @pl.when((w_id + (hop - 1) <= wides - 1) & (w_id > 0))
        def _():
            for i, piece in enumerate((up_part, down_part)):
                source = piece(w_id + (hop - 1))
                remote(source, source, hop_sem.at[hop - 1, 1, i], hopr_sem.at[hop - 1, 1, i], (w_id - 1, me)).start()

    def hop_arrived(hop):
        @pl.when(w_id >= hop)
        def _():
            for i, piece in enumerate((up_part, down_part)):
                target = piece(w_id - hop)
                pltpu.make_async_copy(target, target, hopr_sem.at[hop - 1, 0, i]).wait()

        @pl.when(w_id + hop <= wides - 1)
        def _():
            for i, piece in enumerate((up_part, down_part)):
                target = piece(w_id + hop)
                pltpu.make_async_copy(target, target, hopr_sem.at[hop - 1, 1, i]).wait()

    def hop_sent(hop):
        @pl.when((w_id >= hop - 1) & (w_id < wides - 1))
        def _():
            for i, piece in enumerate((up_part, down_part)):
                source = piece(w_id - (hop - 1))
                pltpu.make_async_copy(source, source, hop_sem.at[hop - 1, 0, i]).wait()

        @pl.when((w_id + (hop - 1) <= wides - 1) & (w_id > 0))
        def _():
            for i, piece in enumerate((up_part, down_part)):
                source = piece(w_id + (hop - 1))
                pltpu.make_async_copy(source, source, hop_sem.at[hop - 1, 1, i]).wait()

    for j in range(1, wides):
        zw = lax.rem(w_id + wides - j, wides)
        arrived(zw, me)
        for k, p in enumerate(p_peers):
            spread(slot(zw, me), zw, me, gp_sem.at[j, k], (w_id, p))
        spread(slot(zw, me), zw, me, gc_sem.at[j, 0], (w_id, core))
    hop_send(1)

    def choose(n, _):
        for mb in range(micros):
            value = yx_in[0, n, 0].astype(F32)
            for j in range(1, micros):
                chosen = flag_ref[mb * micros + j : mb * micros + j + 1, 0:1] > 0
                value = jnp.where(chosen, yx_in[j, n, 0].astype(F32), value)
            uc[mb, 1, part_rows(n), :] = value.astype(BF)
        return 0

    across = lax.broadcasted_iota(jnp.int32, count_ref.shape, 1)

    def spread_out(row, index):
        one = jnp.sum(jnp.where(across == index, row, 0.0), axis=1, keepdims=True)
        return jnp.broadcast_to(one, (1, LANES))

    for mb in range(micros):
        place = sum(jnp.where(assign_ref[j : j + 1, :] == mb, j, 0) for j in range(micros))
        alive = jnp.where(place < count_ref[...], 1.0, 0.0)
        for n in range(narrows):
            live_ref[mb, n : n + 1, :] = spread_out(alive, w_id * narrows + n)
        for j in range(micros):
            chosen = jnp.where(assign_ref[j : j + 1, :] == mb, 1.0, 0.0)
            flag_ref[mb * micros + j : mb * micros + j + 1, :] = spread_out(chosen, w_id * narrows + me)
    lax.fori_loop(0, narrows, choose, 0)
    dwc_ref[...] = jnp.zeros_like(dwc_ref)
    for i in range(1, half):
        zn = lax.rem(q_id + half - i, half) * 2 + parity
        for j in range(wides):
            zw = lax.rem(w_id + wides - j, wides)
            arrived(zw, zn)
            spread(slot(zw, zn), zw, zn, gc_sem.at[j, i], (w_id, core))

    def send(stage, mb, source, target, peer):
        @pl.when(peer != me)
        def _():
            remote(source, target, send_sem.at[stage, mb, peer], recv_sem.at[stage, mb, me], (w_id, peer)).start()

        @pl.when(peer == me)
        def _():
            pltpu.make_async_copy(source, target, recv_sem.at[stage, mb, me]).start()

    def received(stage, mb, peer, target):
        pltpu.make_async_copy(target, target, recv_sem.at[stage, mb, peer]).wait()

    def sent(stage, mb, source):
        def one(k, _):
            peer = lax.rem(me + k, narrows)
            pltpu.make_async_copy(source, source, send_sem.at[stage, mb, peer]).wait()
            return 0

        lax.fori_loop(1, narrows, one, 0)

    def to_some(body, start, stop):
        def one(k, _):
            body(lax.rem(q_id + lax.rem(k, half), half) * 2 + lax.rem(parity + k // half, 2))
            return 0

        lax.fori_loop(start, stop, one, 0)

    def to_all(body):
        to_some(body, 0, narrows)

    def send_rows(which, mb):
        to_all(lambda peer: send(
            which, mb, uc.at[mb, which, part_rows(peer)], in_buf.at[mb, me, which], peer))

    for mb in range(micros):
        send_rows(CF, mb)
    for i in range(half):
        for j in range(wides):
            arrived(j, 2 * i + 1 - parity)
    own.wait()

    if not own_shard:
        fold, group = padded // rows, raw.shape[1]
        for f in range(fold):
            start, stop = f * group, min((f + 1) * group, wts.shape[1])
            if start >= stop:
                break
            for i in range(width // LANES):
                here = lax.broadcasted_iota(jnp.int32, (LANES, raw.shape[0]), 0) + i * LANES
                there = lax.broadcasted_iota(jnp.int32, (LANES, raw.shape[0]), 1)
                match = (here // rows) * padded + f * rows + lax.rem(here, rows) == there
                take = jnp.where(match, 1.0, 0.0).astype(BF)
                wts[i * LANES : (i + 1) * LANES, start:stop] = dot(take, raw[:, : stop - start], 1, 0).astype(BF)
    extra = wts[:, 4 * width :]
    nrm[0:4, :] = norm_rows(extra, narrows)
    wc_buf[...] = jnp.where(lane < narrows, extra.astype(F32), 0).astype(BF)

    def forward(mb, hooks):
        def project(i, _):
            at = pl.ds(i * ROWS, ROWS)
            xhat, _ = norm_stats(pick(tok_ref, mb, at))
            al = (xhat * nrm[0:1, :] + nrm[1:2, :]).astype(BF)
            qkv_buf[mb, at, :] = dot(al, wq[...], 1, 0).astype(BF)
            return 0

        lax.fori_loop(0, blocks, project, 0)
        lse_col[...] = jnp.zeros_like(lse_col)
        keep = lax.broadcasted_iota(jnp.int32, (ROWS, ROWS), 1) <= lax.broadcasted_iota(jnp.int32, (ROWS, ROWS), 0)
        for i in range(blocks):
            keys = (i + 1) * ROWS
            at = pl.ds(i * ROWS, ROWS)

            def pair(hp, _, i=i, keys=keys, at=at):
                lanes = pl.ds(pl.multiple_of(hp * LANES, LANES), LANES)
                klanes = pl.ds(pl.multiple_of(hp * LANES + width, LANES), LANES)
                vlanes = pl.ds(pl.multiple_of(hp * LANES + 2 * width, LANES), LANES)
                q = qkv_buf[mb, at, lanes]
                k = qkv_buf[mb, pl.ds(0, keys), klanes]
                v = qkv_buf[mb, pl.ds(0, keys), vlanes]
                acc = None
                for h in range(2):
                    mine = lane // head == h
                    qm = jnp.where(mine, q * scale, 0).astype(BF)
                    vm = jnp.where(mine, v, 0).astype(BF)
                    s = dot(qm, k, 1, 1)
                    diag = jnp.where(keep, s[:, i * ROWS :], NEG_LARGE)
                    s = diag if i == 0 else jnp.concatenate([s[:, : i * ROWS], diag], axis=1)
                    m = jnp.max(s, axis=1, keepdims=True)
                    p = jnp.exp(s - m)
                    total = jnp.sum(p, axis=1, keepdims=True)
                    one = dot((p * (1.0 / total)).astype(BF), vm, 1, 0)
                    acc = one if acc is None else acc + one
                    lse_col[at, :] = jnp.where(lane == hp * 2 + h, m + jnp.log(total), lse_col[at, :])
                o_buf[mb, at, lanes] = acc.astype(BF)
                return 0

            lax.fori_loop(0, HEADS // 2, pair, 0)
            for hook in hooks.get(i, ()):
                hook()
        lse_buf[mb] = jnp.transpose(lse_col[...])[:HEADS, :]

        def finish(i, _):
            at = pl.ds(i * ROWS, ROWS)
            hidden = pick(tok_ref, mb, at) + dot(o_buf[mb, at, :], wo[...], 1, 0)
            xhat, _ = norm_stats(hidden)
            uc[mb, 0, at, :] = (xhat * nrm[2:3, :] + nrm[3:4, :]).astype(BF)
            return 0

        lax.fori_loop(0, blocks, finish, 0)

    def mix(mb):
        if mb > 0:
            sent(XD, mb - 1, xd_out.at[0])

        def logits(n, _):
            received(U, mb, n, in_buf.at[mb, n, 0])
            received(CF, mb, n, in_buf.at[mb, n, 1])
            w_buf[mb, n] = dot(in_buf[mb, n, 0], wc_buf[...], 1, 0).astype(BF).astype(F32)
            return 0

        lax.fori_loop(0, narrows, logits, 0)

        def rows_of(c, _):
            at = pl.ds(c * 16, 16)
            logit = [
                jnp.where(live_ref[mb, pl.ds(n, 1), :] > 0, w_buf[mb, n, at, :], NEG_LARGE) for n in range(narrows)
            ]
            top = functools.reduce(jnp.maximum, logit)
            exps = [jnp.exp(logit[n] - top) * live_ref[mb, pl.ds(n, 1), :] for n in range(narrows)]
            inverse = 1.0 / functools.reduce(jnp.add, exps)
            weights = [e * inverse for e in exps]
            for n in range(narrows):
                w_buf[mb, n, at, :] = weights[n]
            for which in range(2):
                values = [in_buf[mb, n, which, at, :].astype(F32) for n in range(narrows)]
                for e in range(narrows):
                    acc = functools.reduce(
                        jnp.add, [weights[n][:, e : e + 1] * values[n] for n in range(narrows)])
                    xd_out[e, which, at, :] = acc.astype(BF)
            return 0

        lax.fori_loop(0, part // 16, rows_of, 0)

    def send_mixture(mb, start, stop):
        to_some(lambda peer: send(XD, mb, xd_out.at[peer], xd_in.at[mb, me], peer), start, stop)

    def send_expert(mb, c):
        for k in range(chunk_parts):
            peer = c * chunk_parts + k
            send(YX, mb, xd_in.at[mb, peer], yx_in.at[mb, me], peer)

    def expert(mb):
        sent(U, mb, uc.at[mb, 0, pl.ds(0, part)])
        sent(CF, mb, uc.at[mb, 0, pl.ds(0, part)])
        if mb == micros - 1:
            sent(XD, mb, xd_out.at[0])

        def chunk(c, _):
            c = lax.rem(me // chunk_parts + c, blocks)
            at = pl.ds(c * chunk_parts, chunk_parts)
            for k in range(chunk_parts):
                received(XD, mb, c * chunk_parts + k, xd_in.at[mb, c * chunk_parts + k])
            x = xd_in[mb, at, 0].reshape(ROWS, width)
            dy = xd_in[mb, at, 1].reshape(ROWS, width)

            def tile(j, carry):
                y, dx = carry
                cols = pl.ds(pl.multiple_of(j * width, width), width)
                z = dot(x, up_buf[:, cols], 1, 0)
                zz = z * z
                t = jnp.tanh(GELU_A * (z + GELU_B * z * zz))
                ga = (0.5 * z * (1.0 + t)).astype(BF)
                slope = 0.5 * (1.0 + t) + (0.5 * GELU_A) * z * (1.0 - t * t) * (1.0 + (3.0 * GELU_B) * zz)
                y = y + dot(ga, down_buf[cols, :], 1, 0)
                dz = (dot(dy, down_buf[cols, :], 1, 1) * slope).astype(BF)
                dx = dx + dot(dz, up_buf[:, cols], 1, 1)
                g_buf[folds + j] += dot(ga, dy, 0, 0)
                g_buf[j] += dot(x, dz, 0, 0)
                return y, dx

            zero = jnp.zeros((ROWS, width), F32)
            y, dx = lax.fori_loop(0, folds, tile, (zero, zero))
            xd_in[mb, at, 0] = y.astype(BF).reshape(chunk_parts, part, width)
            xd_in[mb, at, 1] = dx.astype(BF).reshape(chunk_parts, part, width)
            send_expert(mb, c)
            return 0

        lax.fori_loop(0, blocks, chunk, 0)

    tiles = length // width
    per_part = width // part

    def du_place(mb, n):
        tile = n // per_part
        return (h_buf, tile) if mb == 0 else (g_buf, folds + tile)

    def outputs_arrived(mb):
        to_all(lambda peer: received(YX, mb, peer, yx_in.at[mb, peer]))

    def combine(mb):
        def member(n, _):
            buf, tile = du_place(mb, n)

            def rows_of(c, _):
                at = pl.ds(c * 16, 16)
                u = in_buf[mb, n, 0, at, :].astype(F32)
                cf = in_buf[mb, n, 1, at, :].astype(F32)
                weights = w_buf[mb, n, at, :]
                mixed = du = None
                dw = jnp.zeros((16, LANES), F32)
                for e in range(narrows):
                    y = yx_in[mb, e, 0, at, :].astype(F32)
                    dx = yx_in[mb, e, 1, at, :].astype(F32)
                    weight = weights[:, e : e + 1]
                    mixed = weight * y if e == 0 else mixed + weight * y
                    du = weight * dx if e == 0 else du + weight * dx
                    dw = jnp.where(lane == e, jnp.sum(dx * u + cf * y, axis=1, keepdims=True), dw)
                in_buf[mb, n, 1, at, :] = mixed.astype(BF)
                buf[tile, pl.ds(pl.multiple_of(lax.rem(n, per_part) * part + c * 16, 16), 16), :] = du
                dw_buf[n, at, :] = dw
                return 0

            lax.fori_loop(0, part // 16, rows_of, 0)
            return 0

        lax.fori_loop(0, narrows, member, 0)

        def group(n, acc):
            return acc + w_buf[mb, n] * dw_buf[n]

        inner = lax.fori_loop(0, narrows, group, jnp.zeros((part, LANES), F32))

        def finish(n):
            buf, tile = du_place(mb, n)
            dc = (w_buf[mb, n] * (dw_buf[n] - inner)).astype(BF)
            rows_n = pl.ds(pl.multiple_of(lax.rem(n, per_part) * part, part), part)
            du = buf[tile, rows_n, :] + dot(dc, wc_buf[...], 1, 1)
            dwc_ref[...] += dot(in_buf[mb, n, 0], dc, 0, 0)
            in_buf[mb, n, 0] = du.astype(BF)
            send(DU, mb, in_buf.at[mb, n, 0], uc.at[mb, 0, part_rows(me)], n)

        to_all(finish)

    def send_mixed(mb):
        to_all(lambda peer: send(MIX, mb, in_buf.at[mb, peer, 1], xd_out.at[me, mb], peer))

    per_tile = width // ROWS

    def kept(mb, what, i):
        buf, start = (h_buf, 0) if mb == 0 else (g_buf, folds)
        rows_i = pl.ds(pl.multiple_of(lax.rem(i, per_tile) * ROWS, ROWS), ROWS)
        return buf.at[start + what * tiles + i // per_tile, rows_i]

    def gradient_copies(mb):
        buf, start = (h_buf, 0) if mb == 0 else (g_buf, folds)
        return [
            pltpu.make_async_copy(
                buf.at[start + i], gt_ref.at[mb, pl.ds(i * width, width)], io_sem.at[micros + mb * tiles + i])
            for i in range(tiles)
        ]

    def row_copies(mb):
        return [pltpu.make_async_copy(o_buf.at[mb], out_ref.at[mb], io_sem.at[mb])]

    def backward_start(mb):
        to_all(lambda peer: received(DU, mb, peer, uc.at[mb, 0, part_rows(peer)]))

        def first(i, _):
            at = pl.ds(i * ROWS, ROWS)
            low = o_buf[mb, at, :]
            hidden = pick(tok_ref, mb, at) + dot(low, wo[...], 1, 0)
            kept(mb, 1, i)[...] = hidden
            xhat, rstd = norm_stats(hidden)
            du = uc[mb, 0, at, :].astype(F32)
            dn[2:3, :] += jnp.sum(du * xhat, axis=0, keepdims=True)
            dn[3:4, :] += jnp.sum(du, axis=0, keepdims=True)
            dh = uc[mb, 1, at, :].astype(F32) + norm_back(du, nrm[2:3, :], xhat, rstd)
            kept(mb, 0, i)[...] = dh
            db = dh.astype(BF)
            dwo_ref[...] += dot(low, db, 0, 0)
            o_buf[mb, at, :] = dot(db, wo[...], 1, 1).astype(BF)
            return 0

        lax.fori_loop(0, blocks, first, 0)

    def backward_pairs(mb, start, stop):
        keep = lax.broadcasted_iota(jnp.int32, (ROWS, ROWS), 0) <= lax.broadcasted_iota(jnp.int32, (ROWS, ROWS), 1)

        def pair(hp, _):
            lanes = pl.ds(pl.multiple_of(hp * LANES, LANES), LANES)
            klanes = pl.ds(pl.multiple_of(hp * LANES + width, LANES), LANES)
            vlanes = pl.ds(pl.multiple_of(hp * LANES + 2 * width, LANES), LANES)
            for i in range(blocks):
                keys = (i + 1) * ROWS
                at = pl.ds(i * ROWS, ROWS)
                q = qkv_buf[mb, at, lanes]
                k = qkv_buf[mb, pl.ds(0, keys), klanes]
                v = qkv_buf[mb, pl.ds(0, keys), vlanes]
                do = o_buf[mb, at, lanes]
                dq = dk = dv = None
                for h in range(2):
                    mine = lane // head == h
                    qm = jnp.where(mine, q * scale, 0).astype(BF)
                    dom = jnp.where(mine, do, 0).astype(BF)
                    km = jnp.where(mine, k * scale, 0).astype(BF)
                    s = dot(k, qm, 1, 1) - lse_buf[mb, pl.ds(hp * 2 + h, 1), at]
                    diag = jnp.where(keep, s[i * ROWS :], NEG_LARGE)
                    p = jnp.exp(diag if i == 0 else jnp.concatenate([s[: i * ROWS], diag], axis=0))
                    pdp = p * dot(v, dom, 1, 1)
                    inner = jnp.sum(pdp, axis=0, keepdims=True)
                    ds = (pdp - p * inner).astype(BF)
                    a = dot(p.astype(BF), dom, 1, 0)
                    b = dot(ds, qm, 1, 0)
                    c = dot(ds, km, 0, 0)
                    dv, dk, dq = (a, b, c) if h == 0 else (dv + a, dk + b, dq + c)
                qkv_buf[mb, at, lanes] = dq.astype(BF)
                if i:
                    dk_ref[: i * ROWS, :] += dk[: i * ROWS]
                    dv_ref[: i * ROWS, :] += dv[: i * ROWS]
                dk_ref[i * ROWS : keys, :] = dk[i * ROWS :]
                dv_ref[i * ROWS : keys, :] = dv[i * ROWS :]
            qkv_buf[mb, :, klanes] = dk_ref[...].astype(BF)
            qkv_buf[mb, :, vlanes] = dv_ref[...].astype(BF)
            return 0

        lax.fori_loop(start, stop, pair, 0)

    def backward_end(mb):
        def last(i, _):
            at = pl.ds(i * ROWS, ROWS)
            xhat, rstd = norm_stats(pick(tok_ref, mb, at))
            al = (xhat * nrm[0:1, :] + nrm[1:2, :]).astype(BF)
            dqkv = qkv_buf[mb, at, :]
            for j in range(3):
                g_buf[j] += dot(al, dqkv[:, j * width : (j + 1) * width], 0, 0)
            da = dot(dqkv, wq[...], 1, 1)
            dn[0:1, :] += jnp.sum(da * xhat, axis=0, keepdims=True)
            dn[1:2, :] += jnp.sum(da, axis=0, keepdims=True)
            kept(mb, 0, i)[...] += norm_back(da, nrm[0:1, :], xhat, rstd)
            return 0

        lax.fori_loop(0, blocks, last, 0)
        for copy in gradient_copies(mb):
            copy.start()

    def finish_rows(mb):
        to_all(lambda peer: received(MIX, mb, peer, xd_out.at[peer, mb]))

        def rows_of(i, _):
            mixed = xd_out[pl.ds(i * chunk_parts, chunk_parts), mb].reshape(ROWS, width).astype(F32)
            o_buf[mb, pl.ds(i * ROWS, ROWS), :] = (kept(mb, 1, i)[...] + mixed).astype(BF)
            return 0

        lax.fori_loop(0, blocks, rows_of, 0)
        for copy in row_copies(mb):
            copy.start()

    def relay(hop):
        def run():
            hop_arrived(hop)
            if hop < wides - 1:
                hop_send(hop + 1)

        return run

    up_at = pl.ds(pl.multiple_of(w_id * up_rows, up_rows), up_rows)
    down_tile = folds + w_id * down_rows // width
    down_at = pl.ds(pl.multiple_of(lax.rem(w_id * down_rows, width), down_rows), down_rows)

    def own_copies():
        copies = [
            pltpu.make_async_copy(g_buf.at[j, up_at], upg_ref.at[:, pl.ds(j * width, width)], own_sem.at[1 + j])
            for j in range(folds)
        ]
        return copies + [pltpu.make_async_copy(g_buf.at[down_tile, down_at], downg_ref, own_sem.at[1 + folds])]

    relays = [relay(hop) for hop in range(1, wides - 1)]
    early = relays[: (len(relays) + 1) // 2]
    late = relays[len(early) :]
    pairs = HEADS // 2
    for mb in range(micros):
        hooks = {}
        if mb == 0:
            hooks[min(2, blocks - 1)] = early
        elif mb == 1:
            hooks[min(1, blocks - 1)] = late
            hooks[min(2, blocks - 1)] = [lambda: mix(0), lambda: send_mixture(0, 0, narrows)]
        forward(mb, hooks)
        send_rows(U, mb)
    hop_arrived(wides - 1)
    g_buf[...] = jnp.zeros_like(g_buf)
    dwo_ref[...] = jnp.zeros_like(dwo_ref)
    dn[...] = jnp.zeros_like(dn)
    expert(0)
    mix(1)
    outputs_arrived(0)
    send_mixture(1, 0, half)
    combine(0)
    send_mixture(1, half, narrows)
    expert(1)
    for hop in range(1, wides):
        hop_sent(hop)
    for j in range(folds):
        up_buf[:, j * width : (j + 1) * width] = g_buf[j].astype(BF)
        down_buf[j * width : (j + 1) * width, :] = g_buf[folds + j].astype(BF)
    for k, z in enumerate(z_peers):
        for j in range(folds):
            remote(
                up_part(z).at[:, pl.ds(j * width, width)], got_ref.at[k, 0, pl.ds(j * up_rows, up_rows)],
                rs_sem.at[k, 1 + j], rsr_sem.at[k, 1 + j], (z, me)).start()
        remote(down_part(z), got_ref.at[k, 1], rs_sem.at[k, 0], rsr_sem.at[k, 0], (z, me)).start()
    owned = own_copies()
    for copy in owned:
        copy.start()
    backward_start(0)
    backward_pairs(0, 0, pairs // 2)
    for copy in owned:
        copy.wait()
    outputs_arrived(1)
    combine(1)
    backward_pairs(0, pairs // 2, pairs)
    send_mixed(0)
    g_buf[0:3] = jnp.zeros((3, width, width), F32)
    backward_end(0)
    send_mixed(1)
    backward_start(1)
    backward_pairs(1, 0, pairs)
    backward_end(1)

    dwc_ref[...] += jnp.transpose(jnp.concatenate(
        [jnp.zeros((narrows, width), F32), dn[...], jnp.zeros((LANES - 8 - narrows, width), F32)], axis=0))
    spans = [slice(j * width, (j + 1) * width) for j in range(4)] + [slice(4 * width, 4 * width + LANES)]
    q_peers = [lax.rem(q_id + k, half) for k in range(1, half)]

    def parts(zw, zn):
        start = (zw * narrows + zn) * rows // padded * padded
        at = pl.ds(pl.multiple_of(start, padded), padded)
        return [g_buf[j, at, :] for j in range(3)] + [dwo_ref[at, :], dwc_ref[at, :]]

    sends = []
    if own_shard:
        for k in range(half):
            there = lax.rem(q_id + 1 + k, half)

            def fill(z, _, there=there):
                for j, value in enumerate(parts(z, 2 * there + 1 - parity)):
                    s1[there, z, :, spans[j]] = value.astype(BF)
                return 0

            lax.fori_loop(0, wides, fill, 0)
            copy = remote(s1.at[there], r1.at[there], c_sem.at[k], cr_sem.at[there], (w_id, core))
            copy.start()
            sends.append(copy)
        for k in range(half):
            there = lax.rem(q_id + 1 + k, half)
            pltpu.make_async_copy(r1.at[there], r1.at[there], cr_sem.at[there]).wait()
            last = k == half - 1

            sends[k].wait_send()

            def add(z, _, there=there, last=last):
                for j, value in enumerate(parts(z, 2 * there + parity)):
                    value = value + r1[there, z, :, spans[j]].astype(F32)
                    if last:
                        sum_buf[z, :, spans[j]] = value
                    else:
                        s1[there, z, :, spans[j]] = value.astype(BF)
                return 0

            lax.fori_loop(0, wides, add, 0)
            if not last:
                copy = remote(s1.at[there], r2.at[q_id], p_sem.at[k], pr_sem.at[q_id], (w_id, there * 2 + parity))
                copy.start()
                sends.append(copy)
    else:
        plain = [
            pltpu.make_async_copy(g_buf.at[j], shared_ref.at[:, pl.ds(j * width, width)], c_sem.at[j])
            for j in range(3)
        ]
        plain.append(pltpu.make_async_copy(dwo_ref, shared_ref.at[:, pl.ds(3 * width, width)], c_sem.at[3]))
        plain.append(pltpu.make_async_copy(dwc_ref, shared_ref.at[:, pl.ds(4 * width, LANES)], c_sem.at[4]))
        for copy in plain:
            copy.start()
        for copy in plain:
            copy.wait()

    for mb in range(micros):
        finish_rows(mb)
    for copy in gradient_copies(0):
        copy.wait()

    def got_place(k, i):
        at = (k * 2 + i) * down_rows
        return uc.at[at // (2 * length), at // length % 2, pl.ds(at % length, down_rows)]

    brought = []
    for k in range(wides - 1):
        for j in range(folds):
            mine = up_part(0).at[:, pl.ds(j * width, width)]
            theirs = got_ref.at[k, 0, pl.ds(j * up_rows, up_rows)]
            pltpu.make_async_copy(mine, mine, rs_sem.at[k, 1 + j]).wait()
            pltpu.make_async_copy(theirs, theirs, rsr_sem.at[k, 1 + j]).wait()
        pltpu.make_async_copy(down_part(0), down_part(0), rs_sem.at[k, 0]).wait()
        pltpu.make_async_copy(got_ref.at[k, 1], got_ref.at[k, 1], rsr_sem.at[k, 0]).wait()
        for i in range(2):
            brought.append(pltpu.make_async_copy(got_ref.at[k, i], got_place(k, i), hop_sem.at[k, i, 0]))
            brought[-1].start()
    for copy in brought:
        copy.wait()
    sq_buf[...] = jnp.zeros_like(sq_buf)
    mine_up = [h_buf.at[0, pl.ds(j * up_rows, up_rows)] for j in range(folds)]
    mine_down = h_buf.at[1, pl.ds(0, down_rows)]
    back = [
        pltpu.make_async_copy(upg_ref.at[:, pl.ds(j * width, width)], mine_up[j], own_sem.at[1 + j])
        for j in range(folds)
    ]
    back.append(pltpu.make_async_copy(downg_ref, mine_down, own_sem.at[1 + folds]))
    for copy in back:
        copy.start()
    for copy in back:
        copy.wait()
    for j in range(folds):
        value = mine_up[j][...]
        for k in range(wides - 1):
            value = value + got_place(k, 0)[j * up_rows : (j + 1) * up_rows, :].astype(F32)
        mine_up[j][...] = value
        sq_buf[...] += fold_rows(value * value)
    value = mine_down[...]
    for k in range(wides - 1):
        value = value + got_place(k, 1)[...].astype(F32)
    mine_down[...] = value
    sq_buf[...] += fold_rows(value * value)
    owned = [
        pltpu.make_async_copy(mine_up[j], upg_ref.at[:, pl.ds(j * width, width)], own_sem.at[1 + j])
        for j in range(folds)
    ]
    owned.append(pltpu.make_async_copy(mine_down, downg_ref, own_sem.at[1 + folds]))
    for copy in owned:
        copy.start()

    if own_shard:
        for there in q_peers:
            pltpu.make_async_copy(r2.at[there], r2.at[there], pr_sem.at[there]).wait()
        for k in range(wides):
            z = lax.rem(w_id + 1 + k, wides)
            acc = sum_buf[z]
            for there in q_peers:
                acc = acc + r2[there, z].astype(F32)
            if k < wides - 1:
                s3[z] = acc.astype(BF)
                copy = remote(s3.at[z], r3.at[w_id], z_sem.at[k], zr_sem.at[w_id], (z, me))
                copy.start()
                sends.append(copy)
            else:
                shared_ref[...] = acc
        for z in z_peers:
            pltpu.make_async_copy(r3.at[z], r3.at[z], zr_sem.at[z]).wait()
            shared_ref[...] += r3[z].astype(F32)

        value = shared_ref[...]
        sq_buf[...] += fold_rows(value * value)
        n_peers = [lax.rem(me + k, narrows) for k in range(1, narrows)]
        for k, p in enumerate(n_peers):
            copy = remote(sq_buf, sq_n.at[me], sn_sem.at[k], snr_sem.at[me], (w_id, p))
            copy.start()
            sends.append(copy)
    for copy in gradient_copies(1) + row_copies(0) + row_copies(1) + owned:
        copy.wait()
    for copy in gather_sends:
        copy.wait_send()
    for mb in range(micros):
        sent(YX, mb, xd_in.at[mb, 0])
        sent(DU, mb, in_buf.at[mb, 0, 0])
        sent(MIX, mb, in_buf.at[mb, 0, 0])
    if own_shard:
        sq_n[me] = sq_buf[...]
        for p in n_peers:
            pltpu.make_async_copy(sq_n.at[p], sq_n.at[p], snr_sem.at[p]).wait()
        acc = sq_n[0]
        for k in range(1, narrows):
            acc = acc + sq_n[k]
        sq_w[w_id] = acc
        for k, z in enumerate(z_peers):
            copy = remote(sq_w.at[w_id], sq_w.at[w_id], sw_sem.at[k], swr_sem.at[w_id], (z, me))
            copy.start()
            sends.append(copy)
        for z in z_peers:
            pltpu.make_async_copy(sq_w.at[z], sq_w.at[z], swr_sem.at[z]).wait()
        acc = sq_w[0]
        for k in range(1, wides):
            acc = acc + sq_w[k]
        total_ref[...] = acc
    else:
        total_ref[...] = sq_buf[...]
    for copy in sends[half:]:
        copy.wait_send()


def run_block(counts, assign, tokens, cot, shard, up, down, wides, narrows, rows):
    micros, length, width = tokens.shape
    part = length // narrows
    hidden_width = up.shape[1]
    folds = hidden_width // width
    devices = wides * narrows
    hbm = pl.BlockSpec(memory_space=pl.ANY)
    vmem = pl.BlockSpec(memory_space=pltpu.VMEM)
    pairs = pltpu.VMEM((micros, narrows, 2, part, width), BF)
    pairs_one = pltpu.VMEM((narrows, 2, part, width), BF)
    sems = pltpu.SemaphoreType.DMA
    half = narrows // 2
    cols = 4 * width + LANES
    padded = max(rows, 16)
    shard_shape = (padded, cols) if rows == padded else shard[0].shape
    raw_shape = (16, LANES) if rows == padded else (devices * padded, shard_shape[1])
    block = (half, wides, padded, cols) if rows == padded else (1, 1, 16, LANES)
    return pl.pallas_call(
        functools.partial(block_kernel, wides, narrows, rows),
        out_shape=[
            jax.ShapeDtypeStruct((micros, length, width), F32),
            jax.ShapeDtypeStruct((micros, length, width), BF),
            jax.ShapeDtypeStruct((padded if rows == padded else width, cols), F32),
            jax.ShapeDtypeStruct(up.shape, F32),
            jax.ShapeDtypeStruct(down.shape, F32),
            jax.ShapeDtypeStruct((8, LANES), F32),
            jax.ShapeDtypeStruct((wides - 1, 2) + down.shape, BF),
        ],
        in_specs=[vmem] * 3 + [hbm] + [vmem] * len(shard) + [hbm] * 2,
        out_specs=[hbm, hbm, vmem if rows == padded else hbm, hbm, hbm, vmem, hbm],
        scratch_shapes=[
            pltpu.VMEM((8, LANES), F32),
            pltpu.VMEM((micros, narrows, LANES), F32),
            pltpu.VMEM(shard_shape, BF),
            pltpu.VMEM(raw_shape, BF),
            pltpu.VMEM((width, cols), BF),
            pltpu.VMEM((micros, 2, length, width), BF),
            pltpu.VMEM((micros, length, 3 * width), BF),
            pltpu.VMEM((micros, length, width), BF),
            pltpu.VMEM((micros, HEADS, length), F32),
            pltpu.VMEM((8, width), F32),
            pltpu.VMEM((8, width), F32),
            pairs,
            pairs_one,
            pairs,
            pairs,
            pltpu.VMEM((micros, narrows, part, LANES), F32),
            pltpu.VMEM((narrows, part, LANES), F32),
            pltpu.VMEM((width, LANES), BF),
            pltpu.VMEM((width, hidden_width), BF),
            pltpu.VMEM((hidden_width, width), BF),
            pltpu.VMEM((2 * folds, width, width), F32),
            pltpu.VMEM((2 * (length // width), width, width), F32),
            pltpu.VMEM((length, LANES), F32),
            pltpu.VMEM((length, LANES), F32),
            pltpu.VMEM((width, width), F32),
            pltpu.VMEM((width, LANES), F32),
            pltpu.VMEM(block, BF),
            pltpu.VMEM(block, BF),
            pltpu.VMEM(block, BF),
            pltpu.VMEM(block[1:], BF),
            pltpu.VMEM(block[1:], BF),
            pltpu.VMEM(block[1:], F32),
            pltpu.VMEM((8, LANES), F32),
            pltpu.VMEM((narrows, 8, LANES), F32),
            pltpu.VMEM((wides, 8, LANES), F32),
            sems((wides - 1,)),
            sems((wides, half - 1)),
            sems((wides, half)),
            sems((wides, narrows)),
            sems((wides - 1, 2, 2)),
            sems((wides - 1, 2, 2)),
            sems((6, micros, narrows)),
            sems((6, micros, narrows)),
            sems((wides - 1, 1 + folds)),
            sems((wides - 1, 1 + folds)),
            sems((2 + folds,)),
            sems((micros * (1 + length // width),)),
            sems((half,)),
            sems((half,)),
            sems((wides,)),
            sems((half,)),
            sems((half,)),
            sems((wides,)),
            sems((narrows - 1,)),
            sems((narrows,)),
            sems((wides - 1,)),
            sems((wides,)),
        ],
        compiler_params=pltpu.CompilerParams(
            collective_id=0, has_side_effects=True, vmem_limit_bytes=64 << 20),
        name="block",
    )(counts, assign, tokens, cot.reshape(micros, narrows, part, width), *shard, up, down)


def adam_values(weight, first_state, second_state, gradient, factor, rate, decay):
    clipped = gradient * factor
    first_new = BETA_ONE * first_state + (1.0 - BETA_ONE) * clipped
    second_new = BETA_TWO * second_state + (1.0 - BETA_TWO) * clipped * clipped
    first_hat = first_new / (1.0 - BETA_ONE**STEP)
    second_hat = second_new / (1.0 - BETA_TWO**STEP)
    weight_new = weight - rate * (first_hat / (jnp.sqrt(second_hat) + ADAM_EPS) + decay * weight)
    return weight_new, first_new, second_new, weight_new.astype(BF)


def final_kernel(wides, narrows, assign_ref, total_ref, shared_ref, *refs):
    states, refs = refs[:18], refs[18:]
    upg_ref, downg_ref = refs[:2]
    moved = (len(refs) - 29) // 2
    gt_in, out_in = refs[2 : 2 + moved], refs[2 + moved : 2 + 2 * moved]
    out_ref, gt_ref, norm_out = refs[2 + 2 * moved : 5 + 2 * moved]
    news = refs[5 + 2 * moved :]
    step = pl.program_id(0)
    for j in range(moved):
        gt_ref[j] = gt_in[j][0]
        out_ref[j] = out_in[j][0]
    grad_norm = jnp.sqrt(jnp.sum(jnp.sum(total_ref[...], axis=0, keepdims=True), axis=1, keepdims=True))
    factor = CLIP_NORM / jnp.maximum(grad_norm, CLIP_NORM)

    def update(k, gradient, rate, decay):
        values = [ref[0] if len(ref.shape) == 3 else ref[...] for ref in states[3 * k : 3 * k + 3]]
        for ref, value in zip(news[4 * k : 4 * k + 4], adam_values(*values, gradient, factor, rate, decay)):
            if len(ref.shape) == 3:
                ref[0] = value
            else:
                ref[...] = value

    @pl.when(step == 0)
    def _():
        norm_out[...] = grad_norm
        width = states[6].shape[1]
        extra = shared_ref[:, 4 * width :]
        chosen = lax.broadcasted_iota(jnp.int32, (narrows + 8, LANES), 0) == lax.broadcasted_iota(
            jnp.int32, (narrows + 8, LANES), 1)
        turned = lax.dot_general(
            jnp.where(chosen, 1.0, 0.0), extra, (((1,), (1,)), ((), ())), precision=lax.Precision.HIGHEST,
            preferred_element_type=F32)
        update(0, turned[narrows : narrows + 4], 0.3, 0.0)
        update(1, shared_ref[:, : 3 * width], 0.03, DECAY_RATE)
        update(2, shared_ref[:, 3 * width : 4 * width], 0.2, DECAY_RATE)
        update(3, turned[:narrows], 0.015, DECAY_RATE)

    update(4, upg_ref[...], 0.1, DECAY_RATE)
    update(5, downg_ref[...], 0.1, DECAY_RATE)


def run_final(assign, total, shared, states, upg, downg, grad_rows, out_low, wides, narrows):
    steps = max(1, upg.shape[0] // 32)
    whole = lambda x: pl.BlockSpec(x.shape, lambda i, s: (0,) * len(x.shape))
    split2 = lambda x: pl.BlockSpec((x.shape[0] // steps, x.shape[1]), lambda i, s: (i, 0))
    split3 = lambda x: pl.BlockSpec((1, x.shape[1] // steps, x.shape[2]), lambda i, s: (0, i, 0))
    micros, length, width = grad_rows.shape

    def placed(j):
        def index(i, s):
            return s[lax.axis_index("wide") * narrows + lax.axis_index("narrow"), j], i, 0

        return pl.BlockSpec((1, length // steps, width), index)

    taken = [placed(j) for j in range(micros)]
    given = pl.BlockSpec((micros, length // steps, width), lambda i, s: (0, i, 0))
    spec = lambda x: split3(x) if len(x.shape) == 3 else whole(x)
    news = []
    for k in range(6):
        shape = states[3 * k].shape
        news += [jax.ShapeDtypeStruct(shape, F32)] * 3 + [jax.ShapeDtypeStruct(shape, BF)]
    one = jax.ShapeDtypeStruct((1, 1), F32)
    return pl.pallas_call(
        functools.partial(final_kernel, wides, narrows),
        grid_spec=pltpu.PrefetchScalarGridSpec(
            num_scalar_prefetch=1,
            grid=(steps,),
            in_specs=[whole(total), whole(shared)] + [spec(x) for x in states] + [split2(upg), split2(downg)] + taken * 2,
            out_specs=[given, given, whole(one)] + [spec(x) for x in news],
        ),
        out_shape=[
            jax.ShapeDtypeStruct(out_low.shape, BF), jax.ShapeDtypeStruct(grad_rows.shape, F32), one] + news,
        name="final",
    )(assign, total, shared, *states, upg, downg, *[grad_rows] * micros, *[out_low] * micros)


def per_device(tokens, cotangent, seq_counts, micro_assign, *states):
    wides, narrows = lax.axis_size("wide"), lax.axis_size("narrow")
    norm_params, project_weight, output_weight, control_weight, up_weight, down_weight = states[::3]
    rows = project_weight.shape[0]
    padded = max(rows, 16)
    if rows == padded:
        shard = (project_weight, output_weight, control_weight.T, norm_params)
    else:
        norm_turned = norm_params.T
        high = lax.reduce_precision(norm_turned, 8, 7)
        middle = lax.reduce_precision(norm_turned - high, 8, 7)
        lower = norm_turned - high - middle
        extra = jnp.concatenate([control_weight, high, middle, lower], axis=1).astype(BF)
        extra = jnp.pad(extra, ((0, 0), (0, LANES - extra.shape[1])))
        joined = jnp.concatenate([project_weight.astype(BF), output_weight.astype(BF), extra], axis=1)
        fold = padded // rows
        group = -(-(joined.shape[1] // LANES) // fold) * LANES
        joined = jnp.pad(joined, ((0, 0), (0, fold * group - joined.shape[1])))
        shard = (joined.reshape(rows, fold, group).transpose(1, 0, 2).reshape(padded, group),)
    grad_rows, out_low, shared, upg, downg, total, _ = run_block(
        seq_counts[None], micro_assign.T, tokens, cotangent, shard, up_weight[0], down_weight[0], wides, narrows, rows)
    if rows < padded:
        both = ("wide", "narrow")
        shared = lax.psum_scatter(shared, both, scatter_dimension=0, tiled=True)
        total = lax.psum(total.at[0, 0].add(jnp.sum(shared * shared)), both)
    states = states[:9] + tuple(x.T for x in states[9:12]) + states[12:]
    out_rows, grad_tokens, grad_norm, *news = run_final(
        micro_assign, total, shared, states, upg, downg, grad_rows, out_low, wides, narrows)
    news[12:16] = [x.T for x in news[12:16]]
    return (out_rows, grad_tokens, grad_norm.reshape(()), *news)


def solution(mesh):
    both = ("wide", "narrow")
    rows3, cols, rows2, expert = P(both, None, None), P(None, both), P(both, None), P("narrow", "wide", None)
    return jax.shard_map(
        per_device,
        mesh=mesh,
        in_specs=(rows3, rows3, P(), P()) + (cols,) * 3 + (rows2,) * 9 + (expert,) * 6,
        out_specs=(rows3, rows3, P()) + (cols,) * 4 + (rows2,) * 12 + (expert,) * 8,
        check_vma=False,
    )
```

```python
import functools
import math

import jax
import jax.numpy as jnp
from jax import lax
from jax.experimental import pallas as pl
from jax.experimental.pallas import tpu as pltpu
from jax.sharding import PartitionSpec as P

HEADS = 8
STEP = 5
NEG_LARGE = -1e30
NORM_EPS = 1e-05
CLIP_NORM = 0.05
BETA_ONE = 0.5
BETA_TWO = 0.5
ADAM_EPS = 1e-08
DECAY_RATE = 0.1

BF = jnp.bfloat16
F32 = jnp.float32
MESH = pl.DeviceIdType.MESH
LANES = 128
ROWS = 256
GELU_A = math.sqrt(2.0 / math.pi)
GELU_B = 0.044715


def dot(a, b, ca, cb):
    return lax.dot_general(a, b, (((ca,), (cb,)), ((), ())), preferred_element_type=F32)


def norm_stats(v):
    centred = v - jnp.mean(v, axis=-1, keepdims=True)
    rstd = lax.rsqrt(jnp.mean(centred * centred, axis=-1, keepdims=True) + NORM_EPS)
    return centred * rstd, rstd


def norm_back(grad, gain, xhat, rstd):
    t = grad * gain
    return rstd * (t - jnp.mean(t, axis=-1, keepdims=True) - xhat * jnp.mean(t * xhat, axis=-1, keepdims=True))


def remote(src, dst, send, recv, device):
    return pltpu.make_async_remote_copy(
        src_ref=src, dst_ref=dst, send_sem=send, recv_sem=recv, device_id=device, device_id_type=MESH
    )


def greet(devices):
    barrier = pltpu.get_barrier_semaphore()
    for device in devices:
        pl.semaphore_signal(barrier, inc=1, device_id=device, device_id_type=MESH)
    pl.semaphore_wait(barrier, len(devices))


def norm_rows(extra, experts):
    turned = jnp.transpose(extra.astype(F32))
    return turned[experts : experts + 4] + turned[experts + 4 : experts + 8] + turned[experts + 8 : experts + 12]


U, CF, XD, YX, DU, MIX = range(6)


def fold_rows(value):
    acc = value[:8]
    for i in range(8, value.shape[0], 8):
        acc = acc + value[i : i + 8]
    out = acc[:, :LANES]
    for i in range(LANES, value.shape[1], LANES):
        out = out + acc[:, i : i + LANES]
    return out


def block_kernel(wides, narrows, rows, *refs):
    own_shard = rows % 16 == 0
    refs = list(refs)
    count_ref, assign_ref, tok_ref, cot_ref = refs[:4]
    shard_in = refs[4 : 8 if own_shard else 5]
    (upw_ref, downw_ref,
     gt_ref, out_ref, shared_ref, upg_ref, downg_ref, total_ref, got_ref,
     flag_ref, live_ref, shard_ref, raw, wts, uc, qkv_buf, o_buf, lse_buf, nrm, dn, in_buf, xd_out, xd_in, yx_in,
     w_buf, wc_buf, wt_buf, g_buf, h_buf, dk_ref, dv_ref, dwo_ref, dwc_ref,
     s1, r1, r2, s3, r3, sum_buf, sq_buf, sq_n, sq_w,
     gz_sem, gp_sem, gc_sem, gr_sem, hop_sem, hopr_sem, send_sem, recv_sem, rs_sem, rsr_sem, own_sem, io_sem,
     c_sem, p_sem, z_sem, cr_sem, pr_sem, zr_sem, sn_sem, snr_sem, sw_sem, swr_sem) = refs[4 + len(shard_in):]
    lse_col = dk_ref
    if own_shard:
        raw = wts
    w_id, me = lax.axis_index("wide"), lax.axis_index("narrow")
    micros, length, width = tok_ref.shape
    blocks = length // ROWS
    part = length // narrows
    head = width // HEADS
    scale = 1.0 / math.sqrt(head)
    folds = wt_buf.shape[1] // 2
    hidden_width = folds * width
    up_rows = width // wides
    down_rows = hidden_width // wides
    per_shard = width // down_rows
    chunk_parts = ROWS // part
    half = narrows // 2
    q_id, parity = me // 2, lax.rem(me, 2)
    core = me + 1 - 2 * parity
    lane = lax.broadcasted_iota(jnp.int32, (1, LANES), 1)
    padded = shard_ref.shape[0]
    wq, wo = wts.at[:, pl.ds(0, 3 * width)], wts.at[:, pl.ds(3 * width, width)]

    def part_rows(n):
        return pl.ds(pl.multiple_of(n * part, part), part)

    def pick(ref, mb, at):
        value = ref[0, at, :].astype(F32)
        for j in range(1, micros):
            chosen = flag_ref[mb * micros + j : mb * micros + j + 1, 0:1] > 0
            value = jnp.where(chosen, ref[j, at, :].astype(F32), value)
        return value

    loads = [
        pltpu.make_async_copy(
            upw_ref.at[:, pl.ds(j * width, width)], h_buf.at[0, pl.ds(j * up_rows, up_rows)], own_sem.at[1 + j])
        for j in range(folds)
    ]
    loads.append(pltpu.make_async_copy(downw_ref, h_buf.at[1, pl.ds(0, down_rows)], own_sem.at[1 + folds]))
    for j in range(micros):
        loads.append(pltpu.make_async_copy(cot_ref.at[j], yx_in.at[j, :, 0], io_sem.at[j]))
    for copy in loads:
        copy.start()
    z_peers = [lax.rem(w_id + k, wides) for k in range(1, wides)]
    p_peers = [lax.rem(q_id + k, half) * 2 + parity for k in range(1, half)]
    greet([(z, me) for z in z_peers] + [(w_id, lax.rem(me + k, narrows)) for k in range(1, narrows)])

    if own_shard:
        proj_ref, outw_ref, ctrl_ref, norm_ref = shard_in
        shard_ref[:, : 3 * width] = proj_ref[...].astype(BF)
        shard_ref[:, 3 * width : 4 * width] = outw_ref[...].astype(BF)

        def spot(count, start):
            at = lax.broadcasted_iota(jnp.int32, (count, LANES), 0) + start
            return jnp.where(at == lax.broadcasted_iota(jnp.int32, (count, LANES), 1), 1.0, 0.0).astype(BF)

        extra = dot(ctrl_ref[...].astype(BF), spot(narrows, 0), 0, 0)
        left = norm_ref[...]
        for k in range(3):
            low = left.astype(BF)
            extra = extra + dot(low, spot(4, narrows + 4 * k), 0, 0)
            left = left - low.astype(F32)
        shard_ref[:, 4 * width :] = extra.astype(BF)
    else:
        shard_ref[...] = shard_in[0][...]

    def slot(zw, zn):
        return raw.at[pl.ds(pl.multiple_of((zw * narrows + zn) * padded, padded), padded)]

    own = pltpu.make_async_copy(shard_ref, slot(w_id, me), own_sem.at[0])
    own.start()
    gather_sends = []

    def spread(src, zw, zn, sem, device):
        copy = remote(src, slot(zw, zn), sem, gr_sem.at[zw, zn], device)
        copy.start()
        gather_sends.append(copy)

    def arrived(zw, zn):
        pltpu.make_async_copy(shard_ref, slot(zw, zn), gr_sem.at[zw, zn]).wait()

    for k, z in enumerate(z_peers):
        spread(shard_ref, w_id, me, gz_sem.at[k], (z, me))
    for k, p in enumerate(p_peers):
        spread(shard_ref, w_id, me, gp_sem.at[0, k], (w_id, p))
    spread(shard_ref, w_id, me, gc_sem.at[0, 0], (w_id, core))

    for copy in loads:
        copy.wait()
    for j in range(folds):
        rows_j = slice(j * up_rows, (j + 1) * up_rows)
        wt_buf[w_id, j] = h_buf[0, rows_j, :].astype(BF)
        wt_buf[w_id, folds + j] = h_buf[1, rows_j, :].astype(BF)

    def hop_send(hop):
        @pl.when((w_id >= hop - 1) & (w_id < wides - 1))
        def _():
            source = wt_buf.at[w_id - (hop - 1)]
            remote(source, source, hop_sem.at[hop - 1, 0], hopr_sem.at[hop - 1, 0], (w_id + 1, me)).start()

        @pl.when((w_id + (hop - 1) <= wides - 1) & (w_id > 0))
        def _():
            source = wt_buf.at[w_id + (hop - 1)]
            remote(source, source, hop_sem.at[hop - 1, 1], hopr_sem.at[hop - 1, 1], (w_id - 1, me)).start()

    def hop_arrived(hop):
        @pl.when(w_id >= hop)
        def _():
            pltpu.make_async_copy(wt_buf.at[0], wt_buf.at[w_id - hop], hopr_sem.at[hop - 1, 0]).wait()

        @pl.when(w_id + hop <= wides - 1)
        def _():
            pltpu.make_async_copy(wt_buf.at[0], wt_buf.at[w_id + hop], hopr_sem.at[hop - 1, 1]).wait()

    def hop_sent(hop):
        @pl.when((w_id >= hop - 1) & (w_id < wides - 1))
        def _():
            pltpu.make_async_copy(wt_buf.at[0], wt_buf.at[0], hop_sem.at[hop - 1, 0]).wait()

        @pl.when((w_id + (hop - 1) <= wides - 1) & (w_id > 0))
        def _():
            pltpu.make_async_copy(wt_buf.at[0], wt_buf.at[0], hop_sem.at[hop - 1, 1]).wait()

    for j in range(1, wides):
        zw = lax.rem(w_id + wides - j, wides)
        arrived(zw, me)
        for k, p in enumerate(p_peers):
            spread(slot(zw, me), zw, me, gp_sem.at[j, k], (w_id, p))
        spread(slot(zw, me), zw, me, gc_sem.at[j, 0], (w_id, core))
    hop_send(1)

    def choose(n, _):
        for mb in range(micros):
            value = yx_in[0, n, 0].astype(F32)
            for j in range(1, micros):
                chosen = flag_ref[mb * micros + j : mb * micros + j + 1, 0:1] > 0
                value = jnp.where(chosen, yx_in[j, n, 0].astype(F32), value)
            uc[mb, 1, part_rows(n), :] = value.astype(BF)
        return 0

    across = lax.broadcasted_iota(jnp.int32, count_ref.shape, 1)

    def spread_out(row, index):
        one = jnp.sum(jnp.where(across == index, row, 0.0), axis=1, keepdims=True)
        return jnp.broadcast_to(one, (1, LANES))

    for mb in range(micros):
        place = sum(jnp.where(assign_ref[j : j + 1, :] == mb, j, 0) for j in range(micros))
        alive = jnp.where(place < count_ref[...], 1.0, 0.0)
        for n in range(narrows):
            live_ref[mb, n : n + 1, :] = spread_out(alive, w_id * narrows + n)
        for j in range(micros):
            chosen = jnp.where(assign_ref[j : j + 1, :] == mb, 1.0, 0.0)
            flag_ref[mb * micros + j : mb * micros + j + 1, :] = spread_out(chosen, w_id * narrows + me)
    lax.fori_loop(0, narrows, choose, 0)
    dwc_ref[...] = jnp.zeros_like(dwc_ref)
    for i in range(1, half):
        zn = lax.rem(q_id + half - i, half) * 2 + parity
        for j in range(wides):
            zw = lax.rem(w_id + wides - j, wides)
            arrived(zw, zn)
            spread(slot(zw, zn), zw, zn, gc_sem.at[j, i], (w_id, core))

    def send(stage, mb, source, target, peer):
        @pl.when(peer != me)
        def _():
            remote(source, target, send_sem.at[stage, mb, peer], recv_sem.at[stage, mb, me], (w_id, peer)).start()

        @pl.when(peer == me)
        def _():
            pltpu.make_async_copy(source, target, recv_sem.at[stage, mb, me]).start()

    def received(stage, mb, peer, target):
        pltpu.make_async_copy(target, target, recv_sem.at[stage, mb, peer]).wait()

    def sent(stage, mb, source):
        def one(k, _):
            peer = lax.rem(me + k, narrows)
            pltpu.make_async_copy(source, source, send_sem.at[stage, mb, peer]).wait()
            return 0

        lax.fori_loop(1, narrows, one, 0)

    def to_some(body, start, stop):
        def one(k, _):
            body(lax.rem(q_id + lax.rem(k, half), half) * 2 + lax.rem(parity + k // half, 2))
            return 0

        lax.fori_loop(start, stop, one, 0)

    def to_all(body):
        to_some(body, 0, narrows)

    def send_rows(which, mb):
        to_all(lambda peer: send(
            which, mb, uc.at[mb, which, part_rows(peer)], in_buf.at[mb, me, which], peer))

    for mb in range(micros):
        send_rows(CF, mb)
    for i in range(half):
        for j in range(wides):
            arrived(j, 2 * i + 1 - parity)
    own.wait()

    if not own_shard:
        fold, group = padded // rows, raw.shape[1]
        for f in range(fold):
            start, stop = f * group, min((f + 1) * group, wts.shape[1])
            if start >= stop:
                break
            for i in range(width // LANES):
                here = lax.broadcasted_iota(jnp.int32, (LANES, raw.shape[0]), 0) + i * LANES
                there = lax.broadcasted_iota(jnp.int32, (LANES, raw.shape[0]), 1)
                match = (here // rows) * padded + f * rows + lax.rem(here, rows) == there
                take = jnp.where(match, 1.0, 0.0).astype(BF)
                wts[i * LANES : (i + 1) * LANES, start:stop] = dot(take, raw[:, : stop - start], 1, 0).astype(BF)
    extra = wts[:, 4 * width :]
    nrm[0:4, :] = norm_rows(extra, narrows)
    wc_buf[...] = jnp.where(lane < narrows, extra.astype(F32), 0).astype(BF)

    def forward(mb, hooks):
        def project(i, _):
            at = pl.ds(i * ROWS, ROWS)
            xhat, _ = norm_stats(pick(tok_ref, mb, at))
            al = (xhat * nrm[0:1, :] + nrm[1:2, :]).astype(BF)
            qkv_buf[mb, at, :] = dot(al, wq[...], 1, 0).astype(BF)
            return 0

        lax.fori_loop(0, blocks, project, 0)
        lse_col[...] = jnp.zeros_like(lse_col)
        keep = lax.broadcasted_iota(jnp.int32, (ROWS, ROWS), 1) <= lax.broadcasted_iota(jnp.int32, (ROWS, ROWS), 0)
        for i in range(blocks):
            keys = (i + 1) * ROWS
            at = pl.ds(i * ROWS, ROWS)

            def pair(hp, _, i=i, keys=keys, at=at):
                lanes = pl.ds(pl.multiple_of(hp * LANES, LANES), LANES)
                klanes = pl.ds(pl.multiple_of(hp * LANES + width, LANES), LANES)
                vlanes = pl.ds(pl.multiple_of(hp * LANES + 2 * width, LANES), LANES)
                q = qkv_buf[mb, at, lanes]
                k = qkv_buf[mb, pl.ds(0, keys), klanes]
                v = qkv_buf[mb, pl.ds(0, keys), vlanes]
                acc = None
                for h in range(2):
                    mine = lane // head == h
                    qm = jnp.where(mine, q * scale, 0).astype(BF)
                    vm = jnp.where(mine, v, 0).astype(BF)
                    s = dot(qm, k, 1, 1)
                    diag = jnp.where(keep, s[:, i * ROWS :], NEG_LARGE)
                    s = diag if i == 0 else jnp.concatenate([s[:, : i * ROWS], diag], axis=1)
                    m = jnp.max(s, axis=1, keepdims=True)
                    p = jnp.exp(s - m)
                    total = jnp.sum(p, axis=1, keepdims=True)
                    one = dot((p * (1.0 / total)).astype(BF), vm, 1, 0)
                    acc = one if acc is None else acc + one
                    lse_col[at, :] = jnp.where(lane == hp * 2 + h, m + jnp.log(total), lse_col[at, :])
                o_buf[mb, at, lanes] = acc.astype(BF)
                return 0

            lax.fori_loop(0, HEADS // 2, pair, 0, unroll=4)
            for hook in hooks.get(i, ()):
                hook()
        lse_buf[mb] = jnp.transpose(lse_col[...])[:HEADS, :]

        def finish(i, _):
            at = pl.ds(i * ROWS, ROWS)
            hidden = pick(tok_ref, mb, at) + dot(o_buf[mb, at, :], wo[...], 1, 0)
            xhat, _ = norm_stats(hidden)
            uc[mb, 0, at, :] = (xhat * nrm[2:3, :] + nrm[3:4, :]).astype(BF)
            return 0

        lax.fori_loop(0, blocks, finish, 0)

    def cells():
        across = lax.broadcasted_iota(jnp.int32, (LANES, narrows * 16), 1)
        lanes_of = jnp.where(lax.broadcasted_iota(jnp.int32, across.shape, 0) == across // 16, 1.0, 0.0).astype(BF)
        square = (narrows * 16, narrows * 16)
        same = lax.rem(lax.broadcasted_iota(jnp.int32, square, 0), 16) == lax.rem(
            lax.broadcasted_iota(jnp.int32, square, 1), 16)
        return lanes_of, same

    def two_parts(value):
        high = value.astype(BF)
        return high, (value - high.astype(F32)).astype(BF)

    def spread_weights(weights):
        lanes_of, same = cells()
        return [jnp.where(same, dot(w, lanes_of, 1, 0), 0.0).astype(BF) for w in two_parts(weights)]

    def mix(mb):
        if mb > 0:
            sent(XD, mb - 1, xd_out.at[0])

        def logits(n, _):
            received(U, mb, n, in_buf.at[mb, n, 0])
            received(CF, mb, n, in_buf.at[mb, n, 1])
            w_buf[mb, n] = dot(in_buf[mb, n, 0], wc_buf[...], 1, 0).astype(BF).astype(F32)
            return 0

        lax.fori_loop(0, narrows, logits, 0)

        def rows_of(c, _):
            at = pl.ds(c * 16, 16)
            logit = [
                jnp.where(live_ref[mb, pl.ds(n, 1), :] > 0, w_buf[mb, n, at, :], NEG_LARGE) for n in range(narrows)
            ]
            top = functools.reduce(jnp.maximum, logit)
            exps = [jnp.exp(logit[n] - top) * live_ref[mb, pl.ds(n, 1), :] for n in range(narrows)]
            inverse = 1.0 / functools.reduce(jnp.add, exps)
            weights = [e * inverse for e in exps]
            for n in range(narrows):
                w_buf[mb, n, at, :] = weights[n]
            joined = spread_weights(jnp.concatenate(weights, axis=0))
            for which in range(2):
                values = in_buf[mb, :, which, at, :].reshape(narrows * 16, width)
                acc = sum(dot(w, values, 0, 0) for w in joined)
                xd_out[:, which, at, :] = acc.astype(BF).reshape(narrows, 16, width)
            return 0

        lax.fori_loop(0, part // 16, rows_of, 0)

    def send_mixture(mb, start, stop):
        to_some(lambda peer: send(XD, mb, xd_out.at[peer], xd_in.at[mb, me], peer), start, stop)

    def send_expert(mb, c):
        for k in range(chunk_parts):
            peer = c * chunk_parts + k
            send(YX, mb, xd_in.at[mb, peer], yx_in.at[mb, me], peer)

    def expert(mb):
        sent(U, mb, uc.at[mb, 0, pl.ds(0, part)])
        sent(CF, mb, uc.at[mb, 0, pl.ds(0, part)])
        if mb > 0:
            sent(YX, mb - 1, xd_in.at[mb - 1, 0])

        def chunk(c, _):
            c = lax.rem(me // chunk_parts + c, blocks)
            at = pl.ds(c * chunk_parts, chunk_parts)
            for k in range(chunk_parts):
                received(XD, mb, c * chunk_parts + k, xd_in.at[mb, c * chunk_parts + k])
            x = xd_in[mb, at, 0].reshape(ROWS, width)
            dy = xd_in[mb, at, 1].reshape(ROWS, width)

            def tile(j, carry):
                y, dx = carry
                up = wt_buf[:, j].reshape(width, width)
                down = wt_buf[pl.ds(j * per_shard, per_shard), pl.ds(folds, folds)].reshape(width, width)
                z = dot(x, up, 1, 0)
                zz = z * z
                t = jnp.tanh(GELU_A * (z + GELU_B * z * zz))
                ga = (0.5 * z * (1.0 + t)).astype(BF)
                slope = 0.5 * (1.0 + t) + (0.5 * GELU_A) * z * (1.0 - t * t) * (1.0 + (3.0 * GELU_B) * zz)
                y = y + dot(ga, down, 1, 0)
                dz = (dot(dy, down, 1, 1) * slope).astype(BF)
                dx = dx + dot(dz, up, 1, 1)
                g_buf[folds + j] += dot(ga, dy, 0, 0)
                g_buf[j] += dot(x, dz, 0, 0)
                return y, dx

            zero = jnp.zeros((ROWS, width), F32)
            y, dx = lax.fori_loop(0, folds, tile, (zero, zero))
            xd_in[mb, at, 0] = y.astype(BF).reshape(chunk_parts, part, width)
            xd_in[mb, at, 1] = dx.astype(BF).reshape(chunk_parts, part, width)
            send_expert(mb, c)
            return 0

        lax.fori_loop(0, blocks, chunk, 0)

    tiles = length // width

    def outputs_arrived(mb):
        to_all(lambda peer: received(YX, mb, peer, yx_in.at[mb, peer]))

    def combine(mb):
        def rows_of(c, _):
            at = pl.ds(c * 16, 16)
            joined = narrows * 16
            lanes_of, same = cells()
            u = in_buf[mb, :, 0, at, :].reshape(joined, width)
            cf = in_buf[mb, :, 1, at, :].reshape(joined, width)
            y = yx_in[mb, :, 0, at, :].reshape(joined, width)
            dx = yx_in[mb, :, 1, at, :].reshape(joined, width)
            weights = w_buf[mb, :, at, :].reshape(joined, LANES)
            spread_out = spread_weights(weights)
            products = jnp.where(same, dot(u, dx, 1, 1) + dot(cf, y, 1, 1), 0.0)
            dw = sum(dot(g, lanes_of, 1, 1) for g in two_parts(products))
            inner = jnp.sum((weights * dw).reshape(narrows, 16, LANES), axis=0, keepdims=True)
            inner = jnp.broadcast_to(inner, (narrows, 16, LANES)).reshape(joined, LANES)
            dc = (weights * (dw - inner)).astype(BF)
            du = sum(dot(w, dx, 1, 0) for w in spread_out) + dot(dc, wc_buf[...], 1, 1)
            mixed = sum(dot(w, y, 1, 0) for w in spread_out)
            dwc_ref[...] += dot(u, dc, 0, 0)
            in_buf[mb, :, 0, at, :] = du.astype(BF).reshape(narrows, 16, width)
            in_buf[mb, :, 1, at, :] = mixed.astype(BF).reshape(narrows, 16, width)
            return 0

        lax.fori_loop(0, part // 16, rows_of, 0, unroll=2)
        to_all(lambda n: send(DU, mb, in_buf.at[mb, n, 0], uc.at[mb, 0, part_rows(me)], n))

    def send_mixed(mb):
        to_all(lambda peer: send(MIX, mb, in_buf.at[mb, peer, 1], xd_in.at[0, me, mb], peer))

    per_tile = width // ROWS

    def kept(mb, what, i):
        buf, start = (h_buf, 0) if mb == 0 else (g_buf, folds)
        rows_i = pl.ds(pl.multiple_of(lax.rem(i, per_tile) * ROWS, ROWS), ROWS)
        return buf.at[start + what * tiles + i // per_tile, rows_i]

    def gradient_copies(mb):
        buf, start = (h_buf, 0) if mb == 0 else (g_buf, folds)
        return [
            pltpu.make_async_copy(
                buf.at[start + i], gt_ref.at[mb, pl.ds(i * width, width)], io_sem.at[micros + mb * tiles + i])
            for i in range(tiles)
        ]

    def row_copies(mb):
        return [pltpu.make_async_copy(o_buf.at[mb], out_ref.at[mb], io_sem.at[mb])]

    def gradients_arrived(mb):
        to_all(lambda peer: received(DU, mb, peer, uc.at[mb, 0, part_rows(peer)]))

    def backward_start(mb):

        def first(i, _):
            at = pl.ds(i * ROWS, ROWS)
            low = o_buf[mb, at, :]
            hidden = pick(tok_ref, mb, at) + dot(low, wo[...], 1, 0)
            kept(mb, 1, i)[...] = hidden
            xhat, rstd = norm_stats(hidden)
            du = uc[mb, 0, at, :].astype(F32)
            dn[2:3, :] += jnp.sum(du * xhat, axis=0, keepdims=True)
            dn[3:4, :] += jnp.sum(du, axis=0, keepdims=True)
            dh = uc[mb, 1, at, :].astype(F32) + norm_back(du, nrm[2:3, :], xhat, rstd)
            kept(mb, 0, i)[...] = dh
            uc[mb, 1, at, :] = dh.astype(BF)
            return 0

        def turn(i, _):
            at = pl.ds(i * ROWS, ROWS)
            o_buf[mb, at, :] = dot(uc[mb, 1, at, :], wo[...], 1, 1).astype(BF)
            return 0

        lax.fori_loop(0, blocks, first, 0)
        product = dot(o_buf[mb], uc[mb, 1], 0, 0)
        dwo_ref[...] = product if mb == 0 else dwo_ref[...] + product
        lax.fori_loop(0, blocks, turn, 0)

    def backward_pairs(mb, start, stop):
        keep = lax.broadcasted_iota(jnp.int32, (ROWS, ROWS), 0) <= lax.broadcasted_iota(jnp.int32, (ROWS, ROWS), 1)

        def pair(hp, _):
            lanes = pl.ds(pl.multiple_of(hp * LANES, LANES), LANES)
            klanes = pl.ds(pl.multiple_of(hp * LANES + width, LANES), LANES)
            vlanes = pl.ds(pl.multiple_of(hp * LANES + 2 * width, LANES), LANES)
            for i in range(blocks):
                keys = (i + 1) * ROWS
                at = pl.ds(i * ROWS, ROWS)
                q = qkv_buf[mb, at, lanes]
                k = qkv_buf[mb, pl.ds(0, keys), klanes]
                v = qkv_buf[mb, pl.ds(0, keys), vlanes]
                do = o_buf[mb, at, lanes]
                dq = dk = dv = None
                for h in range(2):
                    mine = lane // head == h
                    qm = jnp.where(mine, q * scale, 0).astype(BF)
                    dom = jnp.where(mine, do, 0).astype(BF)
                    km = jnp.where(mine, k * scale, 0).astype(BF)
                    s = dot(k, qm, 1, 1) - lse_buf[mb, pl.ds(hp * 2 + h, 1), at]
                    diag = jnp.where(keep, s[i * ROWS :], NEG_LARGE)
                    p = jnp.exp(diag if i == 0 else jnp.concatenate([s[: i * ROWS], diag], axis=0))
                    pdp = p * dot(v, dom, 1, 1)
                    inner = jnp.sum(pdp, axis=0, keepdims=True)
                    ds = (pdp - p * inner).astype(BF)
                    a = dot(p.astype(BF), dom, 1, 0)
                    b = dot(ds, qm, 1, 0)
                    c = dot(ds, km, 0, 0)
                    dv, dk, dq = (a, b, c) if h == 0 else (dv + a, dk + b, dq + c)
                qkv_buf[mb, at, lanes] = dq.astype(BF)
                if i:
                    dk_ref[: i * ROWS, :] += dk[: i * ROWS]
                    dv_ref[: i * ROWS, :] += dv[: i * ROWS]
                dk_ref[i * ROWS : keys, :] = dk[i * ROWS :]
                dv_ref[i * ROWS : keys, :] = dv[i * ROWS :]
            qkv_buf[mb, :, klanes] = dk_ref[...].astype(BF)
            qkv_buf[mb, :, vlanes] = dv_ref[...].astype(BF)
            return 0

        lax.fori_loop(start, stop, pair, 0)

    def backward_end(mb):
        def last(i, _):
            at = pl.ds(i * ROWS, ROWS)
            xhat, rstd = norm_stats(pick(tok_ref, mb, at))
            al = (xhat * nrm[0:1, :] + nrm[1:2, :]).astype(BF)
            uc[mb, 0, at, :] = al
            da = dot(qkv_buf[mb, at, :], wq[...], 1, 1)
            dn[0:1, :] += jnp.sum(da * xhat, axis=0, keepdims=True)
            dn[1:2, :] += jnp.sum(da, axis=0, keepdims=True)
            kept(mb, 0, i)[...] += norm_back(da, nrm[0:1, :], xhat, rstd)
            return 0

        lax.fori_loop(0, blocks, last, 0)
        for copy in gradient_copies(mb):
            copy.start()

        def outer(j, _):
            cols = pl.ds(pl.multiple_of(j * width, width), width)
            product = dot(uc[mb, 0], qkv_buf[mb, :, cols], 0, 0)
            g_buf[j] = product if mb == 0 else g_buf[j] + product
            return 0

        lax.fori_loop(0, 3, outer, 0)

    def finish_rows(mb):
        to_all(lambda peer: received(MIX, mb, peer, xd_in.at[0, peer, mb]))

        def rows_of(i, _):
            mixed = xd_in[0, pl.ds(i * chunk_parts, chunk_parts), mb].reshape(ROWS, width).astype(F32)
            o_buf[mb, pl.ds(i * ROWS, ROWS), :] = (kept(mb, 1, i)[...] + mixed).astype(BF)
            return 0

        lax.fori_loop(0, blocks, rows_of, 0)
        for copy in row_copies(mb):
            copy.start()

    def relay(hop):
        def run():
            hop_arrived(hop)
            if hop < wides - 1:
                hop_send(hop + 1)

        return run

    up_at = pl.ds(pl.multiple_of(w_id * up_rows, up_rows), up_rows)
    down_tile = folds + w_id * down_rows // width
    down_at = pl.ds(pl.multiple_of(lax.rem(w_id * down_rows, width), down_rows), down_rows)

    def own_copies():
        copies = [
            pltpu.make_async_copy(g_buf.at[j, up_at], upg_ref.at[:, pl.ds(j * width, width)], own_sem.at[1 + j])
            for j in range(folds)
        ]
        return copies + [pltpu.make_async_copy(g_buf.at[down_tile, down_at], downg_ref, own_sem.at[1 + folds])]

    relays = [relay(hop) for hop in range(1, wides - 1)]
    early = relays[: (len(relays) + 1) // 2]
    late = relays[len(early) :]
    pairs = HEADS // 2
    for mb in range(micros):
        hooks = {}
        if mb == 0:
            hooks[min(2, blocks - 1)] = early
        elif mb == 1:
            hooks[min(1, blocks - 1)] = late + [lambda: mix(0), lambda: send_mixture(0, 0, narrows)]
        forward(mb, hooks)
        send_rows(U, mb)
    hop_arrived(wides - 1)
    g_buf[...] = jnp.zeros_like(g_buf)
    dn[...] = jnp.zeros_like(dn)
    expert(0)
    mix(1)
    outputs_arrived(0)
    send_mixture(1, 0, half)
    combine(0)
    gradients_arrived(0)
    send_mixture(1, half, narrows)
    backward_start(0)
    backward_pairs(0, 0, 1)
    expert(1)
    for hop in range(1, wides):
        hop_sent(hop)
    for j in range(folds):
        wt_buf[:, j] = g_buf[j].astype(BF).reshape(wides, up_rows, width)
        wt_buf[j * per_shard : (j + 1) * per_shard, folds:] = (
            g_buf[folds + j].astype(BF).reshape(per_shard, folds, up_rows, width))

    def pass_on(way, i):
        part_id = wides - 1 - i if way == 0 else i
        to = w_id + 1 if way == 0 else w_id - 1
        remote(wt_buf.at[part_id], got_ref.at[way, i], rs_sem.at[way, i], rsr_sem.at[way, i], (to, me)).start()

    def taken(way, i, target):
        pltpu.make_async_copy(got_ref.at[way, i], got_ref.at[way, i], rsr_sem.at[way, i]).wait()
        copy = pltpu.make_async_copy(got_ref.at[way, i], target, own_sem.at[0])
        copy.start()
        copy.wait()

    def held(way):
        return yx_in.at[0, pl.ds(0, 2 * folds), way]

    def add_on(step):
        for way in range(2):
            far = w_id if way == 0 else wides - 1 - w_id
            i = step - far
            part_id = wides - 1 - i if way == 0 else i

            @pl.when((far >= 1) & (i >= 0) & (i < wides - 1 - far))
            def _():
                taken(way, i, held(way))
                for j in range(2 * folds):
                    wt_buf[part_id, j] = (
                        wt_buf[part_id, j].astype(F32) + yx_in[0, j, way].astype(F32)).astype(BF)
                pass_on(way, i)

    @pl.when(w_id == 0)
    def _():
        for i in range(wides - 1):
            pass_on(0, i)

    @pl.when(w_id == wides - 1)
    def _():
        for i in range(wides - 1):
            pass_on(1, i)

    owned = own_copies()
    for copy in owned:
        copy.start()
    backward_pairs(0, 1, pairs // 2 + 1)
    for copy in owned:
        copy.wait()
    outputs_arrived(1)
    combine(1)
    add_on(1)
    backward_pairs(0, pairs // 2 + 1, pairs)
    send_mixed(0)
    backward_end(0)
    send_mixed(1)
    gradients_arrived(1)
    backward_start(1)
    for step in range(2, wides - 1):
        add_on(step)
    backward_pairs(1, 0, pairs)
    backward_end(1)

    dwc_ref[...] += jnp.transpose(jnp.concatenate(
        [jnp.zeros((narrows, width), F32), dn[...], jnp.zeros((LANES - 8 - narrows, width), F32)], axis=0))
    spans = [slice(j * width, (j + 1) * width) for j in range(4)] + [slice(4 * width, 4 * width + LANES)]
    q_peers = [lax.rem(q_id + k, half) for k in range(1, half)]

    def parts(zw, zn):
        start = (zw * narrows + zn) * rows // padded * padded
        at = pl.ds(pl.multiple_of(start, padded), padded)
        return [g_buf[j, at, :] for j in range(3)] + [dwo_ref[at, :], dwc_ref[at, :]]

    sends = []
    if own_shard:
        for k in range(half):
            there = lax.rem(q_id + 1 + k, half)

            def fill(z, _, there=there):
                for j, value in enumerate(parts(z, 2 * there + 1 - parity)):
                    s1[there, z, :, spans[j]] = value.astype(BF)
                return 0

            lax.fori_loop(0, wides, fill, 0)
            copy = remote(s1.at[there], r1.at[there], c_sem.at[k], cr_sem.at[there], (w_id, core))
            copy.start()
            sends.append(copy)
        for k in range(half):
            there = lax.rem(q_id + 1 + k, half)
            pltpu.make_async_copy(r1.at[there], r1.at[there], cr_sem.at[there]).wait()
            last = k == half - 1

            sends[k].wait_send()

            def add(z, _, there=there, last=last):
                for j, value in enumerate(parts(z, 2 * there + parity)):
                    value = value + r1[there, z, :, spans[j]].astype(F32)
                    if last:
                        sum_buf[z, :, spans[j]] = value
                    else:
                        s1[there, z, :, spans[j]] = value.astype(BF)
                return 0

            lax.fori_loop(0, wides, add, 0)
            if not last:
                copy = remote(s1.at[there], r2.at[q_id], p_sem.at[k], pr_sem.at[q_id], (w_id, there * 2 + parity))
                copy.start()
                sends.append(copy)
    else:
        plain = [
            pltpu.make_async_copy(g_buf.at[j], shared_ref.at[:, pl.ds(j * width, width)], c_sem.at[j])
            for j in range(3)
        ]
        plain.append(pltpu.make_async_copy(dwo_ref, shared_ref.at[:, pl.ds(3 * width, width)], c_sem.at[3]))
        plain.append(pltpu.make_async_copy(dwc_ref, shared_ref.at[:, pl.ds(4 * width, LANES)], c_sem.at[4]))
        for copy in plain:
            copy.start()
        for copy in plain:
            copy.wait()

    for mb in range(micros):
        finish_rows(mb)
    for copy in gradient_copies(0):
        copy.wait()

    for way in range(2):
        far = w_id if way == 0 else wides - 1 - w_id

        @pl.when(far > 0)
        def _():
            taken(way, wides - 1 - far, held(way))

        @pl.when(far == 0)
        def _():
            for j in range(2 * folds):
                yx_in[0, j, way] = jnp.zeros((up_rows, width), BF)

    sq_buf[...] = jnp.zeros_like(sq_buf)
    mine_up = [h_buf.at[0, pl.ds(j * up_rows, up_rows)] for j in range(folds)]
    mine_down = h_buf.at[1, pl.ds(0, down_rows)]
    back = [
        pltpu.make_async_copy(upg_ref.at[:, pl.ds(j * width, width)], mine_up[j], own_sem.at[1 + j])
        for j in range(folds)
    ]
    back.append(pltpu.make_async_copy(downg_ref, mine_down, own_sem.at[1 + folds]))
    for copy in back:
        copy.start()
    for copy in back:
        copy.wait()
    for j in range(2 * folds):
        mine = h_buf.at[j // folds, pl.ds(j % folds * up_rows, up_rows)]
        value = mine[...] + yx_in[0, j, 0].astype(F32) + yx_in[0, j, 1].astype(F32)
        mine[...] = value
        sq_buf[...] += fold_rows(value * value)
    owned = [
        pltpu.make_async_copy(mine_up[j], upg_ref.at[:, pl.ds(j * width, width)], own_sem.at[1 + j])
        for j in range(folds)
    ]
    owned.append(pltpu.make_async_copy(mine_down, downg_ref, own_sem.at[1 + folds]))
    for copy in owned:
        copy.start()

    if own_shard:
        for there in q_peers:
            pltpu.make_async_copy(r2.at[there], r2.at[there], pr_sem.at[there]).wait()
        for k in range(wides):
            z = lax.rem(w_id + 1 + k, wides)
            acc = sum_buf[z]
            for there in q_peers:
                acc = acc + r2[there, z].astype(F32)
            if k < wides - 1:
                s3[z] = acc.astype(BF)
                copy = remote(s3.at[z], r3.at[w_id], z_sem.at[k], zr_sem.at[w_id], (z, me))
                copy.start()
                sends.append(copy)
            else:
                shared_ref[...] = acc
        for z in z_peers:
            pltpu.make_async_copy(r3.at[z], r3.at[z], zr_sem.at[z]).wait()
            shared_ref[...] += r3[z].astype(F32)

        value = shared_ref[...]
        sq_buf[...] += fold_rows(value * value)
        n_peers = [lax.rem(me + k, narrows) for k in range(1, narrows)]
        for k, p in enumerate(n_peers):
            copy = remote(sq_buf, sq_n.at[me], sn_sem.at[k], snr_sem.at[me], (w_id, p))
            copy.start()
            sends.append(copy)
    for copy in gradient_copies(1) + row_copies(0) + row_copies(1) + owned:
        copy.wait()
    for copy in gather_sends:
        copy.wait_send()
    for i in range(wides - 1):
        for way in range(2):
            far = w_id if way == 0 else wides - 1 - w_id

            @pl.when(i < wides - 1 - far)
            def _():
                pltpu.make_async_copy(wt_buf.at[0], wt_buf.at[0], rs_sem.at[way, i]).wait()
    sent(XD, micros - 1, xd_out.at[0])
    sent(YX, micros - 1, xd_in.at[micros - 1, 0])
    for mb in range(micros):
        sent(DU, mb, in_buf.at[mb, 0, 0])
        sent(MIX, mb, in_buf.at[mb, 0, 0])
    if own_shard:
        sq_n[me] = sq_buf[...]
        for p in n_peers:
            pltpu.make_async_copy(sq_n.at[p], sq_n.at[p], snr_sem.at[p]).wait()
        acc = sq_n[0]
        for k in range(1, narrows):
            acc = acc + sq_n[k]
        sq_w[w_id] = acc
        for k, z in enumerate(z_peers):
            copy = remote(sq_w.at[w_id], sq_w.at[w_id], sw_sem.at[k], swr_sem.at[w_id], (z, me))
            copy.start()
            sends.append(copy)
        for z in z_peers:
            pltpu.make_async_copy(sq_w.at[z], sq_w.at[z], swr_sem.at[z]).wait()
        acc = sq_w[0]
        for k in range(1, wides):
            acc = acc + sq_w[k]
        total_ref[...] = acc
    else:
        total_ref[...] = sq_buf[...]
    for copy in sends[half:]:
        copy.wait_send()


def run_block(counts, assign, tokens, cot, shard, up, down, wides, narrows, rows):
    micros, length, width = tokens.shape
    part = length // narrows
    hidden_width = up.shape[1]
    folds = hidden_width // width
    devices = wides * narrows
    hbm = pl.BlockSpec(memory_space=pl.ANY)
    vmem = pl.BlockSpec(memory_space=pltpu.VMEM)
    pairs = pltpu.VMEM((micros, narrows, 2, part, width), BF)
    pairs_one = pltpu.VMEM((narrows, 2, part, width), BF)
    sems = pltpu.SemaphoreType.DMA
    half = narrows // 2
    cols = 4 * width + LANES
    padded = max(rows, 16)
    shard_shape = (padded, cols) if rows == padded else shard[0].shape
    raw_shape = (16, LANES) if rows == padded else (devices * padded, shard_shape[1])
    block = (half, wides, padded, cols) if rows == padded else (1, 1, 16, LANES)
    return pl.pallas_call(
        functools.partial(block_kernel, wides, narrows, rows),
        out_shape=[
            jax.ShapeDtypeStruct((micros, length, width), F32),
            jax.ShapeDtypeStruct((micros, length, width), BF),
            jax.ShapeDtypeStruct((padded if rows == padded else width, cols), F32),
            jax.ShapeDtypeStruct(up.shape, F32),
            jax.ShapeDtypeStruct(down.shape, F32),
            jax.ShapeDtypeStruct((8, LANES), F32),
            jax.ShapeDtypeStruct((2, wides - 1, 2 * folds, up.shape[0], width), BF),
        ],
        in_specs=[vmem] * 3 + [hbm] + [vmem] * len(shard) + [hbm] * 2,
        out_specs=[hbm, hbm, vmem if rows == padded else hbm, hbm, hbm, vmem, hbm],
        scratch_shapes=[
            pltpu.VMEM((8, LANES), F32),
            pltpu.VMEM((micros, narrows, LANES), F32),
            pltpu.VMEM(shard_shape, BF),
            pltpu.VMEM(raw_shape, BF),
            pltpu.VMEM((width, cols), BF),
            pltpu.VMEM((micros, 2, length, width), BF),
            pltpu.VMEM((micros, length, 3 * width), BF),
            pltpu.VMEM((micros, length, width), BF),
            pltpu.VMEM((micros, HEADS, length), F32),
            pltpu.VMEM((8, width), F32),
            pltpu.VMEM((8, width), F32),
            pairs,
            pairs_one,
            pairs,
            pairs,
            pltpu.VMEM((micros, narrows, part, LANES), F32),
            pltpu.VMEM((width, LANES), BF),
            pltpu.VMEM((wides, 2 * folds, up.shape[0], width), BF),
            pltpu.VMEM((2 * folds, width, width), F32),
            pltpu.VMEM((2 * (length // width), width, width), F32),
            pltpu.VMEM((length, LANES), F32),
            pltpu.VMEM((length, LANES), F32),
            pltpu.VMEM((width, width), F32),
            pltpu.VMEM((width, LANES), F32),
            pltpu.VMEM(block, BF),
            pltpu.VMEM(block, BF),
            pltpu.VMEM(block, BF),
            pltpu.VMEM(block[1:], BF),
            pltpu.VMEM(block[1:], BF),
            pltpu.VMEM(block[1:], F32),
            pltpu.VMEM((8, LANES), F32),
            pltpu.VMEM((narrows, 8, LANES), F32),
            pltpu.VMEM((wides, 8, LANES), F32),
            sems((wides - 1,)),
            sems((wides, half - 1)),
            sems((wides, half)),
            sems((wides, narrows)),
            sems((wides - 1, 2)),
            sems((wides - 1, 2)),
            sems((6, micros, narrows)),
            sems((6, micros, narrows)),
            sems((2, wides - 1)),
            sems((2, wides - 1)),
            sems((2 + folds,)),
            sems((micros * (1 + length // width),)),
            sems((half,)),
            sems((half,)),
            sems((wides,)),
            sems((half,)),
            sems((half,)),
            sems((wides,)),
            sems((narrows - 1,)),
            sems((narrows,)),
            sems((wides - 1,)),
            sems((wides,)),
        ],
        compiler_params=pltpu.CompilerParams(
            collective_id=0, has_side_effects=True, vmem_limit_bytes=64 << 20),
        name="block",
    )(counts, assign, tokens, cot.reshape(micros, narrows, part, width), *shard, up, down)


def adam_values(weight, first_state, second_state, gradient, factor, rate, decay):
    clipped = gradient * factor
    first_new = BETA_ONE * first_state + (1.0 - BETA_ONE) * clipped
    second_new = BETA_TWO * second_state + (1.0 - BETA_TWO) * clipped * clipped
    first_hat = first_new / (1.0 - BETA_ONE**STEP)
    second_hat = second_new / (1.0 - BETA_TWO**STEP)
    weight_new = weight - rate * (first_hat / (jnp.sqrt(second_hat) + ADAM_EPS) + decay * weight)
    return weight_new, first_new, second_new, weight_new.astype(BF)


def final_kernel(wides, narrows, assign_ref, total_ref, shared_ref, *refs):
    states, refs = refs[:18], refs[18:]
    upg_ref, downg_ref = refs[:2]
    moved = (len(refs) - 29) // 2
    gt_in, out_in = refs[2 : 2 + moved], refs[2 + moved : 2 + 2 * moved]
    out_ref, gt_ref, norm_out = refs[2 + 2 * moved : 5 + 2 * moved]
    news = refs[5 + 2 * moved :]
    step = pl.program_id(0)
    for j in range(moved):
        gt_ref[j] = gt_in[j][0]
        out_ref[j] = out_in[j][0]
    grad_norm = jnp.sqrt(jnp.sum(jnp.sum(total_ref[...], axis=0, keepdims=True), axis=1, keepdims=True))
    factor = CLIP_NORM / jnp.maximum(grad_norm, CLIP_NORM)

    def update(k, gradient, rate, decay):
        values = [ref[0] if len(ref.shape) == 3 else ref[...] for ref in states[3 * k : 3 * k + 3]]
        for ref, value in zip(news[4 * k : 4 * k + 4], adam_values(*values, gradient, factor, rate, decay)):
            if len(ref.shape) == 3:
                ref[0] = value
            else:
                ref[...] = value

    @pl.when(step == 0)
    def _():
        norm_out[...] = grad_norm
        width = states[6].shape[1]
        extra = shared_ref[:, 4 * width :]
        chosen = lax.broadcasted_iota(jnp.int32, (narrows + 8, LANES), 0) == lax.broadcasted_iota(
            jnp.int32, (narrows + 8, LANES), 1)
        turned = lax.dot_general(
            jnp.where(chosen, 1.0, 0.0), extra, (((1,), (1,)), ((), ())), precision=lax.Precision.HIGHEST,
            preferred_element_type=F32)
        update(0, turned[narrows : narrows + 4], 0.3, 0.0)
        update(1, shared_ref[:, : 3 * width], 0.03, DECAY_RATE)
        update(2, shared_ref[:, 3 * width : 4 * width], 0.2, DECAY_RATE)
        update(3, turned[:narrows], 0.015, DECAY_RATE)

    update(4, upg_ref[...], 0.1, DECAY_RATE)
    update(5, downg_ref[...], 0.1, DECAY_RATE)


def run_final(assign, total, shared, states, upg, downg, grad_rows, out_low, wides, narrows):
    steps = max(1, upg.shape[0] // 32)
    whole = lambda x: pl.BlockSpec(x.shape, lambda i, s: (0,) * len(x.shape))
    split2 = lambda x: pl.BlockSpec((x.shape[0] // steps, x.shape[1]), lambda i, s: (i, 0))
    split3 = lambda x: pl.BlockSpec((1, x.shape[1] // steps, x.shape[2]), lambda i, s: (0, i, 0))
    micros, length, width = grad_rows.shape

    def placed(j):
        def index(i, s):
            return s[lax.axis_index("wide") * narrows + lax.axis_index("narrow"), j], i, 0

        return pl.BlockSpec((1, length // steps, width), index)

    taken = [placed(j) for j in range(micros)]
    given = pl.BlockSpec((micros, length // steps, width), lambda i, s: (0, i, 0))
    spec = lambda x: split3(x) if len(x.shape) == 3 else whole(x)
    news = []
    for k in range(6):
        shape = states[3 * k].shape
        news += [jax.ShapeDtypeStruct(shape, F32)] * 3 + [jax.ShapeDtypeStruct(shape, BF)]
    one = jax.ShapeDtypeStruct((1, 1), F32)
    return pl.pallas_call(
        functools.partial(final_kernel, wides, narrows),
        grid_spec=pltpu.PrefetchScalarGridSpec(
            num_scalar_prefetch=1,
            grid=(steps,),
            in_specs=[whole(total), whole(shared)] + [spec(x) for x in states] + [split2(upg), split2(downg)] + taken * 2,
            out_specs=[given, given, whole(one)] + [spec(x) for x in news],
        ),
        out_shape=[
            jax.ShapeDtypeStruct(out_low.shape, BF), jax.ShapeDtypeStruct(grad_rows.shape, F32), one] + news,
        name="final",
    )(assign, total, shared, *states, upg, downg, *[grad_rows] * micros, *[out_low] * micros)


def per_device(tokens, cotangent, seq_counts, micro_assign, *states):
    wides, narrows = lax.axis_size("wide"), lax.axis_size("narrow")
    norm_params, project_weight, output_weight, control_weight, up_weight, down_weight = states[::3]
    rows = project_weight.shape[0]
    padded = max(rows, 16)
    if rows == padded:
        shard = (project_weight, output_weight, control_weight.T, norm_params)
    else:
        norm_turned = norm_params.T
        high = lax.reduce_precision(norm_turned, 8, 7)
        middle = lax.reduce_precision(norm_turned - high, 8, 7)
        lower = norm_turned - high - middle
        extra = jnp.concatenate([control_weight, high, middle, lower], axis=1).astype(BF)
        extra = jnp.pad(extra, ((0, 0), (0, LANES - extra.shape[1])))
        joined = jnp.concatenate([project_weight.astype(BF), output_weight.astype(BF), extra], axis=1)
        fold = padded // rows
        group = -(-(joined.shape[1] // LANES) // fold) * LANES
        joined = jnp.pad(joined, ((0, 0), (0, fold * group - joined.shape[1])))
        shard = (joined.reshape(rows, fold, group).transpose(1, 0, 2).reshape(padded, group),)
    grad_rows, out_low, shared, upg, downg, total, _ = run_block(
        seq_counts[None], micro_assign.T, tokens, cotangent, shard, up_weight[0], down_weight[0], wides, narrows, rows)
    if rows < padded:
        both = ("wide", "narrow")
        shared = lax.psum_scatter(shared, both, scatter_dimension=0, tiled=True)
        total = lax.psum(total.at[0, 0].add(jnp.sum(shared * shared)), both)
    states = states[:9] + tuple(x.T for x in states[9:12]) + states[12:]
    out_rows, grad_tokens, grad_norm, *news = run_final(
        micro_assign, total, shared, states, upg, downg, grad_rows, out_low, wides, narrows)
    news[12:16] = [x.T for x in news[12:16]]
    return (out_rows, grad_tokens, grad_norm.reshape(()), *news)


def solution(mesh):
    both = ("wide", "narrow")
    rows3, cols, rows2, expert = P(both, None, None), P(None, both), P(both, None), P("narrow", "wide", None)
    return jax.shard_map(
        per_device,
        mesh=mesh,
        in_specs=(rows3, rows3, P(), P()) + (cols,) * 3 + (rows2,) * 9 + (expert,) * 6,
        out_specs=(rows3, rows3, P()) + (cols,) * 4 + (rows2,) * 12 + (expert,) * 8,
        check_vma=False,
    )
```

```python
import functools
import math

import jax
import jax.numpy as jnp
from jax import lax
from jax.experimental import pallas as pl
from jax.experimental.pallas import tpu as pltpu
from jax.sharding import PartitionSpec as P

HEADS = 8
STEP = 5
NEG_LARGE = -1e30
NORM_EPS = 1e-05
CLIP_NORM = 0.05
BETA_ONE = 0.5
BETA_TWO = 0.5
ADAM_EPS = 1e-08
DECAY_RATE = 0.1

BF = jnp.bfloat16
F32 = jnp.float32
MESH = pl.DeviceIdType.MESH
LANES = 128
ROWS = 256
GROUPS = 4
GELU_A = math.sqrt(2.0 / math.pi)
GELU_B = 0.044715


def dot(a, b, ca, cb):
    return lax.dot_general(a, b, (((ca,), (cb,)), ((), ())), preferred_element_type=F32)


def norm_stats(v):
    centred = v - jnp.mean(v, axis=-1, keepdims=True)
    rstd = lax.rsqrt(jnp.mean(centred * centred, axis=-1, keepdims=True) + NORM_EPS)
    return centred * rstd, rstd


def norm_back(grad, gain, xhat, rstd):
    t = grad * gain
    return rstd * (t - jnp.mean(t, axis=-1, keepdims=True) - xhat * jnp.mean(t * xhat, axis=-1, keepdims=True))


def remote(src, dst, send, recv, device):
    return pltpu.make_async_remote_copy(
        src_ref=src, dst_ref=dst, send_sem=send, recv_sem=recv, device_id=device, device_id_type=MESH
    )


def greet(devices):
    barrier = pltpu.get_barrier_semaphore()
    for device in devices:
        pl.semaphore_signal(barrier, inc=1, device_id=device, device_id_type=MESH)
    pl.semaphore_wait(barrier, len(devices))


def norm_rows(extra, experts):
    turned = jnp.transpose(extra.astype(F32))
    return turned[experts : experts + 4] + turned[experts + 4 : experts + 8] + turned[experts + 8 : experts + 12]


U, CF, XD, YX, DU, MIX = range(6)


def fold_rows(value):
    acc = value[:8]
    for i in range(8, value.shape[0], 8):
        acc = acc + value[i : i + 8]
    out = acc[:, :LANES]
    for i in range(LANES, value.shape[1], LANES):
        out = out + acc[:, i : i + LANES]
    return out


def block_kernel(wides, narrows, rows, *refs):
    own_shard = rows % 16 == 0
    refs = list(refs)
    count_ref, assign_ref, tok_ref, cot_ref = refs[:4]
    shard_in = refs[4 : 8 if own_shard else 5]
    (upw_ref, downw_ref,
     gt_ref, out_ref, shared_ref, upg_ref, downg_ref, total_ref, got_ref,
     flag_ref, live_ref, shard_ref, raw, wts, uc, qkv_buf, o_buf, lse_buf, nrm, dn, in_buf, xd_out, xd_in, yx_in,
     w_buf, wc_buf, wt_buf, g_buf, h_buf, dk_ref, dv_ref, dwo_ref, dwc_ref,
     *tail) = refs[4 + len(shard_in):]
    reducers = [tail[6 * g : 6 * g + 6] for g in range(GROUPS)]
    (sq_buf, sq_n, sq_w,
     gz_sem, gp_sem, gc_sem, gr_sem, hop_sem, hopr_sem, send_sem, recv_sem, rs_sem, rsr_sem, own_sem, io_sem,
     c_sem, p_sem, z_sem, cr_sem, pr_sem, zr_sem, sn_sem, snr_sem, sw_sem, swr_sem) = tail[6 * GROUPS :]
    lse_col = dk_ref
    if own_shard:
        raw = wts
    w_id, me = lax.axis_index("wide"), lax.axis_index("narrow")
    micros, length, width = tok_ref.shape
    blocks = length // ROWS
    part = length // narrows
    head = width // HEADS
    scale = 1.0 / math.sqrt(head)
    folds = wt_buf.shape[1] // 2
    hidden_width = folds * width
    up_rows = width // wides
    down_rows = hidden_width // wides
    per_shard = width // down_rows
    chunk_parts = ROWS // part
    half = narrows // 2
    q_id, parity = me // 2, lax.rem(me, 2)
    core = me + 1 - 2 * parity
    lane = lax.broadcasted_iota(jnp.int32, (1, LANES), 1)
    padded = shard_ref.shape[0]
    wq, wo = wts.at[:, pl.ds(0, 3 * width)], wts.at[:, pl.ds(3 * width, width)]

    def part_rows(n):
        return pl.ds(pl.multiple_of(n * part, part), part)

    def pick(ref, mb, at):
        value = ref[0, at, :].astype(F32)
        for j in range(1, micros):
            chosen = flag_ref[mb * micros + j : mb * micros + j + 1, 0:1] > 0
            value = jnp.where(chosen, ref[j, at, :].astype(F32), value)
        return value

    loads = [
        pltpu.make_async_copy(
            upw_ref.at[:, pl.ds(j * width, width)], h_buf.at[0, pl.ds(j * up_rows, up_rows)], own_sem.at[1 + j])
        for j in range(folds)
    ]
    loads.append(pltpu.make_async_copy(downw_ref, h_buf.at[1, pl.ds(0, down_rows)], own_sem.at[1 + folds]))
    for j in range(micros):
        loads.append(pltpu.make_async_copy(cot_ref.at[j], yx_in.at[j, :, 0], io_sem.at[j]))
    for copy in loads:
        copy.start()
    z_peers = [lax.rem(w_id + k, wides) for k in range(1, wides)]
    p_peers = [lax.rem(q_id + k, half) * 2 + parity for k in range(1, half)]
    greet([(z, me) for z in z_peers] + [(w_id, lax.rem(me + k, narrows)) for k in range(1, narrows)])

    if own_shard:
        proj_ref, outw_ref, ctrl_ref, norm_ref = shard_in
        shard_ref[:, : 3 * width] = proj_ref[...].astype(BF)
        shard_ref[:, 3 * width : 4 * width] = outw_ref[...].astype(BF)

        def spot(count, start):
            at = lax.broadcasted_iota(jnp.int32, (count, LANES), 0) + start
            return jnp.where(at == lax.broadcasted_iota(jnp.int32, (count, LANES), 1), 1.0, 0.0).astype(BF)

        extra = dot(ctrl_ref[...].astype(BF), spot(narrows, 0), 0, 0)
        left = norm_ref[...]
        for k in range(3):
            low = left.astype(BF)
            extra = extra + dot(low, spot(4, narrows + 4 * k), 0, 0)
            left = left - low.astype(F32)
        shard_ref[:, 4 * width :] = extra.astype(BF)
    else:
        shard_ref[...] = shard_in[0][...]

    def slot(zw, zn):
        return raw.at[pl.ds(pl.multiple_of((zw * narrows + zn) * padded, padded), padded)]

    own = pltpu.make_async_copy(shard_ref, slot(w_id, me), own_sem.at[0])
    own.start()
    gather_sends = []

    def spread(src, zw, zn, sem, device):
        copy = remote(src, slot(zw, zn), sem, gr_sem.at[zw, zn], device)
        copy.start()
        gather_sends.append(copy)

    def arrived(zw, zn):
        pltpu.make_async_copy(shard_ref, slot(zw, zn), gr_sem.at[zw, zn]).wait()

    for k, z in enumerate(z_peers):
        spread(shard_ref, w_id, me, gz_sem.at[k], (z, me))
    for k, p in enumerate(p_peers):
        spread(shard_ref, w_id, me, gp_sem.at[0, k], (w_id, p))
    spread(shard_ref, w_id, me, gc_sem.at[0, 0], (w_id, core))

    for copy in loads:
        copy.wait()
    for j in range(folds):
        rows_j = slice(j * up_rows, (j + 1) * up_rows)
        wt_buf[w_id, j] = h_buf[0, rows_j, :].astype(BF)
        wt_buf[w_id, folds + j] = h_buf[1, rows_j, :].astype(BF)

    def hop_send(hop):
        @pl.when((w_id >= hop - 1) & (w_id < wides - 1))
        def _():
            source = wt_buf.at[w_id - (hop - 1)]
            remote(source, source, hop_sem.at[hop - 1, 0], hopr_sem.at[hop - 1, 0], (w_id + 1, me)).start()

        @pl.when((w_id + (hop - 1) <= wides - 1) & (w_id > 0))
        def _():
            source = wt_buf.at[w_id + (hop - 1)]
            remote(source, source, hop_sem.at[hop - 1, 1], hopr_sem.at[hop - 1, 1], (w_id - 1, me)).start()

    def hop_arrived(hop):
        @pl.when(w_id >= hop)
        def _():
            pltpu.make_async_copy(wt_buf.at[0], wt_buf.at[w_id - hop], hopr_sem.at[hop - 1, 0]).wait()

        @pl.when(w_id + hop <= wides - 1)
        def _():
            pltpu.make_async_copy(wt_buf.at[0], wt_buf.at[w_id + hop], hopr_sem.at[hop - 1, 1]).wait()

    def hop_sent(hop):
        @pl.when((w_id >= hop - 1) & (w_id < wides - 1))
        def _():
            pltpu.make_async_copy(wt_buf.at[0], wt_buf.at[0], hop_sem.at[hop - 1, 0]).wait()

        @pl.when((w_id + (hop - 1) <= wides - 1) & (w_id > 0))
        def _():
            pltpu.make_async_copy(wt_buf.at[0], wt_buf.at[0], hop_sem.at[hop - 1, 1]).wait()

    for j in range(1, wides):
        zw = lax.rem(w_id + wides - j, wides)
        arrived(zw, me)
        for k, p in enumerate(p_peers):
            spread(slot(zw, me), zw, me, gp_sem.at[j, k], (w_id, p))
        spread(slot(zw, me), zw, me, gc_sem.at[j, 0], (w_id, core))
    hop_send(1)

    def choose(n, _):
        for mb in range(micros):
            value = yx_in[0, n, 0].astype(F32)
            for j in range(1, micros):
                chosen = flag_ref[mb * micros + j : mb * micros + j + 1, 0:1] > 0
                value = jnp.where(chosen, yx_in[j, n, 0].astype(F32), value)
            uc[mb, 1, part_rows(n), :] = value.astype(BF)
        return 0

    across = lax.broadcasted_iota(jnp.int32, count_ref.shape, 1)

    def spread_out(row, index):
        one = jnp.sum(jnp.where(across == index, row, 0.0), axis=1, keepdims=True)
        return jnp.broadcast_to(one, (1, LANES))

    for mb in range(micros):
        place = sum(jnp.where(assign_ref[j : j + 1, :] == mb, j, 0) for j in range(micros))
        alive = jnp.where(place < count_ref[...], 1.0, 0.0)
        for n in range(narrows):
            live_ref[mb, n : n + 1, :] = spread_out(alive, w_id * narrows + n)
        for j in range(micros):
            chosen = jnp.where(assign_ref[j : j + 1, :] == mb, 1.0, 0.0)
            flag_ref[mb * micros + j : mb * micros + j + 1, :] = spread_out(chosen, w_id * narrows + me)
    lax.fori_loop(0, narrows, choose, 0)
    dwc_ref[...] = jnp.zeros_like(dwc_ref)
    for i in range(1, half):
        zn = lax.rem(q_id + half - i, half) * 2 + parity
        for j in range(wides):
            zw = lax.rem(w_id + wides - j, wides)
            arrived(zw, zn)
            spread(slot(zw, zn), zw, zn, gc_sem.at[j, i], (w_id, core))

    def send(stage, mb, source, target, peer):
        @pl.when(peer != me)
        def _():
            remote(source, target, send_sem.at[stage, mb, peer], recv_sem.at[stage, mb, me], (w_id, peer)).start()

        @pl.when(peer == me)
        def _():
            pltpu.make_async_copy(source, target, recv_sem.at[stage, mb, me]).start()

    def received(stage, mb, peer, target):
        pltpu.make_async_copy(target, target, recv_sem.at[stage, mb, peer]).wait()

    def sent(stage, mb, source):
        def one(k, _):
            peer = lax.rem(me + k, narrows)
            pltpu.make_async_copy(source, source, send_sem.at[stage, mb, peer]).wait()
            return 0

        lax.fori_loop(1, narrows, one, 0)

    def to_some(body, start, stop):
        def one(k, _):
            body(lax.rem(q_id + lax.rem(k, half), half) * 2 + lax.rem(parity + k // half, 2))
            return 0

        lax.fori_loop(start, stop, one, 0)

    def to_all(body):
        to_some(body, 0, narrows)

    def send_rows(which, mb):
        to_all(lambda peer: send(
            which, mb, uc.at[mb, which, part_rows(peer)], in_buf.at[mb, me, which], peer))

    for mb in range(micros):
        send_rows(CF, mb)
    for i in range(half):
        for j in range(wides):
            arrived(j, 2 * i + 1 - parity)
    own.wait()

    if not own_shard:
        fold, group = padded // rows, raw.shape[1]
        for f in range(fold):
            start, stop = f * group, min((f + 1) * group, wts.shape[1])
            if start >= stop:
                break
            for i in range(width // LANES):
                here = lax.broadcasted_iota(jnp.int32, (LANES, raw.shape[0]), 0) + i * LANES
                there = lax.broadcasted_iota(jnp.int32, (LANES, raw.shape[0]), 1)
                match = (here // rows) * padded + f * rows + lax.rem(here, rows) == there
                take = jnp.where(match, 1.0, 0.0).astype(BF)
                wts[i * LANES : (i + 1) * LANES, start:stop] = dot(take, raw[:, : stop - start], 1, 0).astype(BF)
    extra = wts[:, 4 * width :]
    nrm[0:4, :] = norm_rows(extra, narrows)
    wc_buf[...] = jnp.where(lane < narrows, extra.astype(F32), 0).astype(BF)

    def forward(mb, hooks):
        def project(i, _):
            at = pl.ds(i * ROWS, ROWS)
            xhat, _ = norm_stats(pick(tok_ref, mb, at))
            al = (xhat * nrm[0:1, :] + nrm[1:2, :]).astype(BF)
            qkv_buf[mb, at, :] = dot(al, wq[...], 1, 0).astype(BF)
            return 0

        lax.fori_loop(0, blocks, project, 0)
        lse_col[...] = jnp.zeros_like(lse_col)
        keep = lax.broadcasted_iota(jnp.int32, (ROWS, ROWS), 1) <= lax.broadcasted_iota(jnp.int32, (ROWS, ROWS), 0)
        for i in range(blocks):
            keys = (i + 1) * ROWS
            at = pl.ds(i * ROWS, ROWS)

            def pair(hp, _, i=i, keys=keys, at=at):
                lanes = pl.ds(pl.multiple_of(hp * LANES, LANES), LANES)
                klanes = pl.ds(pl.multiple_of(hp * LANES + width, LANES), LANES)
                vlanes = pl.ds(pl.multiple_of(hp * LANES + 2 * width, LANES), LANES)
                q = qkv_buf[mb, at, lanes]
                k = qkv_buf[mb, pl.ds(0, keys), klanes]
                v = qkv_buf[mb, pl.ds(0, keys), vlanes]
                acc = None
                for h in range(2):
                    mine = lane // head == h
                    qm = jnp.where(mine, q * scale, 0).astype(BF)
                    vm = jnp.where(mine, v, 0).astype(BF)
                    s = dot(qm, k, 1, 1)
                    diag = jnp.where(keep, s[:, i * ROWS :], NEG_LARGE)
                    s = diag if i == 0 else jnp.concatenate([s[:, : i * ROWS], diag], axis=1)
                    m = jnp.max(s, axis=1, keepdims=True)
                    p = jnp.exp(s - m)
                    total = jnp.sum(p, axis=1, keepdims=True)
                    one = dot((p * (1.0 / total)).astype(BF), vm, 1, 0)
                    acc = one if acc is None else acc + one
                    lse_col[at, :] = jnp.where(lane == hp * 2 + h, m + jnp.log(total), lse_col[at, :])
                o_buf[mb, at, lanes] = acc.astype(BF)
                return 0

            lax.fori_loop(0, HEADS // 2, pair, 0, unroll=4)
            for hook in hooks.get(i, ()):
                hook()
        lse_buf[mb] = jnp.transpose(lse_col[...])[:HEADS, :]

        def finish(i, _):
            at = pl.ds(i * ROWS, ROWS)
            hidden = pick(tok_ref, mb, at) + dot(o_buf[mb, at, :], wo[...], 1, 0)
            xhat, _ = norm_stats(hidden)
            uc[mb, 0, at, :] = (xhat * nrm[2:3, :] + nrm[3:4, :]).astype(BF)
            return 0

        lax.fori_loop(0, blocks, finish, 0)

    def cells():
        across = lax.broadcasted_iota(jnp.int32, (LANES, narrows * 16), 1)
        lanes_of = jnp.where(lax.broadcasted_iota(jnp.int32, across.shape, 0) == across // 16, 1.0, 0.0).astype(BF)
        square = (narrows * 16, narrows * 16)
        same = lax.rem(lax.broadcasted_iota(jnp.int32, square, 0), 16) == lax.rem(
            lax.broadcasted_iota(jnp.int32, square, 1), 16)
        return lanes_of, same

    def two_parts(value):
        high = value.astype(BF)
        return high, (value - high.astype(F32)).astype(BF)

    def spread_weights(weights):
        lanes_of, same = cells()
        return [jnp.where(same, dot(w, lanes_of, 1, 0), 0.0).astype(BF) for w in two_parts(weights)]

    def mix(mb):
        if mb > 0:
            sent(XD, mb - 1, xd_out.at[0])

        def logits(n, _):
            received(U, mb, n, in_buf.at[mb, n, 0])
            received(CF, mb, n, in_buf.at[mb, n, 1])
            w_buf[mb, n] = dot(in_buf[mb, n, 0], wc_buf[...], 1, 0).astype(BF).astype(F32)
            return 0

        lax.fori_loop(0, narrows, logits, 0)

        def rows_of(c, _):
            at = pl.ds(c * 16, 16)
            logit = [
                jnp.where(live_ref[mb, pl.ds(n, 1), :] > 0, w_buf[mb, n, at, :], NEG_LARGE) for n in range(narrows)
            ]
            top = functools.reduce(jnp.maximum, logit)
            exps = [jnp.exp(logit[n] - top) * live_ref[mb, pl.ds(n, 1), :] for n in range(narrows)]
            inverse = 1.0 / functools.reduce(jnp.add, exps)
            weights = [e * inverse for e in exps]
            for n in range(narrows):
                w_buf[mb, n, at, :] = weights[n]
            joined = spread_weights(jnp.concatenate(weights, axis=0))
            for which in range(2):
                values = in_buf[mb, :, which, at, :].reshape(narrows * 16, width)
                acc = sum(dot(w, values, 0, 0) for w in joined)
                xd_out[:, which, at, :] = acc.astype(BF).reshape(narrows, 16, width)
            return 0

        lax.fori_loop(0, part // 16, rows_of, 0)

    def send_mixture(mb, start, stop):
        to_some(lambda peer: send(XD, mb, xd_out.at[peer], xd_in.at[mb, me], peer), start, stop)

    def send_expert(mb, c):
        for k in range(chunk_parts):
            peer = c * chunk_parts + k
            send(YX, mb, xd_in.at[mb, peer], yx_in.at[mb, me], peer)

    def expert(mb):
        sent(U, mb, uc.at[mb, 0, pl.ds(0, part)])
        sent(CF, mb, uc.at[mb, 0, pl.ds(0, part)])
        if mb > 0:
            sent(YX, mb - 1, xd_in.at[mb - 1, 0])

        def chunk(c, _):
            c = lax.rem(me // chunk_parts + c, blocks)
            at = pl.ds(c * chunk_parts, chunk_parts)
            for k in range(chunk_parts):
                received(XD, mb, c * chunk_parts + k, xd_in.at[mb, c * chunk_parts + k])
            x = xd_in[mb, at, 0].reshape(ROWS, width)
            dy = xd_in[mb, at, 1].reshape(ROWS, width)

            def tile(j, carry):
                y, dx = carry
                up = wt_buf[:, j].reshape(width, width)
                down = wt_buf[pl.ds(j * per_shard, per_shard), pl.ds(folds, folds)].reshape(width, width)
                z = dot(x, up, 1, 0)
                zz = z * z
                t = jnp.tanh(GELU_A * (z + GELU_B * z * zz))
                ga = (0.5 * z * (1.0 + t)).astype(BF)
                slope = 0.5 * (1.0 + t) + (0.5 * GELU_A) * z * (1.0 - t * t) * (1.0 + (3.0 * GELU_B) * zz)
                y = y + dot(ga, down, 1, 0)
                dz = (dot(dy, down, 1, 1) * slope).astype(BF)
                dx = dx + dot(dz, up, 1, 1)
                g_buf[folds + j] += dot(ga, dy, 0, 0)
                g_buf[j] += dot(x, dz, 0, 0)
                return y, dx

            zero = jnp.zeros((ROWS, width), F32)
            y, dx = lax.fori_loop(0, folds, tile, (zero, zero))
            xd_in[mb, at, 0] = y.astype(BF).reshape(chunk_parts, part, width)
            xd_in[mb, at, 1] = dx.astype(BF).reshape(chunk_parts, part, width)
            send_expert(mb, c)
            return 0

        lax.fori_loop(0, blocks, chunk, 0)

    tiles = length // width

    def outputs_arrived(mb):
        to_all(lambda peer: received(YX, mb, peer, yx_in.at[mb, peer]))

    def combine(mb):
        def rows_of(c, _):
            at = pl.ds(c * 16, 16)
            joined = narrows * 16
            lanes_of, same = cells()
            u = in_buf[mb, :, 0, at, :].reshape(joined, width)
            cf = in_buf[mb, :, 1, at, :].reshape(joined, width)
            y = yx_in[mb, :, 0, at, :].reshape(joined, width)
            dx = yx_in[mb, :, 1, at, :].reshape(joined, width)
            weights = w_buf[mb, :, at, :].reshape(joined, LANES)
            spread_out = spread_weights(weights)
            products = jnp.where(same, dot(u, dx, 1, 1) + dot(cf, y, 1, 1), 0.0)
            dw = sum(dot(g, lanes_of, 1, 1) for g in two_parts(products))
            inner = jnp.sum((weights * dw).reshape(narrows, 16, LANES), axis=0, keepdims=True)
            inner = jnp.broadcast_to(inner, (narrows, 16, LANES)).reshape(joined, LANES)
            dc = (weights * (dw - inner)).astype(BF)
            du = sum(dot(w, dx, 1, 0) for w in spread_out) + dot(dc, wc_buf[...], 1, 1)
            mixed = sum(dot(w, y, 1, 0) for w in spread_out)
            dwc_ref[...] += dot(u, dc, 0, 0)
            in_buf[mb, :, 0, at, :] = du.astype(BF).reshape(narrows, 16, width)
            in_buf[mb, :, 1, at, :] = mixed.astype(BF).reshape(narrows, 16, width)
            return 0

        lax.fori_loop(0, part // 16, rows_of, 0, unroll=2)
        to_all(lambda n: send(DU, mb, in_buf.at[mb, n, 0], uc.at[mb, 0, part_rows(me)], n))

    def send_mixed(mb):
        to_all(lambda peer: send(MIX, mb, in_buf.at[mb, peer, 1], xd_in.at[0, me, mb], peer))

    per_tile = width // ROWS

    def kept(mb, what, i):
        buf, start = (h_buf, 0) if mb == 0 else (g_buf, folds)
        rows_i = pl.ds(pl.multiple_of(lax.rem(i, per_tile) * ROWS, ROWS), ROWS)
        return buf.at[start + what * tiles + i // per_tile, rows_i]

    def gradient_copies(mb):
        buf, start = (h_buf, 0) if mb == 0 else (g_buf, folds)
        return [
            pltpu.make_async_copy(
                buf.at[start + i], gt_ref.at[mb, pl.ds(i * width, width)], io_sem.at[micros + mb * tiles + i])
            for i in range(tiles)
        ]

    def row_copies(mb):
        return [pltpu.make_async_copy(o_buf.at[mb], out_ref.at[mb], io_sem.at[mb])]

    def gradients_arrived(mb):
        to_all(lambda peer: received(DU, mb, peer, uc.at[mb, 0, part_rows(peer)]))

    def backward_start(mb):

        def first(i, _):
            at = pl.ds(i * ROWS, ROWS)
            low = o_buf[mb, at, :]
            hidden = pick(tok_ref, mb, at) + dot(low, wo[...], 1, 0)
            kept(mb, 1, i)[...] = hidden
            xhat, rstd = norm_stats(hidden)
            du = uc[mb, 0, at, :].astype(F32)
            dn[2:3, :] += jnp.sum(du * xhat, axis=0, keepdims=True)
            dn[3:4, :] += jnp.sum(du, axis=0, keepdims=True)
            dh = uc[mb, 1, at, :].astype(F32) + norm_back(du, nrm[2:3, :], xhat, rstd)
            kept(mb, 0, i)[...] = dh
            uc[mb, 1, at, :] = dh.astype(BF)
            xhat, _ = norm_stats(pick(tok_ref, mb, at))
            uc[mb, 0, at, :] = (xhat * nrm[0:1, :] + nrm[1:2, :]).astype(BF)
            return 0

        def turn(i, _):
            at = pl.ds(i * ROWS, ROWS)
            o_buf[mb, at, :] = dot(uc[mb, 1, at, :], wo[...], 1, 1).astype(BF)
            return 0

        lax.fori_loop(0, blocks, first, 0)
        product = dot(o_buf[mb], uc[mb, 1], 0, 0)
        dwo_ref[...] = product if mb == 0 else dwo_ref[...] + product
        lax.fori_loop(0, blocks, turn, 0)

    def backward_pairs(mb, start, stop):
        keep = lax.broadcasted_iota(jnp.int32, (ROWS, ROWS), 0) <= lax.broadcasted_iota(jnp.int32, (ROWS, ROWS), 1)

        def pair(hp, _):
            lanes = pl.ds(pl.multiple_of(hp * LANES, LANES), LANES)
            klanes = pl.ds(pl.multiple_of(hp * LANES + width, LANES), LANES)
            vlanes = pl.ds(pl.multiple_of(hp * LANES + 2 * width, LANES), LANES)
            for i in range(blocks):
                keys = (i + 1) * ROWS
                at = pl.ds(i * ROWS, ROWS)
                q = qkv_buf[mb, at, lanes]
                k = qkv_buf[mb, pl.ds(0, keys), klanes]
                v = qkv_buf[mb, pl.ds(0, keys), vlanes]
                do = o_buf[mb, at, lanes]
                dq = dk = dv = None
                for h in range(2):
                    mine = lane // head == h
                    qm = jnp.where(mine, q * scale, 0).astype(BF)
                    dom = jnp.where(mine, do, 0).astype(BF)
                    km = jnp.where(mine, k * scale, 0).astype(BF)
                    s = dot(k, qm, 1, 1) - lse_buf[mb, pl.ds(hp * 2 + h, 1), at]
                    diag = jnp.where(keep, s[i * ROWS :], NEG_LARGE)
                    p = jnp.exp(diag if i == 0 else jnp.concatenate([s[: i * ROWS], diag], axis=0))
                    pdp = p * dot(v, dom, 1, 1)
                    inner = jnp.sum(pdp, axis=0, keepdims=True)
                    ds = (pdp - p * inner).astype(BF)
                    a = dot(p.astype(BF), dom, 1, 0)
                    b = dot(ds, qm, 1, 0)
                    c = dot(ds, km, 0, 0)
                    dv, dk, dq = (a, b, c) if h == 0 else (dv + a, dk + b, dq + c)
                qkv_buf[mb, at, lanes] = dq.astype(BF)
                if i:
                    dk_ref[: i * ROWS, :] += dk[: i * ROWS]
                    dv_ref[: i * ROWS, :] += dv[: i * ROWS]
                dk_ref[i * ROWS : keys, :] = dk[i * ROWS :]
                dv_ref[i * ROWS : keys, :] = dv[i * ROWS :]
            qkv_buf[mb, :, klanes] = dk_ref[...].astype(BF)
            qkv_buf[mb, :, vlanes] = dv_ref[...].astype(BF)
            return 0

        lax.fori_loop(start, stop, pair, 0)

    def backward_end(mb):
        def last(i, _):
            at = pl.ds(i * ROWS, ROWS)
            xhat, rstd = norm_stats(pick(tok_ref, mb, at))
            da = dot(qkv_buf[mb, at, :], wq[...], 1, 1)
            dn[0:1, :] += jnp.sum(da * xhat, axis=0, keepdims=True)
            dn[1:2, :] += jnp.sum(da, axis=0, keepdims=True)
            kept(mb, 0, i)[...] += norm_back(da, nrm[0:1, :], xhat, rstd)
            return 0

        lax.fori_loop(0, blocks, last, 0)
        for copy in gradient_copies(mb):
            copy.start()

    def outer_half(mb, side):
        def outer(j, _):
            cols = pl.ds(pl.multiple_of(j * width + side * (width // 2), LANES), width // 2)
            product = dot(uc[mb, 0], qkv_buf[mb, :, cols], 0, 0)
            to = slice(side * (width // 2), (side + 1) * (width // 2))
            g_buf[j, :, to] = product if mb == 0 else g_buf[j, :, to] + product
            return 0

        lax.fori_loop(0, 3, outer, 0)

    def finish_rows(mb):
        to_all(lambda peer: received(MIX, mb, peer, xd_in.at[0, peer, mb]))

        def rows_of(i, _):
            mixed = xd_in[0, pl.ds(i * chunk_parts, chunk_parts), mb].reshape(ROWS, width).astype(F32)
            o_buf[mb, pl.ds(i * ROWS, ROWS), :] = (kept(mb, 1, i)[...] + mixed).astype(BF)
            return 0

        lax.fori_loop(0, blocks, rows_of, 0)
        for copy in row_copies(mb):
            copy.start()

    q_peers = [lax.rem(q_id + k, half) for k in range(1, half)]
    side = width // 2
    groups = [
        [(dwo_ref, 0, width, 3 * width)],
        [(g_buf.at[j], 0, side, j * width) for j in range(3)],
        [(g_buf.at[j], side, side, j * width + side) for j in range(3)],
        [(dwc_ref, 0, LANES, 4 * width)],
    ]
    sends = []

    def parts(g, zw, zn):
        at = pl.ds(pl.multiple_of((zw * narrows + zn) * rows, padded), padded)
        found, start = [], 0
        for ref, col, size, _ in groups[g]:
            found.append((slice(start, start + size), ref[at, col : col + size]))
            start += size
        return found

    def to_core(g):
        if not own_shard:
            return
        s1, r1 = reducers[g][:2]
        for k in range(half):
            there = lax.rem(q_id + 1 + k, half)

            def fill(z, _, there=there):
                for cols, value in parts(g, z, 2 * there + 1 - parity):
                    s1[there, z, :, cols] = value.astype(BF)
                return 0

            lax.fori_loop(0, wides, fill, 0)
            remote(s1.at[there], r1.at[there], c_sem.at[g, k], cr_sem.at[g, there], (w_id, core)).start()

    def to_chips(g):
        if not own_shard:
            return
        s1, r1, r2, _, _, sum_buf = reducers[g]
        for k in range(half):
            there = lax.rem(q_id + 1 + k, half)
            pltpu.make_async_copy(r1.at[there], r1.at[there], cr_sem.at[g, there]).wait()
            pltpu.make_async_copy(s1.at[there], s1.at[there], c_sem.at[g, k]).wait()
            last = k == half - 1

            def add(z, _, there=there, last=last):
                for cols, value in parts(g, z, 2 * there + parity):
                    value = value + r1[there, z, :, cols].astype(F32)
                    if last:
                        sum_buf[z, :, cols] = value
                    else:
                        s1[there, z, :, cols] = value.astype(BF)
                return 0

            lax.fori_loop(0, wides, add, 0)
            if not last:
                copy = remote(
                    s1.at[there], r2.at[q_id], p_sem.at[g, k], pr_sem.at[g, q_id], (w_id, there * 2 + parity))
                copy.start()
                sends.append(copy)

    def to_planes(g):
        if not own_shard:
            return
        _, _, r2, s3, r3, sum_buf = reducers[g]
        for there in q_peers:
            pltpu.make_async_copy(r2.at[there], r2.at[there], pr_sem.at[g, there]).wait()
        for k in range(wides):
            z = lax.rem(w_id + 1 + k, wides)
            acc = sum_buf[z]
            for there in q_peers:
                acc = acc + r2[there, z].astype(F32)
            if k < wides - 1:
                s3[z] = acc.astype(BF)
                copy = remote(s3.at[z], r3.at[w_id], z_sem.at[g, k], zr_sem.at[g, w_id], (z, me))
                copy.start()
                sends.append(copy)
            else:
                sum_buf[z] = acc

    def owned_rows(g):
        _, _, _, _, r3, sum_buf = reducers[g]
        acc = sum_buf[w_id]
        for z in z_peers:
            pltpu.make_async_copy(r3.at[z], r3.at[z], zr_sem.at[g, z]).wait()
            acc = acc + r3[z].astype(F32)
        start = 0
        for _, _, size, to in groups[g]:
            shared_ref[:, to : to + size] = acc[:, start : start + size]
            start += size

    def relay(hop):
        def run():
            hop_arrived(hop)
            if hop < wides - 1:
                hop_send(hop + 1)

        return run

    up_at = pl.ds(pl.multiple_of(w_id * up_rows, up_rows), up_rows)
    down_tile = folds + w_id * down_rows // width
    down_at = pl.ds(pl.multiple_of(lax.rem(w_id * down_rows, width), down_rows), down_rows)

    def own_copies():
        copies = [
            pltpu.make_async_copy(g_buf.at[j, up_at], upg_ref.at[:, pl.ds(j * width, width)], own_sem.at[1 + j])
            for j in range(folds)
        ]
        return copies + [pltpu.make_async_copy(g_buf.at[down_tile, down_at], downg_ref, own_sem.at[1 + folds])]

    relays = [relay(hop) for hop in range(1, wides - 1)]
    early = relays[: (len(relays) + 1) // 2]
    late = relays[len(early) :]
    pairs = HEADS // 2
    for mb in range(micros):
        hooks = {}
        if mb == 0:
            hooks[min(2, blocks - 1)] = early
        elif mb == 1:
            hooks[min(1, blocks - 1)] = late + [lambda: mix(0), lambda: send_mixture(0, 0, narrows)]
        forward(mb, hooks)
        send_rows(U, mb)
    hop_arrived(wides - 1)
    g_buf[...] = jnp.zeros_like(g_buf)
    dn[...] = jnp.zeros_like(dn)
    expert(0)
    mix(1)
    outputs_arrived(0)
    send_mixture(1, 0, half)
    combine(0)
    gradients_arrived(0)
    send_mixture(1, half, narrows)
    backward_start(0)
    backward_pairs(0, 0, 1)
    expert(1)
    for hop in range(1, wides):
        hop_sent(hop)
    for j in range(folds):
        wt_buf[:, j] = g_buf[j].astype(BF).reshape(wides, up_rows, width)
        wt_buf[j * per_shard : (j + 1) * per_shard, folds:] = (
            g_buf[folds + j].astype(BF).reshape(per_shard, folds, up_rows, width))

    def pass_on(way, i):
        part_id = wides - 1 - i if way == 0 else i
        to = w_id + 1 if way == 0 else w_id - 1
        remote(wt_buf.at[part_id], got_ref.at[way, i], rs_sem.at[way, i], rsr_sem.at[way, i], (to, me)).start()

    def taken(way, i, target):
        pltpu.make_async_copy(got_ref.at[way, i], got_ref.at[way, i], rsr_sem.at[way, i]).wait()
        copy = pltpu.make_async_copy(got_ref.at[way, i], target, own_sem.at[0])
        copy.start()
        copy.wait()

    def held(way):
        return yx_in.at[0, pl.ds(0, 2 * folds), way]

    def add_on(step):
        for way in range(2):
            far = w_id if way == 0 else wides - 1 - w_id
            i = step - far
            part_id = wides - 1 - i if way == 0 else i

            @pl.when((far >= 1) & (i >= 0) & (i < wides - 1 - far))
            def _():
                taken(way, i, held(way))
                for j in range(2 * folds):
                    wt_buf[part_id, j] = (
                        wt_buf[part_id, j].astype(F32) + yx_in[0, j, way].astype(F32)).astype(BF)
                pass_on(way, i)

    @pl.when(w_id == 0)
    def _():
        for i in range(wides - 1):
            pass_on(0, i)

    @pl.when(w_id == wides - 1)
    def _():
        for i in range(wides - 1):
            pass_on(1, i)

    owned = own_copies()
    for copy in owned:
        copy.start()
    backward_pairs(0, 1, pairs // 2 + 1)
    for copy in owned:
        copy.wait()
    outputs_arrived(1)
    combine(1)
    add_on(1)
    backward_pairs(0, pairs // 2 + 1, pairs)
    send_mixed(0)
    outer_half(0, 0)
    outer_half(0, 1)
    backward_end(0)
    send_mixed(1)
    gradients_arrived(1)
    backward_start(1)
    for step in range(2, wides - 1):
        add_on(step)
    to_core(0)
    backward_pairs(1, 0, pairs // 2)
    to_chips(0)
    outer_half(1, 0)
    to_core(1)
    backward_pairs(1, pairs // 2, pairs // 2 + 1)
    to_chips(1)
    to_planes(0)
    backward_pairs(1, pairs // 2 + 1, pairs)
    outer_half(1, 1)
    to_core(2)
    to_planes(1)
    backward_end(1)

    dwc_ref[...] += jnp.transpose(jnp.concatenate(
        [jnp.zeros((narrows, width), F32), dn[...], jnp.zeros((LANES - 8 - narrows, width), F32)], axis=0))
    to_core(3)
    to_chips(2)
    to_chips(3)
    if not own_shard:
        plain = [
            pltpu.make_async_copy(g_buf.at[j], shared_ref.at[:, pl.ds(j * width, width)], c_sem.at[0, j])
            for j in range(3)
        ]
        plain.append(pltpu.make_async_copy(dwo_ref, shared_ref.at[:, pl.ds(3 * width, width)], c_sem.at[0, 3]))
        plain.append(pltpu.make_async_copy(dwc_ref, shared_ref.at[:, pl.ds(4 * width, LANES)], c_sem.at[0, 4]))
        for copy in plain:
            copy.start()
        for copy in plain:
            copy.wait()
    for mb in range(micros):
        finish_rows(mb)
    for copy in gradient_copies(0):
        copy.wait()

    for way in range(2):
        far = w_id if way == 0 else wides - 1 - w_id

        @pl.when(far > 0)
        def _():
            taken(way, wides - 1 - far, held(way))

        @pl.when(far == 0)
        def _():
            for j in range(2 * folds):
                yx_in[0, j, way] = jnp.zeros((up_rows, width), BF)

    sq_buf[...] = jnp.zeros_like(sq_buf)
    mine_up = [h_buf.at[0, pl.ds(j * up_rows, up_rows)] for j in range(folds)]
    mine_down = h_buf.at[1, pl.ds(0, down_rows)]
    back = [
        pltpu.make_async_copy(upg_ref.at[:, pl.ds(j * width, width)], mine_up[j], own_sem.at[1 + j])
        for j in range(folds)
    ]
    back.append(pltpu.make_async_copy(downg_ref, mine_down, own_sem.at[1 + folds]))
    for copy in back:
        copy.start()
    for copy in back:
        copy.wait()
    for j in range(2 * folds):
        mine = h_buf.at[j // folds, pl.ds(j % folds * up_rows, up_rows)]
        value = mine[...] + yx_in[0, j, 0].astype(F32) + yx_in[0, j, 1].astype(F32)
        mine[...] = value
        sq_buf[...] += fold_rows(value * value)
    owned = [
        pltpu.make_async_copy(mine_up[j], upg_ref.at[:, pl.ds(j * width, width)], own_sem.at[1 + j])
        for j in range(folds)
    ]
    owned.append(pltpu.make_async_copy(mine_down, downg_ref, own_sem.at[1 + folds]))
    for copy in owned:
        copy.start()

    if own_shard:
        to_planes(2)
        to_planes(3)
        for g in range(GROUPS):
            owned_rows(g)

        value = shared_ref[...]
        sq_buf[...] += fold_rows(value * value)
        n_peers = [lax.rem(me + k, narrows) for k in range(1, narrows)]
        for k, p in enumerate(n_peers):
            copy = remote(sq_buf, sq_n.at[me], sn_sem.at[k], snr_sem.at[me], (w_id, p))
            copy.start()
            sends.append(copy)
    for copy in gradient_copies(1) + row_copies(0) + row_copies(1) + owned:
        copy.wait()
    for copy in gather_sends:
        copy.wait_send()
    for i in range(wides - 1):
        for way in range(2):
            far = w_id if way == 0 else wides - 1 - w_id

            @pl.when(i < wides - 1 - far)
            def _():
                pltpu.make_async_copy(wt_buf.at[0], wt_buf.at[0], rs_sem.at[way, i]).wait()
    sent(XD, micros - 1, xd_out.at[0])
    sent(YX, micros - 1, xd_in.at[micros - 1, 0])
    for mb in range(micros):
        sent(DU, mb, in_buf.at[mb, 0, 0])
        sent(MIX, mb, in_buf.at[mb, 0, 0])
    if own_shard:
        sq_n[me] = sq_buf[...]
        for p in n_peers:
            pltpu.make_async_copy(sq_n.at[p], sq_n.at[p], snr_sem.at[p]).wait()
        acc = sq_n[0]
        for k in range(1, narrows):
            acc = acc + sq_n[k]
        sq_w[w_id] = acc
        for k, z in enumerate(z_peers):
            copy = remote(sq_w.at[w_id], sq_w.at[w_id], sw_sem.at[k], swr_sem.at[w_id], (z, me))
            copy.start()
            sends.append(copy)
        for z in z_peers:
            pltpu.make_async_copy(sq_w.at[z], sq_w.at[z], swr_sem.at[z]).wait()
        acc = sq_w[0]
        for k in range(1, wides):
            acc = acc + sq_w[k]
        total_ref[...] = acc
    else:
        total_ref[...] = sq_buf[...]
    for copy in sends:
        copy.wait_send()


def run_block(counts, assign, tokens, cot, shard, up, down, wides, narrows, rows):
    micros, length, width = tokens.shape
    part = length // narrows
    hidden_width = up.shape[1]
    folds = hidden_width // width
    devices = wides * narrows
    hbm = pl.BlockSpec(memory_space=pl.ANY)
    vmem = pl.BlockSpec(memory_space=pltpu.VMEM)
    pairs = pltpu.VMEM((micros, narrows, 2, part, width), BF)
    pairs_one = pltpu.VMEM((narrows, 2, part, width), BF)
    sems = pltpu.SemaphoreType.DMA
    half = narrows // 2
    cols = 4 * width + LANES
    padded = max(rows, 16)
    shard_shape = (padded, cols) if rows == padded else shard[0].shape
    raw_shape = (16, LANES) if rows == padded else (devices * padded, shard_shape[1])
    reducers = []
    for group_cols in (width, 3 * width // 2, 3 * width // 2, LANES):
        block = (half, wides, padded, group_cols) if rows == padded else (1, 1, 16, LANES)
        reducers += [pltpu.VMEM(block, BF)] * 3 + [pltpu.VMEM(block[1:], BF)] * 2 + [pltpu.VMEM(block[1:], F32)]
    return pl.pallas_call(
        functools.partial(block_kernel, wides, narrows, rows),
        out_shape=[
            jax.ShapeDtypeStruct((micros, length, width), F32),
            jax.ShapeDtypeStruct((micros, length, width), BF),
            jax.ShapeDtypeStruct((padded if rows == padded else width, cols), F32),
            jax.ShapeDtypeStruct(up.shape, F32),
            jax.ShapeDtypeStruct(down.shape, F32),
            jax.ShapeDtypeStruct((8, LANES), F32),
            jax.ShapeDtypeStruct((2, wides - 1, 2 * folds, up.shape[0], width), BF),
        ],
        in_specs=[vmem] * 3 + [hbm] + [vmem] * len(shard) + [hbm] * 2,
        out_specs=[hbm, hbm, vmem if rows == padded else hbm, hbm, hbm, vmem, hbm],
        scratch_shapes=[
            pltpu.VMEM((8, LANES), F32),
            pltpu.VMEM((micros, narrows, LANES), F32),
            pltpu.VMEM(shard_shape, BF),
            pltpu.VMEM(raw_shape, BF),
            pltpu.VMEM((width, cols), BF),
            pltpu.VMEM((micros, 2, length, width), BF),
            pltpu.VMEM((micros, length, 3 * width), BF),
            pltpu.VMEM((micros, length, width), BF),
            pltpu.VMEM((micros, HEADS, length), F32),
            pltpu.VMEM((8, width), F32),
            pltpu.VMEM((8, width), F32),
            pairs,
            pairs_one,
            pairs,
            pairs,
            pltpu.VMEM((micros, narrows, part, LANES), F32),
            pltpu.VMEM((width, LANES), BF),
            pltpu.VMEM((wides, 2 * folds, up.shape[0], width), BF),
            pltpu.VMEM((2 * folds, width, width), F32),
            pltpu.VMEM((2 * (length // width), width, width), F32),
            pltpu.VMEM((length, LANES), F32),
            pltpu.VMEM((length, LANES), F32),
            pltpu.VMEM((width, width), F32),
            pltpu.VMEM((width, LANES), F32),
            *reducers,
            pltpu.VMEM((8, LANES), F32),
            pltpu.VMEM((narrows, 8, LANES), F32),
            pltpu.VMEM((wides, 8, LANES), F32),
            sems((wides - 1,)),
            sems((wides, half - 1)),
            sems((wides, half)),
            sems((wides, narrows)),
            sems((wides - 1, 2)),
            sems((wides - 1, 2)),
            sems((6, micros, narrows)),
            sems((6, micros, narrows)),
            sems((2, wides - 1)),
            sems((2, wides - 1)),
            sems((2 + folds,)),
            sems((micros * (1 + length // width),)),
            sems((GROUPS, max(half, 5))),
            sems((GROUPS, half)),
            sems((GROUPS, wides)),
            sems((GROUPS, half)),
            sems((GROUPS, half)),
            sems((GROUPS, wides)),
            sems((narrows - 1,)),
            sems((narrows,)),
            sems((wides - 1,)),
            sems((wides,)),
        ],
        compiler_params=pltpu.CompilerParams(
            collective_id=0, has_side_effects=True, vmem_limit_bytes=64 << 20),
        name="block",
    )(counts, assign, tokens, cot.reshape(micros, narrows, part, width), *shard, up, down)


def adam_values(weight, first_state, second_state, gradient, factor, rate, decay):
    clipped = gradient * factor
    first_new = BETA_ONE * first_state + (1.0 - BETA_ONE) * clipped
    second_new = BETA_TWO * second_state + (1.0 - BETA_TWO) * clipped * clipped
    first_hat = first_new / (1.0 - BETA_ONE**STEP)
    second_hat = second_new / (1.0 - BETA_TWO**STEP)
    weight_new = weight - rate * (first_hat / (jnp.sqrt(second_hat) + ADAM_EPS) + decay * weight)
    return weight_new, first_new, second_new, weight_new.astype(BF)


def final_kernel(wides, narrows, assign_ref, total_ref, shared_ref, *refs):
    states, refs = refs[:18], refs[18:]
    upg_ref, downg_ref = refs[:2]
    moved = (len(refs) - 29) // 2
    gt_in, out_in = refs[2 : 2 + moved], refs[2 + moved : 2 + 2 * moved]
    out_ref, gt_ref, norm_out = refs[2 + 2 * moved : 5 + 2 * moved]
    news = refs[5 + 2 * moved :]
    step = pl.program_id(0)
    for j in range(moved):
        gt_ref[j] = gt_in[j][0]
        out_ref[j] = out_in[j][0]
    grad_norm = jnp.sqrt(jnp.sum(jnp.sum(total_ref[...], axis=0, keepdims=True), axis=1, keepdims=True))
    factor = CLIP_NORM / jnp.maximum(grad_norm, CLIP_NORM)

    def update(k, gradient, rate, decay):
        values = [ref[0] if len(ref.shape) == 3 else ref[...] for ref in states[3 * k : 3 * k + 3]]
        for ref, value in zip(news[4 * k : 4 * k + 4], adam_values(*values, gradient, factor, rate, decay)):
            if len(ref.shape) == 3:
                ref[0] = value
            else:
                ref[...] = value

    @pl.when(step == 0)
    def _():
        norm_out[...] = grad_norm
        width = states[6].shape[1]
        extra = shared_ref[:, 4 * width :]
        chosen = lax.broadcasted_iota(jnp.int32, (narrows + 8, LANES), 0) == lax.broadcasted_iota(
            jnp.int32, (narrows + 8, LANES), 1)
        turned = lax.dot_general(
            jnp.where(chosen, 1.0, 0.0), extra, (((1,), (1,)), ((), ())), precision=lax.Precision.HIGHEST,
            preferred_element_type=F32)
        update(0, turned[narrows : narrows + 4], 0.3, 0.0)
        update(1, shared_ref[:, : 3 * width], 0.03, DECAY_RATE)
        update(2, shared_ref[:, 3 * width : 4 * width], 0.2, DECAY_RATE)
        update(3, turned[:narrows], 0.015, DECAY_RATE)

    update(4, upg_ref[...], 0.1, DECAY_RATE)
    update(5, downg_ref[...], 0.1, DECAY_RATE)


def run_final(assign, total, shared, states, upg, downg, grad_rows, out_low, wides, narrows):
    steps = max(1, upg.shape[0] // 32)
    whole = lambda x: pl.BlockSpec(x.shape, lambda i, s: (0,) * len(x.shape))
    split2 = lambda x: pl.BlockSpec((x.shape[0] // steps, x.shape[1]), lambda i, s: (i, 0))
    split3 = lambda x: pl.BlockSpec((1, x.shape[1] // steps, x.shape[2]), lambda i, s: (0, i, 0))
    micros, length, width = grad_rows.shape

    def placed(j):
        def index(i, s):
            return s[j, lax.axis_index("wide") * narrows + lax.axis_index("narrow")], i, 0

        return pl.BlockSpec((1, length // steps, width), index)

    taken = [placed(j) for j in range(micros)]
    given = pl.BlockSpec((micros, length // steps, width), lambda i, s: (0, i, 0))
    spec = lambda x: split3(x) if len(x.shape) == 3 else whole(x)
    news = []
    for k in range(6):
        shape = states[3 * k].shape
        news += [jax.ShapeDtypeStruct(shape, F32)] * 3 + [jax.ShapeDtypeStruct(shape, BF)]
    one = jax.ShapeDtypeStruct((1, 1), F32)
    return pl.pallas_call(
        functools.partial(final_kernel, wides, narrows),
        grid_spec=pltpu.PrefetchScalarGridSpec(
            num_scalar_prefetch=1,
            grid=(steps,),
            in_specs=[whole(total), whole(shared)] + [spec(x) for x in states] + [split2(upg), split2(downg)] + taken * 2,
            out_specs=[given, given, whole(one)] + [spec(x) for x in news],
        ),
        out_shape=[
            jax.ShapeDtypeStruct(out_low.shape, BF), jax.ShapeDtypeStruct(grad_rows.shape, F32), one] + news,
        name="final",
    )(assign, total, shared, *states, upg, downg, *[grad_rows] * micros, *[out_low] * micros)


def per_device(tokens, cotangent, seq_counts, micro_assign, *states):
    wides, narrows = lax.axis_size("wide"), lax.axis_size("narrow")
    norm_params, project_weight, output_weight, control_weight, up_weight, down_weight = states[::3]
    rows = project_weight.shape[0]
    padded = max(rows, 16)
    if rows == padded:
        shard = (project_weight, output_weight, control_weight.T, norm_params)
    else:
        norm_turned = norm_params.T
        high = lax.reduce_precision(norm_turned, 8, 7)
        middle = lax.reduce_precision(norm_turned - high, 8, 7)
        lower = norm_turned - high - middle
        extra = jnp.concatenate([control_weight, high, middle, lower], axis=1).astype(BF)
        extra = jnp.pad(extra, ((0, 0), (0, LANES - extra.shape[1])))
        joined = jnp.concatenate([project_weight.astype(BF), output_weight.astype(BF), extra], axis=1)
        fold = padded // rows
        group = -(-(joined.shape[1] // LANES) // fold) * LANES
        joined = jnp.pad(joined, ((0, 0), (0, fold * group - joined.shape[1])))
        shard = (joined.reshape(rows, fold, group).transpose(1, 0, 2).reshape(padded, group),)
    grad_rows, out_low, shared, upg, downg, total, _ = run_block(
        seq_counts[None], micro_assign.T, tokens, cotangent, shard, up_weight[0], down_weight[0], wides, narrows, rows)
    if rows < padded:
        both = ("wide", "narrow")
        shared = lax.psum_scatter(shared, both, scatter_dimension=0, tiled=True)
        total = lax.psum(total.at[0, 0].add(jnp.sum(shared * shared)), both)
    states = states[:9] + tuple(x.T for x in states[9:12]) + states[12:]
    out_rows, grad_tokens, grad_norm, *news = run_final(
        micro_assign.T, total, shared, states, upg, downg, grad_rows, out_low, wides, narrows)
    news[12:16] = [x.T for x in news[12:16]]
    return (out_rows, grad_tokens, grad_norm.reshape(()), *news)


def solution(mesh):
    both = ("wide", "narrow")
    rows3, cols, rows2, expert = P(both, None, None), P(None, both), P(both, None), P("narrow", "wide", None)
    return jax.shard_map(
        per_device,
        mesh=mesh,
        in_specs=(rows3, rows3, P(), P()) + (cols,) * 3 + (rows2,) * 9 + (expert,) * 6,
        out_specs=(rows3, rows3, P()) + (cols,) * 4 + (rows2,) * 12 + (expert,) * 8,
        check_vma=False,
    )
```

```python
import functools
import math

import jax
import jax.numpy as jnp
from jax import lax
from jax.experimental import pallas as pl
from jax.experimental.pallas import tpu as pltpu
from jax.sharding import PartitionSpec as P

HEADS = 8
STEP = 5
NEG_LARGE = -1e30
NORM_EPS = 1e-05
CLIP_NORM = 0.05
BETA_ONE = 0.5
BETA_TWO = 0.5
ADAM_EPS = 1e-08
DECAY_RATE = 0.1

BF = jnp.bfloat16
F32 = jnp.float32
MESH = pl.DeviceIdType.MESH
LANES = 128
ROWS = 256
GROUPS = 4
GELU_A = math.sqrt(2.0 / math.pi)
GELU_B = 0.044715


def dot(a, b, ca, cb):
    return lax.dot_general(a, b, (((ca,), (cb,)), ((), ())), preferred_element_type=F32)


def norm_stats(v):
    centred = v - jnp.mean(v, axis=-1, keepdims=True)
    rstd = lax.rsqrt(jnp.mean(centred * centred, axis=-1, keepdims=True) + NORM_EPS)
    return centred * rstd, rstd


def norm_back(grad, gain, xhat, rstd):
    t = grad * gain
    return rstd * (t - jnp.mean(t, axis=-1, keepdims=True) - xhat * jnp.mean(t * xhat, axis=-1, keepdims=True))


def remote(src, dst, send, recv, device):
    return pltpu.make_async_remote_copy(
        src_ref=src, dst_ref=dst, send_sem=send, recv_sem=recv, device_id=device, device_id_type=MESH
    )


def greet(devices):
    barrier = pltpu.get_barrier_semaphore()
    for device in devices:
        pl.semaphore_signal(barrier, inc=1, device_id=device, device_id_type=MESH)
    pl.semaphore_wait(barrier, len(devices))


def norm_rows(extra, experts):
    turned = jnp.transpose(extra.astype(F32))
    return turned[experts : experts + 4] + turned[experts + 4 : experts + 8] + turned[experts + 8 : experts + 12]


U, CF, XD, YX, DU, MIX = range(6)


def fold_rows(value):
    acc = value[:8]
    for i in range(8, value.shape[0], 8):
        acc = acc + value[i : i + 8]
    out = acc[:, :LANES]
    for i in range(LANES, value.shape[1], LANES):
        out = out + acc[:, i : i + LANES]
    return out


def block_kernel(wides, narrows, rows, *refs):
    own_shard = rows % 16 == 0
    refs = list(refs)
    count_ref, assign_ref, tok_ref, cot_ref = refs[:4]
    shard_in = refs[4 : 8 if own_shard else 5]
    (upw_ref, downw_ref,
     gt_ref, out_ref, shared_ref, upg_ref, downg_ref, total_ref, got_ref,
     flag_ref, live_ref, shard_ref, raw, wts, uc, qkv_buf, o_buf, lse_buf, nrm, dn, in_buf, xd_out, xd_in, yx_in,
     w_buf, wc_buf, wt_buf, g_buf, h_buf, dk_ref, dv_ref, dwo_ref, dwc_ref,
     *tail) = refs[4 + len(shard_in):]
    reducers = [tail[6 * g : 6 * g + 6] for g in range(GROUPS)]
    (sq_buf, sq_n, sq_w,
     gz_sem, gp_sem, gc_sem, gr_sem, hop_sem, hopr_sem, send_sem, recv_sem, rs_sem, rsr_sem, own_sem, io_sem,
     c_sem, p_sem, z_sem, cr_sem, pr_sem, zr_sem, sn_sem, snr_sem, sw_sem, swr_sem) = tail[6 * GROUPS :]
    lse_col = dk_ref
    if own_shard:
        raw = wts
    w_id, me = lax.axis_index("wide"), lax.axis_index("narrow")
    micros, length, width = tok_ref.shape
    blocks = length // ROWS
    part = length // narrows
    head = width // HEADS
    scale = 1.0 / math.sqrt(head)
    folds = wt_buf.shape[1] // 2
    hidden_width = folds * width
    up_rows = width // wides
    down_rows = hidden_width // wides
    per_shard = width // down_rows
    chunk_parts = ROWS // part
    half = narrows // 2
    q_id, parity = me // 2, lax.rem(me, 2)
    core = me + 1 - 2 * parity
    lane = lax.broadcasted_iota(jnp.int32, (1, LANES), 1)
    padded = shard_ref.shape[0]
    wq, wo = wts.at[:, pl.ds(0, 3 * width)], wts.at[:, pl.ds(3 * width, width)]

    def part_rows(n):
        return pl.ds(pl.multiple_of(n * part, part), part)

    def pick(ref, mb, at):
        value = ref[0, at, :].astype(F32)
        for j in range(1, micros):
            chosen = flag_ref[mb * micros + j : mb * micros + j + 1, 0:1] > 0
            value = jnp.where(chosen, ref[j, at, :].astype(F32), value)
        return value

    loads = [
        pltpu.make_async_copy(
            upw_ref.at[:, pl.ds(j * width, width)], h_buf.at[0, pl.ds(j * up_rows, up_rows)], own_sem.at[1 + j])
        for j in range(folds)
    ]
    loads.append(pltpu.make_async_copy(downw_ref, h_buf.at[1, pl.ds(0, down_rows)], own_sem.at[1 + folds]))
    for j in range(micros):
        loads.append(pltpu.make_async_copy(cot_ref.at[j], yx_in.at[j, :, 0], io_sem.at[j]))
    for copy in loads:
        copy.start()
    z_peers = [lax.rem(w_id + k, wides) for k in range(1, wides)]
    p_peers = [lax.rem(q_id + k, half) * 2 + parity for k in range(1, half)]
    greet([(z, me) for z in z_peers] + [(w_id, lax.rem(me + k, narrows)) for k in range(1, narrows)])

    if own_shard:
        proj_ref, outw_ref, ctrl_ref, norm_ref = shard_in
        shard_ref[:, : 3 * width] = proj_ref[...].astype(BF)
        shard_ref[:, 3 * width : 4 * width] = outw_ref[...].astype(BF)

        def spot(count, start):
            at = lax.broadcasted_iota(jnp.int32, (count, LANES), 0) + start
            return jnp.where(at == lax.broadcasted_iota(jnp.int32, (count, LANES), 1), 1.0, 0.0).astype(BF)

        extra = dot(ctrl_ref[...].astype(BF), spot(narrows, 0), 0, 0)
        left = norm_ref[...]
        for k in range(3):
            low = left.astype(BF)
            extra = extra + dot(low, spot(4, narrows + 4 * k), 0, 0)
            left = left - low.astype(F32)
        shard_ref[:, 4 * width :] = extra.astype(BF)
    else:
        shard_ref[...] = shard_in[0][...]

    def slot(zw, zn):
        return raw.at[pl.ds(pl.multiple_of((zw * narrows + zn) * padded, padded), padded)]

    own = pltpu.make_async_copy(shard_ref, slot(w_id, me), own_sem.at[0])
    own.start()
    gather_sends = []

    def spread(src, zw, zn, sem, device):
        copy = remote(src, slot(zw, zn), sem, gr_sem.at[zw, zn], device)
        copy.start()
        gather_sends.append(copy)

    def arrived(zw, zn):
        pltpu.make_async_copy(shard_ref, slot(zw, zn), gr_sem.at[zw, zn]).wait()

    for k, z in enumerate(z_peers):
        spread(shard_ref, w_id, me, gz_sem.at[k], (z, me))
    for k, p in enumerate(p_peers):
        spread(shard_ref, w_id, me, gp_sem.at[0, k], (w_id, p))
    spread(shard_ref, w_id, me, gc_sem.at[0, 0], (w_id, core))

    for copy in loads:
        copy.wait()
    for j in range(folds):
        rows_j = slice(j * up_rows, (j + 1) * up_rows)
        wt_buf[w_id, j] = h_buf[0, rows_j, :].astype(BF)
        wt_buf[w_id, folds + j] = h_buf[1, rows_j, :].astype(BF)

    def hop_send(hop):
        @pl.when((w_id >= hop - 1) & (w_id < wides - 1))
        def _():
            source = wt_buf.at[w_id - (hop - 1)]
            remote(source, source, hop_sem.at[hop - 1, 0], hopr_sem.at[hop - 1, 0], (w_id + 1, me)).start()

        @pl.when((w_id + (hop - 1) <= wides - 1) & (w_id > 0))
        def _():
            source = wt_buf.at[w_id + (hop - 1)]
            remote(source, source, hop_sem.at[hop - 1, 1], hopr_sem.at[hop - 1, 1], (w_id - 1, me)).start()

    def hop_arrived(hop):
        @pl.when(w_id >= hop)
        def _():
            pltpu.make_async_copy(wt_buf.at[0], wt_buf.at[w_id - hop], hopr_sem.at[hop - 1, 0]).wait()

        @pl.when(w_id + hop <= wides - 1)
        def _():
            pltpu.make_async_copy(wt_buf.at[0], wt_buf.at[w_id + hop], hopr_sem.at[hop - 1, 1]).wait()

    def hop_sent(hop):
        @pl.when((w_id >= hop - 1) & (w_id < wides - 1))
        def _():
            pltpu.make_async_copy(wt_buf.at[0], wt_buf.at[0], hop_sem.at[hop - 1, 0]).wait()

        @pl.when((w_id + (hop - 1) <= wides - 1) & (w_id > 0))
        def _():
            pltpu.make_async_copy(wt_buf.at[0], wt_buf.at[0], hop_sem.at[hop - 1, 1]).wait()

    for j in range(1, wides):
        zw = lax.rem(w_id + wides - j, wides)
        arrived(zw, me)
        for k, p in enumerate(p_peers):
            spread(slot(zw, me), zw, me, gp_sem.at[j, k], (w_id, p))
        spread(slot(zw, me), zw, me, gc_sem.at[j, 0], (w_id, core))
    hop_send(1)

    def choose(n, _):
        for mb in range(micros):
            value = yx_in[0, n, 0].astype(F32)
            for j in range(1, micros):
                chosen = flag_ref[mb * micros + j : mb * micros + j + 1, 0:1] > 0
                value = jnp.where(chosen, yx_in[j, n, 0].astype(F32), value)
            uc[mb, 1, part_rows(n), :] = value.astype(BF)
        return 0

    across = lax.broadcasted_iota(jnp.int32, count_ref.shape, 1)

    def spread_out(row, index):
        one = jnp.sum(jnp.where(across == index, row, 0.0), axis=1, keepdims=True)
        return jnp.broadcast_to(one, (1, LANES))

    for mb in range(micros):
        place = sum(jnp.where(assign_ref[j : j + 1, :] == mb, j, 0) for j in range(micros))
        alive = jnp.where(place < count_ref[...], 1.0, 0.0)
        for n in range(narrows):
            live_ref[mb, n : n + 1, :] = spread_out(alive, w_id * narrows + n)
        for j in range(micros):
            chosen = jnp.where(assign_ref[j : j + 1, :] == mb, 1.0, 0.0)
            flag_ref[mb * micros + j : mb * micros + j + 1, :] = spread_out(chosen, w_id * narrows + me)
    lax.fori_loop(0, narrows, choose, 0)
    dwc_ref[...] = jnp.zeros_like(dwc_ref)
    for i in range(1, half):
        zn = lax.rem(q_id + half - i, half) * 2 + parity
        for j in range(wides):
            zw = lax.rem(w_id + wides - j, wides)
            arrived(zw, zn)
            spread(slot(zw, zn), zw, zn, gc_sem.at[j, i], (w_id, core))

    def send(stage, mb, source, target, peer):
        @pl.when(peer != me)
        def _():
            remote(source, target, send_sem.at[stage, mb, peer], recv_sem.at[stage, mb, me], (w_id, peer)).start()

        @pl.when(peer == me)
        def _():
            pltpu.make_async_copy(source, target, recv_sem.at[stage, mb, me]).start()

    def received(stage, mb, peer, target):
        pltpu.make_async_copy(target, target, recv_sem.at[stage, mb, peer]).wait()

    def sent(stage, mb, source):
        def one(k, _):
            peer = lax.rem(me + k, narrows)
            pltpu.make_async_copy(source, source, send_sem.at[stage, mb, peer]).wait()
            return 0

        lax.fori_loop(1, narrows, one, 0)

    def to_some(body, start, stop):
        def one(k, _):
            body(lax.rem(q_id + lax.rem(k, half), half) * 2 + lax.rem(parity + k // half, 2))
            return 0

        lax.fori_loop(start, stop, one, 0)

    def to_all(body):
        to_some(body, 0, narrows)

    def send_rows(which, mb):
        to_all(lambda peer: send(
            which, mb, uc.at[mb, which, part_rows(peer)], in_buf.at[mb, me, which], peer))

    for mb in range(micros):
        send_rows(CF, mb)
    for i in range(half):
        for j in range(wides):
            arrived(j, 2 * i + 1 - parity)
    own.wait()

    if not own_shard:
        fold, group = padded // rows, raw.shape[1]
        for f in range(fold):
            start, stop = f * group, min((f + 1) * group, wts.shape[1])
            if start >= stop:
                break
            for i in range(width // LANES):
                here = lax.broadcasted_iota(jnp.int32, (LANES, raw.shape[0]), 0) + i * LANES
                there = lax.broadcasted_iota(jnp.int32, (LANES, raw.shape[0]), 1)
                match = (here // rows) * padded + f * rows + lax.rem(here, rows) == there
                take = jnp.where(match, 1.0, 0.0).astype(BF)
                wts[i * LANES : (i + 1) * LANES, start:stop] = dot(take, raw[:, : stop - start], 1, 0).astype(BF)
    extra = wts[:, 4 * width :]
    nrm[0:4, :] = norm_rows(extra, narrows)
    wc_buf[...] = jnp.where(lane < narrows, extra.astype(F32), 0).astype(BF)

    def forward(mb, hooks):
        def project(i, _):
            at = pl.ds(i * ROWS, ROWS)
            xhat, _ = norm_stats(pick(tok_ref, mb, at))
            al = (xhat * nrm[0:1, :] + nrm[1:2, :]).astype(BF)
            qkv_buf[mb, at, :] = dot(al, wq[...], 1, 0).astype(BF)
            return 0

        lax.fori_loop(0, blocks, project, 0)
        lse_col[...] = jnp.zeros_like(lse_col)
        keep = lax.broadcasted_iota(jnp.int32, (ROWS, ROWS), 1) <= lax.broadcasted_iota(jnp.int32, (ROWS, ROWS), 0)
        for i in range(blocks):
            keys = (i + 1) * ROWS
            at = pl.ds(i * ROWS, ROWS)

            def pair(hp, _, i=i, keys=keys, at=at):
                lanes = pl.ds(pl.multiple_of(hp * LANES, LANES), LANES)
                klanes = pl.ds(pl.multiple_of(hp * LANES + width, LANES), LANES)
                vlanes = pl.ds(pl.multiple_of(hp * LANES + 2 * width, LANES), LANES)
                q = qkv_buf[mb, at, lanes]
                k = qkv_buf[mb, pl.ds(0, keys), klanes]
                v = qkv_buf[mb, pl.ds(0, keys), vlanes]
                acc = None
                for h in range(2):
                    mine = lane // head == h
                    qm = jnp.where(mine, q * scale, 0).astype(BF)
                    vm = jnp.where(mine, v, 0).astype(BF)
                    s = dot(qm, k, 1, 1)
                    diag = jnp.where(keep, s[:, i * ROWS :], NEG_LARGE)
                    s = diag if i == 0 else jnp.concatenate([s[:, : i * ROWS], diag], axis=1)
                    m = jnp.max(s, axis=1, keepdims=True)
                    p = jnp.exp(s - m)
                    total = jnp.sum(p, axis=1, keepdims=True)
                    one = dot((p * (1.0 / total)).astype(BF), vm, 1, 0)
                    acc = one if acc is None else acc + one
                    lse_col[at, :] = jnp.where(lane == hp * 2 + h, m + jnp.log(total), lse_col[at, :])
                o_buf[mb, at, lanes] = acc.astype(BF)
                return 0

            lax.fori_loop(0, HEADS // 2, pair, 0, unroll=4)
            for hook in hooks.get(i, ()):
                hook()
        lse_buf[mb] = jnp.transpose(lse_col[...])[:HEADS, :]

        def finish(i, _):
            at = pl.ds(i * ROWS, ROWS)
            hidden = pick(tok_ref, mb, at) + dot(o_buf[mb, at, :], wo[...], 1, 0)
            xhat, _ = norm_stats(hidden)
            uc[mb, 0, at, :] = (xhat * nrm[2:3, :] + nrm[3:4, :]).astype(BF)
            return 0

        lax.fori_loop(0, blocks, finish, 0)

    def cells():
        across = lax.broadcasted_iota(jnp.int32, (LANES, narrows * 16), 1)
        lanes_of = jnp.where(lax.broadcasted_iota(jnp.int32, across.shape, 0) == across // 16, 1.0, 0.0).astype(BF)
        square = (narrows * 16, narrows * 16)
        same = lax.rem(lax.broadcasted_iota(jnp.int32, square, 0), 16) == lax.rem(
            lax.broadcasted_iota(jnp.int32, square, 1), 16)
        return lanes_of, same

    def two_parts(value):
        high = value.astype(BF)
        return high, (value - high.astype(F32)).astype(BF)

    def spread_weights(weights):
        lanes_of, same = cells()
        return [jnp.where(same, dot(w, lanes_of, 1, 0), 0.0).astype(BF) for w in two_parts(weights)]

    def mix(mb):
        if mb > 0:
            sent(XD, mb - 1, xd_out.at[0])

        def logits(n, _):
            received(U, mb, n, in_buf.at[mb, n, 0])
            received(CF, mb, n, in_buf.at[mb, n, 1])
            w_buf[mb, n] = dot(in_buf[mb, n, 0], wc_buf[...], 1, 0).astype(BF).astype(F32)
            return 0

        lax.fori_loop(0, narrows, logits, 0)

        def rows_of(c, _):
            at = pl.ds(c * 16, 16)
            logit = [
                jnp.where(live_ref[mb, pl.ds(n, 1), :] > 0, w_buf[mb, n, at, :], NEG_LARGE) for n in range(narrows)
            ]
            top = functools.reduce(jnp.maximum, logit)
            exps = [jnp.exp(logit[n] - top) * live_ref[mb, pl.ds(n, 1), :] for n in range(narrows)]
            inverse = 1.0 / functools.reduce(jnp.add, exps)
            weights = [e * inverse for e in exps]
            for n in range(narrows):
                w_buf[mb, n, at, :] = weights[n]
            joined = spread_weights(jnp.concatenate(weights, axis=0))
            for which in range(2):
                values = in_buf[mb, :, which, at, :].reshape(narrows * 16, width)
                acc = sum(dot(w, values, 0, 0) for w in joined)
                xd_out[:, which, at, :] = acc.astype(BF).reshape(narrows, 16, width)
            return 0

        lax.fori_loop(0, part // 16, rows_of, 0, unroll=2)

    def send_mixture(mb, start, stop):
        to_some(lambda peer: send(XD, mb, xd_out.at[peer], xd_in.at[mb, me], peer), start, stop)

    def send_expert(mb, c):
        for k in range(chunk_parts):
            peer = c * chunk_parts + k
            send(YX, mb, xd_in.at[mb, peer], yx_in.at[mb, me], peer)

    def expert(mb):
        sent(U, mb, uc.at[mb, 0, pl.ds(0, part)])
        sent(CF, mb, uc.at[mb, 0, pl.ds(0, part)])
        if mb > 0:
            sent(YX, mb - 1, xd_in.at[mb - 1, 0])

        def chunk(c, _):
            c = lax.rem(me // chunk_parts + c, blocks)
            at = pl.ds(c * chunk_parts, chunk_parts)
            for k in range(chunk_parts):
                received(XD, mb, c * chunk_parts + k, xd_in.at[mb, c * chunk_parts + k])
            x = xd_in[mb, at, 0].reshape(ROWS, width)
            dy = xd_in[mb, at, 1].reshape(ROWS, width)

            def tile(j, carry):
                y, dx = carry
                up = wt_buf[:, j].reshape(width, width)
                down = wt_buf[pl.ds(j * per_shard, per_shard), pl.ds(folds, folds)].reshape(width, width)
                z = dot(x, up, 1, 0)
                zz = z * z
                t = jnp.tanh(GELU_A * (z + GELU_B * z * zz))
                ga = (0.5 * z * (1.0 + t)).astype(BF)
                slope = 0.5 * (1.0 + t) + (0.5 * GELU_A) * z * (1.0 - t * t) * (1.0 + (3.0 * GELU_B) * zz)
                y = y + dot(ga, down, 1, 0)
                dz = (dot(dy, down, 1, 1) * slope).astype(BF)
                dx = dx + dot(dz, up, 1, 1)
                g_buf[folds + j] += dot(ga, dy, 0, 0)
                g_buf[j] += dot(x, dz, 0, 0)
                return y, dx

            zero = jnp.zeros((ROWS, width), F32)
            y, dx = lax.fori_loop(0, folds, tile, (zero, zero))
            xd_in[mb, at, 0] = y.astype(BF).reshape(chunk_parts, part, width)
            xd_in[mb, at, 1] = dx.astype(BF).reshape(chunk_parts, part, width)
            send_expert(mb, c)
            return 0

        lax.fori_loop(0, blocks, chunk, 0)

    tiles = length // width

    def outputs_arrived(mb):
        to_all(lambda peer: received(YX, mb, peer, yx_in.at[mb, peer]))

    def combine(mb):
        def rows_of(c, _):
            at = pl.ds(c * 16, 16)
            joined = narrows * 16
            lanes_of, same = cells()
            u = in_buf[mb, :, 0, at, :].reshape(joined, width)
            cf = in_buf[mb, :, 1, at, :].reshape(joined, width)
            y = yx_in[mb, :, 0, at, :].reshape(joined, width)
            dx = yx_in[mb, :, 1, at, :].reshape(joined, width)
            weights = w_buf[mb, :, at, :].reshape(joined, LANES)
            spread_out = spread_weights(weights)
            products = jnp.where(same, dot(u, dx, 1, 1) + dot(cf, y, 1, 1), 0.0)
            dw = sum(dot(g, lanes_of, 1, 1) for g in two_parts(products))
            inner = jnp.sum((weights * dw).reshape(narrows, 16, LANES), axis=0, keepdims=True)
            inner = jnp.broadcast_to(inner, (narrows, 16, LANES)).reshape(joined, LANES)
            dc = (weights * (dw - inner)).astype(BF)
            du = sum(dot(w, dx, 1, 0) for w in spread_out) + dot(dc, wc_buf[...], 1, 1)
            mixed = sum(dot(w, y, 1, 0) for w in spread_out)
            dwc_ref[...] += dot(u, dc, 0, 0)
            in_buf[mb, :, 0, at, :] = du.astype(BF).reshape(narrows, 16, width)
            in_buf[mb, :, 1, at, :] = mixed.astype(BF).reshape(narrows, 16, width)
            return 0

        lax.fori_loop(0, part // 16, rows_of, 0, unroll=4)
        to_all(lambda n: send(DU, mb, in_buf.at[mb, n, 0], uc.at[mb, 0, part_rows(me)], n))

    def send_mixed(mb):
        to_all(lambda peer: send(MIX, mb, in_buf.at[mb, peer, 1], xd_in.at[0, me, mb], peer))

    per_tile = width // ROWS

    def kept(mb, what, i):
        buf, start = (h_buf, 0) if mb == 0 else (g_buf, folds)
        rows_i = pl.ds(pl.multiple_of(lax.rem(i, per_tile) * ROWS, ROWS), ROWS)
        return buf.at[start + what * tiles + i // per_tile, rows_i]

    def gradient_copies(mb):
        buf, start = (h_buf, 0) if mb == 0 else (g_buf, folds)
        return [
            pltpu.make_async_copy(
                buf.at[start + i], gt_ref.at[mb, pl.ds(i * width, width)], io_sem.at[micros + mb * tiles + i])
            for i in range(tiles)
        ]

    def row_copies(mb):
        return [pltpu.make_async_copy(o_buf.at[mb], out_ref.at[mb], io_sem.at[mb])]

    def gradients_arrived(mb):
        to_all(lambda peer: received(DU, mb, peer, uc.at[mb, 0, part_rows(peer)]))

    def backward_start(mb):

        def first(i, _):
            at = pl.ds(i * ROWS, ROWS)
            low = o_buf[mb, at, :]
            hidden = pick(tok_ref, mb, at) + dot(low, wo[...], 1, 0)
            kept(mb, 1, i)[...] = hidden
            xhat, rstd = norm_stats(hidden)
            du = uc[mb, 0, at, :].astype(F32)
            dn[2:3, :] += jnp.sum(du * xhat, axis=0, keepdims=True)
            dn[3:4, :] += jnp.sum(du, axis=0, keepdims=True)
            dh = uc[mb, 1, at, :].astype(F32) + norm_back(du, nrm[2:3, :], xhat, rstd)
            kept(mb, 0, i)[...] = dh
            uc[mb, 1, at, :] = dh.astype(BF)
            xhat, _ = norm_stats(pick(tok_ref, mb, at))
            uc[mb, 0, at, :] = (xhat * nrm[0:1, :] + nrm[1:2, :]).astype(BF)
            return 0

        def turn(i, _):
            at = pl.ds(i * ROWS, ROWS)
            o_buf[mb, at, :] = dot(uc[mb, 1, at, :], wo[...], 1, 1).astype(BF)
            return 0

        lax.fori_loop(0, blocks, first, 0)
        product = dot(o_buf[mb], uc[mb, 1], 0, 0)
        dwo_ref[...] = product if mb == 0 else dwo_ref[...] + product
        lax.fori_loop(0, blocks, turn, 0)

    def backward_pairs(mb, start, stop):
        keep = lax.broadcasted_iota(jnp.int32, (ROWS, ROWS), 0) <= lax.broadcasted_iota(jnp.int32, (ROWS, ROWS), 1)

        def pair(hp, _):
            lanes = pl.ds(pl.multiple_of(hp * LANES, LANES), LANES)
            klanes = pl.ds(pl.multiple_of(hp * LANES + width, LANES), LANES)
            vlanes = pl.ds(pl.multiple_of(hp * LANES + 2 * width, LANES), LANES)
            for i in range(blocks):
                keys = (i + 1) * ROWS
                at = pl.ds(i * ROWS, ROWS)
                q = qkv_buf[mb, at, lanes]
                k = qkv_buf[mb, pl.ds(0, keys), klanes]
                v = qkv_buf[mb, pl.ds(0, keys), vlanes]
                do = o_buf[mb, at, lanes]
                dq = dk = dv = None
                for h in range(2):
                    mine = lane // head == h
                    qm = jnp.where(mine, q * scale, 0).astype(BF)
                    dom = jnp.where(mine, do, 0).astype(BF)
                    km = jnp.where(mine, k * scale, 0).astype(BF)
                    s = dot(k, qm, 1, 1) - lse_buf[mb, pl.ds(hp * 2 + h, 1), at]
                    diag = jnp.where(keep, s[i * ROWS :], NEG_LARGE)
                    p = jnp.exp(diag if i == 0 else jnp.concatenate([s[: i * ROWS], diag], axis=0))
                    pdp = p * dot(v, dom, 1, 1)
                    inner = jnp.sum(pdp, axis=0, keepdims=True)
                    ds = (pdp - p * inner).astype(BF)
                    a = dot(p.astype(BF), dom, 1, 0)
                    b = dot(ds, qm, 1, 0)
                    c = dot(ds, km, 0, 0)
                    dv, dk, dq = (a, b, c) if h == 0 else (dv + a, dk + b, dq + c)
                qkv_buf[mb, at, lanes] = dq.astype(BF)
                if i:
                    dk_ref[: i * ROWS, :] += dk[: i * ROWS]
                    dv_ref[: i * ROWS, :] += dv[: i * ROWS]
                dk_ref[i * ROWS : keys, :] = dk[i * ROWS :]
                dv_ref[i * ROWS : keys, :] = dv[i * ROWS :]
            qkv_buf[mb, :, klanes] = dk_ref[...].astype(BF)
            qkv_buf[mb, :, vlanes] = dv_ref[...].astype(BF)
            return 0

        lax.fori_loop(start, stop, pair, 0, unroll=stop - start)

    def backward_end(mb):
        def last(i, _):
            at = pl.ds(i * ROWS, ROWS)
            xhat, rstd = norm_stats(pick(tok_ref, mb, at))
            da = dot(qkv_buf[mb, at, :], wq[...], 1, 1)
            dn[0:1, :] += jnp.sum(da * xhat, axis=0, keepdims=True)
            dn[1:2, :] += jnp.sum(da, axis=0, keepdims=True)
            kept(mb, 0, i)[...] += norm_back(da, nrm[0:1, :], xhat, rstd)
            return 0

        lax.fori_loop(0, blocks, last, 0)
        for copy in gradient_copies(mb):
            copy.start()

    def outer_half(mb, side):
        def outer(j, _):
            cols = pl.ds(pl.multiple_of(j * width + side * (width // 2), LANES), width // 2)
            product = dot(uc[mb, 0], qkv_buf[mb, :, cols], 0, 0)
            to = slice(side * (width // 2), (side + 1) * (width // 2))
            g_buf[j, :, to] = product if mb == 0 else g_buf[j, :, to] + product
            return 0

        lax.fori_loop(0, 3, outer, 0)

    def finish_rows(mb):
        to_all(lambda peer: received(MIX, mb, peer, xd_in.at[0, peer, mb]))

        def rows_of(i, _):
            mixed = xd_in[0, pl.ds(i * chunk_parts, chunk_parts), mb].reshape(ROWS, width).astype(F32)
            o_buf[mb, pl.ds(i * ROWS, ROWS), :] = (kept(mb, 1, i)[...] + mixed).astype(BF)
            return 0

        lax.fori_loop(0, blocks, rows_of, 0)
        for copy in row_copies(mb):
            copy.start()

    q_peers = [lax.rem(q_id + k, half) for k in range(1, half)]
    side = width // 2
    groups = [
        [(dwo_ref, 0, width, 3 * width)],
        [(g_buf.at[j], 0, side, j * width) for j in range(3)],
        [(g_buf.at[j], side, side, j * width + side) for j in range(3)],
        [(dwc_ref, 0, LANES, 4 * width)],
    ]
    sends = []

    def parts(g, zw, zn):
        at = pl.ds(pl.multiple_of((zw * narrows + zn) * rows, padded), padded)
        found, start = [], 0
        for ref, col, size, _ in groups[g]:
            found.append((slice(start, start + size), ref[at, col : col + size]))
            start += size
        return found

    def to_core(g):
        if not own_shard:
            return
        s1, r1 = reducers[g][:2]
        for k in range(half):
            there = lax.rem(q_id + 1 + k, half)

            def fill(z, _, there=there):
                for cols, value in parts(g, z, 2 * there + 1 - parity):
                    s1[there, z, :, cols] = value.astype(BF)
                return 0

            lax.fori_loop(0, wides, fill, 0)
            remote(s1.at[there], r1.at[there], c_sem.at[g, k], cr_sem.at[g, there], (w_id, core)).start()

    def to_chips(g):
        if not own_shard:
            return
        s1, r1, r2, _, _, sum_buf = reducers[g]
        for k in range(half):
            there = lax.rem(q_id + 1 + k, half)
            pltpu.make_async_copy(r1.at[there], r1.at[there], cr_sem.at[g, there]).wait()
            pltpu.make_async_copy(s1.at[there], s1.at[there], c_sem.at[g, k]).wait()
            last = k == half - 1

            def add(z, _, there=there, last=last):
                for cols, value in parts(g, z, 2 * there + parity):
                    value = value + r1[there, z, :, cols].astype(F32)
                    if last:
                        sum_buf[z, :, cols] = value
                    else:
                        s1[there, z, :, cols] = value.astype(BF)
                return 0

            lax.fori_loop(0, wides, add, 0)
            if not last:
                copy = remote(
                    s1.at[there], r2.at[q_id], p_sem.at[g, k], pr_sem.at[g, q_id], (w_id, there * 2 + parity))
                copy.start()
                sends.append(copy)

    def to_planes(g):
        if not own_shard:
            return
        _, _, r2, s3, r3, sum_buf = reducers[g]
        for there in q_peers:
            pltpu.make_async_copy(r2.at[there], r2.at[there], pr_sem.at[g, there]).wait()
        for k in range(wides):
            z = lax.rem(w_id + 1 + k, wides)
            acc = sum_buf[z]
            for there in q_peers:
                acc = acc + r2[there, z].astype(F32)
            if k < wides - 1:
                s3[z] = acc.astype(BF)
                copy = remote(s3.at[z], r3.at[w_id], z_sem.at[g, k], zr_sem.at[g, w_id], (z, me))
                copy.start()
                sends.append(copy)
            else:
                sum_buf[z] = acc

    def owned_rows(g):
        _, _, _, _, r3, sum_buf = reducers[g]
        acc = sum_buf[w_id]
        for z in z_peers:
            pltpu.make_async_copy(r3.at[z], r3.at[z], zr_sem.at[g, z]).wait()
            acc = acc + r3[z].astype(F32)
        start = 0
        for _, _, size, to in groups[g]:
            shared_ref[:, to : to + size] = acc[:, start : start + size]
            start += size

    def relay(hop):
        def run():
            hop_arrived(hop)
            if hop < wides - 1:
                hop_send(hop + 1)

        return run

    up_at = pl.ds(pl.multiple_of(w_id * up_rows, up_rows), up_rows)
    down_tile = folds + w_id * down_rows // width
    down_at = pl.ds(pl.multiple_of(lax.rem(w_id * down_rows, width), down_rows), down_rows)

    def own_copies():
        copies = [
            pltpu.make_async_copy(g_buf.at[j, up_at], upg_ref.at[:, pl.ds(j * width, width)], own_sem.at[1 + j])
            for j in range(folds)
        ]
        return copies + [pltpu.make_async_copy(g_buf.at[down_tile, down_at], downg_ref, own_sem.at[1 + folds])]

    relays = [relay(hop) for hop in range(1, wides - 1)]
    early = relays[: (len(relays) + 1) // 2]
    late = relays[len(early) :]
    pairs = HEADS // 2
    for mb in range(micros):
        hooks = {}
        if mb == 0:
            hooks[min(2, blocks - 1)] = early
        elif mb == 1:
            hooks[min(1, blocks - 1)] = late + [lambda: mix(0), lambda: send_mixture(0, 0, narrows)]
        forward(mb, hooks)
        send_rows(U, mb)
    hop_arrived(wides - 1)
    g_buf[...] = jnp.zeros_like(g_buf)
    dn[...] = jnp.zeros_like(dn)
    expert(0)
    mix(1)
    outputs_arrived(0)
    send_mixture(1, 0, half)
    combine(0)
    gradients_arrived(0)
    send_mixture(1, half, narrows)
    backward_start(0)
    backward_pairs(0, 0, 1)
    expert(1)
    for hop in range(1, wides):
        hop_sent(hop)
    for j in range(folds):
        wt_buf[:, j] = g_buf[j].astype(BF).reshape(wides, up_rows, width)
        wt_buf[j * per_shard : (j + 1) * per_shard, folds:] = (
            g_buf[folds + j].astype(BF).reshape(per_shard, folds, up_rows, width))

    def pass_on(way, i):
        part_id = wides - 1 - i if way == 0 else i
        to = w_id + 1 if way == 0 else w_id - 1
        remote(wt_buf.at[part_id], got_ref.at[way, i], rs_sem.at[way, i], rsr_sem.at[way, i], (to, me)).start()

    def taken(way, i, target):
        pltpu.make_async_copy(got_ref.at[way, i], got_ref.at[way, i], rsr_sem.at[way, i]).wait()
        copy = pltpu.make_async_copy(got_ref.at[way, i], target, own_sem.at[0])
        copy.start()
        copy.wait()

    def held(way):
        return yx_in.at[0, pl.ds(0, 2 * folds), way]

    def add_on(step):
        for way in range(2):
            far = w_id if way == 0 else wides - 1 - w_id
            i = step - far
            part_id = wides - 1 - i if way == 0 else i

            @pl.when((far >= 1) & (i >= 0) & (i < wides - 1 - far))
            def _():
                taken(way, i, held(way))
                for j in range(2 * folds):
                    wt_buf[part_id, j] = (
                        wt_buf[part_id, j].astype(F32) + yx_in[0, j, way].astype(F32)).astype(BF)
                pass_on(way, i)

    @pl.when(w_id == 0)
    def _():
        for i in range(wides - 1):
            pass_on(0, i)

    @pl.when(w_id == wides - 1)
    def _():
        for i in range(wides - 1):
            pass_on(1, i)

    owned = own_copies()
    for copy in owned:
        copy.start()
    backward_pairs(0, 1, pairs // 2 + 1)
    for copy in owned:
        copy.wait()
    outputs_arrived(1)
    combine(1)
    add_on(1)
    backward_pairs(0, pairs // 2 + 1, pairs)
    send_mixed(0)
    outer_half(0, 0)
    outer_half(0, 1)
    backward_end(0)
    send_mixed(1)
    gradients_arrived(1)
    backward_start(1)
    for step in range(2, wides - 1):
        add_on(step)
    to_core(0)
    backward_pairs(1, 0, pairs // 2)
    to_chips(0)
    outer_half(1, 0)
    to_core(1)
    backward_pairs(1, pairs // 2, pairs // 2 + 1)
    to_chips(1)
    to_planes(0)
    backward_pairs(1, pairs // 2 + 1, pairs)
    outer_half(1, 1)
    to_core(2)
    to_planes(1)
    backward_end(1)

    dwc_ref[...] += jnp.transpose(jnp.concatenate(
        [jnp.zeros((narrows, width), F32), dn[...], jnp.zeros((LANES - 8 - narrows, width), F32)], axis=0))
    to_core(3)
    to_chips(2)
    to_chips(3)
    if not own_shard:
        plain = [
            pltpu.make_async_copy(g_buf.at[j], shared_ref.at[:, pl.ds(j * width, width)], c_sem.at[0, j])
            for j in range(3)
        ]
        plain.append(pltpu.make_async_copy(dwo_ref, shared_ref.at[:, pl.ds(3 * width, width)], c_sem.at[0, 3]))
        plain.append(pltpu.make_async_copy(dwc_ref, shared_ref.at[:, pl.ds(4 * width, LANES)], c_sem.at[0, 4]))
        for copy in plain:
            copy.start()
        for copy in plain:
            copy.wait()
    for mb in range(micros):
        finish_rows(mb)
    for copy in gradient_copies(0):
        copy.wait()

    for way in range(2):
        far = w_id if way == 0 else wides - 1 - w_id

        @pl.when(far > 0)
        def _():
            taken(way, wides - 1 - far, held(way))

        @pl.when(far == 0)
        def _():
            for j in range(2 * folds):
                yx_in[0, j, way] = jnp.zeros((up_rows, width), BF)

    sq_buf[...] = jnp.zeros_like(sq_buf)
    mine_up = [h_buf.at[0, pl.ds(j * up_rows, up_rows)] for j in range(folds)]
    mine_down = h_buf.at[1, pl.ds(0, down_rows)]
    back = [
        pltpu.make_async_copy(upg_ref.at[:, pl.ds(j * width, width)], mine_up[j], own_sem.at[1 + j])
        for j in range(folds)
    ]
    back.append(pltpu.make_async_copy(downg_ref, mine_down, own_sem.at[1 + folds]))
    for copy in back:
        copy.start()
    for copy in back:
        copy.wait()
    for j in range(2 * folds):
        mine = h_buf.at[j // folds, pl.ds(j % folds * up_rows, up_rows)]
        value = mine[...] + yx_in[0, j, 0].astype(F32) + yx_in[0, j, 1].astype(F32)
        mine[...] = value
        sq_buf[...] += fold_rows(value * value)
    owned = [
        pltpu.make_async_copy(mine_up[j], upg_ref.at[:, pl.ds(j * width, width)], own_sem.at[1 + j])
        for j in range(folds)
    ]
    owned.append(pltpu.make_async_copy(mine_down, downg_ref, own_sem.at[1 + folds]))
    for copy in owned:
        copy.start()

    if own_shard:
        to_planes(2)
        to_planes(3)
        for g in range(GROUPS):
            owned_rows(g)

        value = shared_ref[...]
        sq_buf[...] += fold_rows(value * value)
        n_peers = [lax.rem(me + k, narrows) for k in range(1, narrows)]
        for k, p in enumerate(n_peers):
            copy = remote(sq_buf, sq_n.at[me], sn_sem.at[k], snr_sem.at[me], (w_id, p))
            copy.start()
            sends.append(copy)
    for copy in gradient_copies(1) + row_copies(0) + row_copies(1) + owned:
        copy.wait()
    for copy in gather_sends:
        copy.wait_send()
    for i in range(wides - 1):
        for way in range(2):
            far = w_id if way == 0 else wides - 1 - w_id

            @pl.when(i < wides - 1 - far)
            def _():
                pltpu.make_async_copy(wt_buf.at[0], wt_buf.at[0], rs_sem.at[way, i]).wait()
    sent(XD, micros - 1, xd_out.at[0])
    sent(YX, micros - 1, xd_in.at[micros - 1, 0])
    for mb in range(micros):
        sent(DU, mb, in_buf.at[mb, 0, 0])
        sent(MIX, mb, in_buf.at[mb, 0, 0])
    if own_shard:
        sq_n[me] = sq_buf[...]
        for p in n_peers:
            pltpu.make_async_copy(sq_n.at[p], sq_n.at[p], snr_sem.at[p]).wait()
        acc = sq_n[0]
        for k in range(1, narrows):
            acc = acc + sq_n[k]
        sq_w[w_id] = acc
        for k, z in enumerate(z_peers):
            copy = remote(sq_w.at[w_id], sq_w.at[w_id], sw_sem.at[k], swr_sem.at[w_id], (z, me))
            copy.start()
            sends.append(copy)
        for z in z_peers:
            pltpu.make_async_copy(sq_w.at[z], sq_w.at[z], swr_sem.at[z]).wait()
        acc = sq_w[0]
        for k in range(1, wides):
            acc = acc + sq_w[k]
        total_ref[...] = acc
    else:
        total_ref[...] = sq_buf[...]
    for copy in sends:
        copy.wait_send()


def run_block(counts, assign, tokens, cot, shard, up, down, wides, narrows, rows):
    micros, length, width = tokens.shape
    part = length // narrows
    hidden_width = up.shape[1]
    folds = hidden_width // width
    devices = wides * narrows
    hbm = pl.BlockSpec(memory_space=pl.ANY)
    vmem = pl.BlockSpec(memory_space=pltpu.VMEM)
    pairs = pltpu.VMEM((micros, narrows, 2, part, width), BF)
    pairs_one = pltpu.VMEM((narrows, 2, part, width), BF)
    sems = pltpu.SemaphoreType.DMA
    half = narrows // 2
    cols = 4 * width + LANES
    padded = max(rows, 16)
    shard_shape = (padded, cols) if rows == padded else shard[0].shape
    raw_shape = (16, LANES) if rows == padded else (devices * padded, shard_shape[1])
    reducers = []
    for group_cols in (width, 3 * width // 2, 3 * width // 2, LANES):
        block = (half, wides, padded, group_cols) if rows == padded else (1, 1, 16, LANES)
        reducers += [pltpu.VMEM(block, BF)] * 3 + [pltpu.VMEM(block[1:], BF)] * 2 + [pltpu.VMEM(block[1:], F32)]
    return pl.pallas_call(
        functools.partial(block_kernel, wides, narrows, rows),
        out_shape=[
            jax.ShapeDtypeStruct((micros, length, width), F32),
            jax.ShapeDtypeStruct((micros, length, width), BF),
            jax.ShapeDtypeStruct((padded if rows == padded else width, cols), F32),
            jax.ShapeDtypeStruct(up.shape, F32),
            jax.ShapeDtypeStruct(down.shape, F32),
            jax.ShapeDtypeStruct((8, LANES), F32),
            jax.ShapeDtypeStruct((2, wides - 1, 2 * folds, up.shape[0], width), BF),
        ],
        in_specs=[vmem] * 3 + [hbm] + [vmem] * len(shard) + [hbm] * 2,
        out_specs=[hbm, hbm, vmem if rows == padded else hbm, hbm, hbm, vmem, hbm],
        scratch_shapes=[
            pltpu.VMEM((8, LANES), F32),
            pltpu.VMEM((micros, narrows, LANES), F32),
            pltpu.VMEM(shard_shape, BF),
            pltpu.VMEM(raw_shape, BF),
            pltpu.VMEM((width, cols), BF),
            pltpu.VMEM((micros, 2, length, width), BF),
            pltpu.VMEM((micros, length, 3 * width), BF),
            pltpu.VMEM((micros, length, width), BF),
            pltpu.VMEM((micros, HEADS, length), F32),
            pltpu.VMEM((8, width), F32),
            pltpu.VMEM((8, width), F32),
            pairs,
            pairs_one,
            pairs,
            pairs,
            pltpu.VMEM((micros, narrows, part, LANES), F32),
            pltpu.VMEM((width, LANES), BF),
            pltpu.VMEM((wides, 2 * folds, up.shape[0], width), BF),
            pltpu.VMEM((2 * folds, width, width), F32),
            pltpu.VMEM((2 * (length // width), width, width), F32),
            pltpu.VMEM((length, LANES), F32),
            pltpu.VMEM((length, LANES), F32),
            pltpu.VMEM((width, width), F32),
            pltpu.VMEM((width, LANES), F32),
            *reducers,
            pltpu.VMEM((8, LANES), F32),
            pltpu.VMEM((narrows, 8, LANES), F32),
            pltpu.VMEM((wides, 8, LANES), F32),
            sems((wides - 1,)),
            sems((wides, half - 1)),
            sems((wides, half)),
            sems((wides, narrows)),
            sems((wides - 1, 2)),
            sems((wides - 1, 2)),
            sems((6, micros, narrows)),
            sems((6, micros, narrows)),
            sems((2, wides - 1)),
            sems((2, wides - 1)),
            sems((2 + folds,)),
            sems((micros * (1 + length // width),)),
            sems((GROUPS, max(half, 5))),
            sems((GROUPS, half)),
            sems((GROUPS, wides)),
            sems((GROUPS, half)),
            sems((GROUPS, half)),
            sems((GROUPS, wides)),
            sems((narrows - 1,)),
            sems((narrows,)),
            sems((wides - 1,)),
            sems((wides,)),
        ],
        compiler_params=pltpu.CompilerParams(
            collective_id=0, has_side_effects=True, vmem_limit_bytes=64 << 20),
        name="block",
    )(counts, assign, tokens, cot.reshape(micros, narrows, part, width), *shard, up, down)


def adam_values(weight, first_state, second_state, gradient, factor, rate, decay):
    clipped = gradient * factor
    first_new = BETA_ONE * first_state + (1.0 - BETA_ONE) * clipped
    second_new = BETA_TWO * second_state + (1.0 - BETA_TWO) * clipped * clipped
    first_hat = first_new / (1.0 - BETA_ONE**STEP)
    second_hat = second_new / (1.0 - BETA_TWO**STEP)
    weight_new = weight - rate * (first_hat / (jnp.sqrt(second_hat) + ADAM_EPS) + decay * weight)
    return weight_new, first_new, second_new, weight_new.astype(BF)


def final_kernel(wides, narrows, assign_ref, total_ref, shared_ref, *refs):
    states, refs = refs[:18], refs[18:]
    upg_ref, downg_ref = refs[:2]
    moved = (len(refs) - 29) // 2
    gt_in, out_in = refs[2 : 2 + moved], refs[2 + moved : 2 + 2 * moved]
    out_ref, gt_ref, norm_out = refs[2 + 2 * moved : 5 + 2 * moved]
    news = refs[5 + 2 * moved :]
    step = pl.program_id(0)
    for j in range(moved):
        gt_ref[j] = gt_in[j][0]
        out_ref[j] = out_in[j][0]
    grad_norm = jnp.sqrt(jnp.sum(jnp.sum(total_ref[...], axis=0, keepdims=True), axis=1, keepdims=True))
    factor = CLIP_NORM / jnp.maximum(grad_norm, CLIP_NORM)

    def update(k, gradient, rate, decay):
        values = [ref[0] if len(ref.shape) == 3 else ref[...] for ref in states[3 * k : 3 * k + 3]]
        for ref, value in zip(news[4 * k : 4 * k + 4], adam_values(*values, gradient, factor, rate, decay)):
            if len(ref.shape) == 3:
                ref[0] = value
            else:
                ref[...] = value

    @pl.when(step == 0)
    def _():
        norm_out[...] = grad_norm
        width = states[6].shape[1]
        extra = shared_ref[:, 4 * width :]
        chosen = lax.broadcasted_iota(jnp.int32, (narrows + 8, LANES), 0) == lax.broadcasted_iota(
            jnp.int32, (narrows + 8, LANES), 1)
        turned = lax.dot_general(
            jnp.where(chosen, 1.0, 0.0), extra, (((1,), (1,)), ((), ())), precision=lax.Precision.HIGHEST,
            preferred_element_type=F32)
        update(0, turned[narrows : narrows + 4], 0.3, 0.0)
        update(1, shared_ref[:, : 3 * width], 0.03, DECAY_RATE)
        update(2, shared_ref[:, 3 * width : 4 * width], 0.2, DECAY_RATE)
        update(3, turned[:narrows], 0.015, DECAY_RATE)

    update(4, upg_ref[...], 0.1, DECAY_RATE)
    update(5, downg_ref[...], 0.1, DECAY_RATE)


def run_final(assign, total, shared, states, upg, downg, grad_rows, out_low, wides, narrows):
    steps = max(1, upg.shape[0] // 32)
    whole = lambda x: pl.BlockSpec(x.shape, lambda i, s: (0,) * len(x.shape))
    split2 = lambda x: pl.BlockSpec((x.shape[0] // steps, x.shape[1]), lambda i, s: (i, 0))
    split3 = lambda x: pl.BlockSpec((1, x.shape[1] // steps, x.shape[2]), lambda i, s: (0, i, 0))
    micros, length, width = grad_rows.shape

    def placed(j):
        def index(i, s):
            return s[j, lax.axis_index("wide") * narrows + lax.axis_index("narrow")], i, 0

        return pl.BlockSpec((1, length // steps, width), index)

    taken = [placed(j) for j in range(micros)]
    given = pl.BlockSpec((micros, length // steps, width), lambda i, s: (0, i, 0))
    spec = lambda x: split3(x) if len(x.shape) == 3 else whole(x)
    news = []
    for k in range(6):
        shape = states[3 * k].shape
        news += [jax.ShapeDtypeStruct(shape, F32)] * 3 + [jax.ShapeDtypeStruct(shape, BF)]
    one = jax.ShapeDtypeStruct((1, 1), F32)
    return pl.pallas_call(
        functools.partial(final_kernel, wides, narrows),
        grid_spec=pltpu.PrefetchScalarGridSpec(
            num_scalar_prefetch=1,
            grid=(steps,),
            in_specs=[whole(total), whole(shared)] + [spec(x) for x in states] + [split2(upg), split2(downg)] + taken * 2,
            out_specs=[given, given, whole(one)] + [spec(x) for x in news],
        ),
        out_shape=[
            jax.ShapeDtypeStruct(out_low.shape, BF), jax.ShapeDtypeStruct(grad_rows.shape, F32), one] + news,
        name="final",
    )(assign, total, shared, *states, upg, downg, *[grad_rows] * micros, *[out_low] * micros)


def per_device(tokens, cotangent, seq_counts, micro_assign, *states):
    wides, narrows = lax.axis_size("wide"), lax.axis_size("narrow")
    norm_params, project_weight, output_weight, control_weight, up_weight, down_weight = states[::3]
    rows = project_weight.shape[0]
    padded = max(rows, 16)
    if rows == padded:
        shard = (project_weight, output_weight, control_weight.T, norm_params)
    else:
        norm_turned = norm_params.T
        high = lax.reduce_precision(norm_turned, 8, 7)
        middle = lax.reduce_precision(norm_turned - high, 8, 7)
        lower = norm_turned - high - middle
        extra = jnp.concatenate([control_weight, high, middle, lower], axis=1).astype(BF)
        extra = jnp.pad(extra, ((0, 0), (0, LANES - extra.shape[1])))
        joined = jnp.concatenate([project_weight.astype(BF), output_weight.astype(BF), extra], axis=1)
        fold = padded // rows
        group = -(-(joined.shape[1] // LANES) // fold) * LANES
        joined = jnp.pad(joined, ((0, 0), (0, fold * group - joined.shape[1])))
        shard = (joined.reshape(rows, fold, group).transpose(1, 0, 2).reshape(padded, group),)
    grad_rows, out_low, shared, upg, downg, total, _ = run_block(
        seq_counts[None], micro_assign.T, tokens, cotangent, shard, up_weight[0], down_weight[0], wides, narrows, rows)
    if rows < padded:
        both = ("wide", "narrow")
        shared = lax.psum_scatter(shared, both, scatter_dimension=0, tiled=True)
        total = lax.psum(total.at[0, 0].add(jnp.sum(shared * shared)), both)
    states = states[:9] + tuple(x.T for x in states[9:12]) + states[12:]
    out_rows, grad_tokens, grad_norm, *news = run_final(
        micro_assign.T, total, shared, states, upg, downg, grad_rows, out_low, wides, narrows)
    news[12:16] = [x.T for x in news[12:16]]
    return (out_rows, grad_tokens, grad_norm.reshape(()), *news)


def solution(mesh):
    both = ("wide", "narrow")
    rows3, cols, rows2, expert = P(both, None, None), P(None, both), P(both, None), P("narrow", "wide", None)
    return jax.shard_map(
        per_device,
        mesh=mesh,
        in_specs=(rows3, rows3, P(), P()) + (cols,) * 3 + (rows2,) * 9 + (expert,) * 6,
        out_specs=(rows3, rows3, P()) + (cols,) * 4 + (rows2,) * 12 + (expert,) * 8,
        check_vma=False,
    )
```
